32 devices in a mesh: obs: 4 (over x, core), flux: 8 (over z, y).
Axes of the slice: x: 2, y: 2, z: 4, core: 2. Of those that a mesh axis runs over, the one named last changes fastest.
Arguments:
- probes: bfloat16 [384, 32, 128], P('flux'), may hold values from -6 to 6
- prior_tiles: bfloat16 [384, 8, 128, 128], P('flux'), may hold values from -0.1875 to 0.1875
- neighbours: int32 [384, 8], P('flux'), may hold values from 0 to 383, as said below
- jac: bfloat16 [4, 8, 384, 128, 128], P('obs', 'flux'), may hold values from -0.0546875 to 0.0546875
- jac_obs: int32 [4, 8, 384], P('obs', 'flux'), may hold values from 0 to 31
- jac_flux: int32 [4, 8, 384], P('obs', 'flux'), may hold values from 0 to 47
- counts: int32 [4, 8], P('obs', 'flux'), may hold values from 96 to 384
- rinv: float32 [128, 128], P('obs'), may hold values from 0.25 to 2.5
Outputs:
- power: bfloat16 [384, 32, 128], P('flux')
The draws below stay inside these ranges and needn't reach their ends.
Inputs may be any that keep to these rules, and one draw needn't show every extreme that they name: `neighbours`: every entry lies within 12 tiles of its own tile t, and entry 0 is t itself.
All inputs are finite; a program needn't handle non-finite values.
Results may differ from the reference program's by a relative error of at most 0.024.
Values may be sent and summed in bfloat16 or wider, within the bound.
No kernel may reach another device: no remote copies, remote signals or barrier semaphores. Data moves between devices by JAX's collectives and lax.ppermute only.
A program may use at most 128 MiB of HBM per device.

```python
import math
import jax
import jax.numpy as jnp
from jax import lax

BLK = 128
PROBES = 32
NBRS = 8
STEPS = 4
FB_DEV = 48
OB_DEV = 32
NB_DEV = 384
REACH = 12
FB = 384
OBLK = 128
N_OBS = 4
N_FLUX = 8


def draw_neighbours(key, part):
    key_sign = jax.random.fold_in(key, 11)
    key_offset = jax.random.fold_in(key, 12)
    tiles = jnp.arange(FB, dtype=jnp.int32)[:, None]
    signs = jax.random.randint(key_sign, (FB, 1), 0, 2).astype(jnp.int32) * 2 - 1
    offsets = jax.random.randint(key_offset, (FB, NBRS - 2), -REACH, REACH + 1).astype(jnp.int32)
    columns = jnp.concatenate([jnp.zeros((FB, 1), jnp.int32), signs * REACH, offsets], axis=1)
    return jnp.clip(tiles + columns, 0, FB - 1).astype(jnp.int32)


def draw_counts(key, part):
    key_count = jax.random.fold_in(key, 21)
    key_place = jax.random.fold_in(key, 22)
    values = jax.random.randint(key_count, (N_OBS * N_FLUX,), NB_DEV // 4, NB_DEV + 1).astype(jnp.int32)
    place = jax.random.randint(key_place, (), 0, N_OBS * N_FLUX).astype(jnp.int32)
    values = jnp.where(jnp.arange(N_OBS * N_FLUX, dtype=jnp.int32) == place, NB_DEV, values)
    return values.reshape(N_OBS, N_FLUX).astype(jnp.int32)


def set_ends(result, stream_key, least, high):
    extent = result.shape
    spot = [jax.random.randint(jax.random.fold_in(stream_key, axis), (), 0, extent[axis]) for axis in range(len(extent))]
    result = result.at[tuple(spot)].set(least)
    longest = extent.index(max(extent))
    spot[longest] = (spot[longest] + 1) % extent[longest]
    return result.at[tuple(spot)].set(high)


def block_scale(key, extent, shards, smallest, largest):
    factor_of = 1.0
    for axis_at, blocks in shards:
        heights = jax.random.uniform(jax.random.fold_in(jax.random.fold_in(key, 6), axis_at), (blocks,), jnp.float32, smallest / len(shards), largest / len(shards))
        factor_of = factor_of * jnp.repeat(jnp.exp(heights), extent[axis_at] // blocks).reshape((-1,) + (1,) * (len(extent) - 1 - axis_at))
    return factor_of


def gaussian(rng, extent, scale, most, cuts=(), held_as=jnp.bfloat16):
    values = jax.random.normal(rng, extent, jnp.float32) * scale
    if len(cuts) > 0:
        values = block_scale(rng, extent, cuts, -0.22, 0.18) * values
    return jnp.clip(values, min=-most, max=most).astype(held_as)


def setup_inputs(seed: int = 0) -> dict:
    key_of = jax.random.split(jax.random.key(seed), 9)
    return {
        "probes": gaussian(key_of[0], (FB, PROBES, BLK), 1.0, 6.0, ((0, 8),)),
        "prior_tiles": gaussian(key_of[1], (FB, NBRS, BLK, BLK), (BLK * NBRS) ** -0.5, 0.1875, ((0, 8),)),
        "neighbours": draw_neighbours(jax.random.fold_in(key_of[8], 71), 0),
        "jac": gaussian(key_of[3], (N_OBS, N_FLUX, NB_DEV, BLK, BLK), (BLK * NB_DEV * N_FLUX // OB_DEV) ** -0.5, 0.0546875, ((0, 4), (1, 8))),
        "jac_obs": set_ends(jax.random.randint(key_of[4], (N_OBS, N_FLUX, NB_DEV), 0, OB_DEV), jax.random.fold_in(key_of[4], 1), 0, OB_DEV - 1).astype(jnp.int32),
        "jac_flux": set_ends(jax.random.randint(key_of[5], (N_OBS, N_FLUX, NB_DEV), 0, FB_DEV), jax.random.fold_in(key_of[5], 1), 0, FB_DEV - 1).astype(jnp.int32),
        "counts": draw_counts(jax.random.fold_in(key_of[8], 71), 0),
        "rinv": jnp.clip(jnp.exp(math.log(2.5) - 2.3025851 * jax.random.uniform(key_of[7], (OBLK, BLK), jnp.float32) ** block_scale(key_of[7], (OBLK, BLK), ((0, 4),), -0.2, 0.2)), 0.25, 2.5),
    }


def reference(probes, prior_tiles, neighbours, jac, jac_obs, jac_flux, counts, rinv):
    f32 = jnp.float32
    half = jnp.bfloat16
    prior_grouped = prior_tiles.reshape(N_FLUX, FB_DEV, NBRS, BLK, BLK)
    nbr_grouped = neighbours.reshape(N_FLUX, FB_DEV, NBRS)
    flux_groups = jnp.arange(N_FLUX, dtype=jnp.int32)
    all_groups = jnp.arange(N_OBS * N_FLUX, dtype=jnp.int32)
    slots = jnp.arange(NB_DEV, dtype=jnp.int32)
    obs_range = jnp.arange(OB_DEV, dtype=jnp.int32)
    tile_range = jnp.arange(FB_DEV, dtype=jnp.int32)

    def prior_forward(field):
        def one(group):
            picked = field[nbr_grouped[group]]
            return jnp.einsum("tkpc,tkcd->tpd", picked.astype(f32), prior_grouped[group].astype(f32))
        return lax.map(one, flux_groups).reshape(FB, PROBES, BLK).astype(half)

    def prior_adjoint(field):
        grouped = field.reshape(N_FLUX, FB_DEV, PROBES, BLK)

        def one(carry, group):
            contrib = jnp.einsum("tpd,tkcd->tkpc", grouped[group].astype(f32), prior_grouped[group].astype(f32))
            carry = carry.at[nbr_grouped[group].reshape(-1)].add(contrib.reshape(-1, PROBES, BLK))
            return carry, None
        total, unused = lax.scan(one, jnp.zeros((FB, PROBES, BLK), f32), flux_groups)
        return total.astype(half)

    def forward(spread):
        def one(group):
            row = group // N_FLUX
            col = group % N_FLUX
            live = (slots < counts[row, col]).astype(f32)
            shard = lax.dynamic_slice_in_dim(spread, (col * FB_DEV).astype(jnp.int32), FB_DEV, 0)
            picked = shard[jac_flux[row, col]]
            prod = jnp.einsum("npc,nco->npo", picked.astype(f32), jac[row, col].astype(f32))
            hot = (jac_obs[row, col][None, :] == obs_range[:, None]).astype(f32) * live[None, :]
            return jnp.einsum("bn,npo->bpo", hot, prod)
        parts = lax.map(one, all_groups).reshape(N_OBS, N_FLUX, OB_DEV, PROBES, BLK)
        return jnp.sum(parts, axis=1).reshape(OBLK, PROBES, BLK)

    def adjoint(weighted):
        def one(group):
            row = group // N_FLUX
            col = group % N_FLUX
            live = (slots < counts[row, col]).astype(f32)
            shard = lax.dynamic_slice_in_dim(weighted, (row * OB_DEV).astype(jnp.int32), OB_DEV, 0)
            picked = shard[jac_obs[row, col]]
            prod = jnp.einsum("npo,nco->npc", picked.astype(f32), jac[row, col].astype(f32))
            hot = (jac_flux[row, col][None, :] == tile_range[:, None]).astype(f32) * live[None, :]
            return jnp.einsum("tn,npc->tpc", hot, prod)
        parts = lax.map(one, all_groups).reshape(N_OBS, N_FLUX, FB_DEV, PROBES, BLK)
        return jnp.sum(parts, axis=0).reshape(FB, PROBES, BLK).astype(half)

    field = probes
    for step in range(STEPS):
        spread = prior_forward(field)
        predicted = forward(spread)
        weighted = (predicted * rinv[:, None, :]).astype(half)
        back = adjoint(weighted)
        field = prior_adjoint(back)
    return field
```

```python
import functools

import jax
import jax.numpy as jnp
from jax import lax
from jax.experimental import pallas as pl
from jax.experimental.pallas import tpu as pltpu
from jax.sharding import PartitionSpec as P

STEPS = 4
F32 = jnp.float32
HALF = jnp.bfloat16
VMEM_LIMIT = 48 * 2**20


def matmul(a, b):
    return lax.dot_general(a, b, (((1,), (0,)), ((), ())), preferred_element_type=F32)


def matmul_t(a, b):
    return lax.dot_general(a, b, (((1,), (1,)), ((), ())), preferred_element_type=F32)


def chunk_of(count, most):
    return max(c for c in range(1, most + 1) if count % c == 0)


def exchange(value, partner):
    n_obs, n_flux = lax.axis_size("obs"), lax.axis_size("flux")
    route = []
    for i in range(n_obs):
        for j in range(n_flux):
            to = partner(i, j)
            if to is not None:
                route.append((i * n_flux + j, to[0] * n_flux + to[1]))
    return lax.ppermute(value, ("obs", "flux"), route)


def start_copies(source, first, buffer, sems, chunk):
    def one(c, _):
        at = pl.ds(c * chunk, chunk)
        pltpu.make_async_copy(source.at[pl.ds(first + c * chunk, chunk)], buffer.at[at], sems.at[c]).start()
        return 0

    lax.fori_loop(0, buffer.shape[0] // chunk, one, 0)


def wait_copy(source, buffer, sems, chunk, c):
    at = pl.ds(c * chunk, chunk)
    pltpu.make_async_copy(source.at[pl.ds(0, chunk)], buffer.at[at], sems.at[c]).wait()


def jac_kernel(dot, chunk, n_parts, n_outs, src, dst, *refs):
    parts = refs[:n_parts]
    jac = refs[n_parts]
    outs = refs[n_parts + 1 : n_parts + 1 + n_outs]
    x, total, buffer, sems = refs[n_parts + 1 + n_outs :]
    start_copies(jac, 0, buffer, sems, chunk)
    rows = x.shape[0] // n_parts
    for k, part in enumerate(parts):
        x[k * rows : (k + 1) * rows] = part[...]
    total[...] = jnp.zeros_like(total)

    def one(c, _):
        wait_copy(jac, buffer, sems, chunk, c)
        first = c * chunk
        products = [dot(x[src[first + u]], buffer[first + u]) for u in range(chunk)]
        for u in range(chunk):
            total[dst[first + u]] += products[u]
        return 0

    lax.fori_loop(0, buffer.shape[0] // chunk, one, 0)
    rows = (total.shape[0] - 1) // n_outs
    for k, out in enumerate(outs):
        out[...] = total[k * rows : (k + 1) * rows].astype(out.dtype)


def jac_pass(dot, src, dst, parts, jac, out_rows, n_outs, name):
    probes, width = parts[0].shape[1:]
    count = jac.shape[0]
    chunk = chunk_of(count, 48)
    in_rows = len(parts) * parts[0].shape[0]
    smem = pl.BlockSpec(memory_space=pltpu.SMEM)
    vmem = pl.BlockSpec(memory_space=pltpu.VMEM)
    out = (out_rows // n_outs, probes, width)
    return pl.pallas_call(
        functools.partial(jac_kernel, dot, chunk, len(parts), n_outs),
        in_specs=[smem, smem] + [vmem] * len(parts) + [pl.BlockSpec(memory_space=pl.ANY)],
        out_specs=[vmem] * n_outs,
        out_shape=[jax.ShapeDtypeStruct(out, F32 if k == 0 else HALF) for k in range(n_outs)],
        scratch_shapes=[
            pltpu.VMEM((in_rows, probes, width), HALF),
            pltpu.VMEM((out_rows + 1, probes, width), F32),
            pltpu.VMEM(jac.shape, HALF),
            pltpu.SemaphoreType.DMA((count // chunk,)),
        ],
        compiler_params=pltpu.CompilerParams(vmem_limit_bytes=VMEM_LIMIT),
        name=name,
    )(src, dst, *parts, jac)


def gather_kernel(chunk, core, nbr, mine, other, prior, ext, to_core, to_far, buffer, sems):
    tiles, fan = buffer.shape[:2]
    half = tiles
    side = core[0]
    start_copies(prior, side * tiles, buffer, sems, chunk)
    ext[...] = jnp.zeros_like(ext)

    def one(c, _):
        wait_copy(prior, buffer, sems, chunk, c)
        first = c * chunk
        products = []
        for u in range(chunk):
            adjoint = (mine[first + u].astype(F32) + other[first + u].astype(F32)).astype(HALF)
            for k in range(fan):
                products.append(matmul_t(adjoint, buffer[first + u, k]))
        for u in range(chunk):
            for k in range(fan):
                ext[nbr[(first + u) * fan + k]] += products[u * fan + k]
        return 0

    lax.fori_loop(0, tiles // chunk, one, 0)
    to_core[...] = ext[pl.ds(half * (1 - side), half)].astype(HALF)
    to_far[...] = ext[pl.ds(half * side, half)].astype(HALF)


def gather_tiles(core, nbr, mine, other, prior):
    tiles, probes, width = mine.shape
    chunk = chunk_of(tiles, 6)
    smem = pl.BlockSpec(memory_space=pltpu.SMEM)
    vmem = pl.BlockSpec(memory_space=pltpu.VMEM)
    return pl.pallas_call(
        functools.partial(gather_kernel, chunk),
        in_specs=[smem, smem, vmem, vmem, pl.BlockSpec(memory_space=pl.ANY)],
        out_specs=[vmem] * 3,
        out_shape=[
            jax.ShapeDtypeStruct((2 * tiles, probes, width), F32),
            jax.ShapeDtypeStruct((tiles, probes, width), HALF),
            jax.ShapeDtypeStruct((tiles, probes, width), HALF),
        ],
        scratch_shapes=[
            pltpu.VMEM((tiles,) + prior.shape[1:], HALF),
            pltpu.SemaphoreType.DMA((tiles // chunk,)),
        ],
        compiler_params=pltpu.CompilerParams(vmem_limit_bytes=VMEM_LIMIT),
        name="prior_adjoint",
    )(core, nbr, mine, other, prior)


def spread_kernel(chunk, summed, core, nbr, *refs):
    if summed:
        ext, from_core, from_far, prior, out, field, buffer, sems = refs
    else:
        field, prior, out, buffer, sems = refs
    tiles, fan = buffer.shape[:2]
    side = core[0]
    start_copies(prior, side * tiles, buffer, sems, chunk)
    if summed:
        for begin, update in ((tiles * (1 - side), from_core), (tiles * side, from_far)):
            at = pl.ds(begin, tiles)
            field[at] = (ext[at] + update[...].astype(F32)).astype(HALF)

    def one(c, _):
        wait_copy(prior, buffer, sems, chunk, c)
        first = c * chunk
        for u in range(chunk):
            row = [field[nbr[(first + u) * fan + k]] for k in range(fan)]
            tile = buffer[first + u].reshape(fan * buffer.shape[2], buffer.shape[3])
            out[first + u] = matmul(jnp.concatenate(row, axis=1), tile).astype(HALF)
        return 0

    lax.fori_loop(0, tiles // chunk, one, 0)


def spread_tiles(core, nbr, fields, prior):
    summed = len(fields) > 1
    ext_tiles, probes, width = fields[0].shape
    tiles = ext_tiles // 2
    chunk = chunk_of(tiles, 6)
    smem = pl.BlockSpec(memory_space=pltpu.SMEM)
    vmem = pl.BlockSpec(memory_space=pltpu.VMEM)
    scratch = [pltpu.VMEM(fields[0].shape, HALF)] if summed else []
    return pl.pallas_call(
        functools.partial(spread_kernel, chunk, summed),
        in_specs=[smem, smem] + [vmem] * len(fields) + [pl.BlockSpec(memory_space=pl.ANY)],
        out_specs=vmem,
        out_shape=jax.ShapeDtypeStruct((tiles, probes, width), HALF),
        scratch_shapes=scratch
        + [
            pltpu.VMEM((tiles,) + prior.shape[1:], HALF),
            pltpu.SemaphoreType.DMA((tiles // chunk,)),
        ],
        compiler_params=pltpu.CompilerParams(vmem_limit_bytes=VMEM_LIMIT),
        name="prior_spread",
    )(core, nbr, *fields, prior)


def shards(probes, prior_tiles, neighbours, jac, jac_obs, jac_flux, counts, rinv):
    n_obs, n_flux = lax.axis_size("obs"), lax.axis_size("flux")
    tile_count = probes.shape[0]
    half = tile_count // 2
    reach = tile_count // 4
    obs_rows = rinv.shape[0]
    quarter = obs_rows // 4
    blocks = jac[0, 0]
    flux_at = lax.axis_index("flux")
    side = lax.rem(lax.axis_index("obs"), 2)
    corner = lax.rem(flux_at, 4)
    core = side.reshape(1)

    live = jnp.arange(blocks.shape[0], dtype=jnp.int32) < counts[0, 0]
    obs_all, flux_all = jac_obs[0, 0], jac_flux[0, 0]
    obs_at = ((obs_all // quarter) ^ corner) * quarter + obs_all % quarter
    tile_at = ((flux_all // half) ^ side) * half + flux_all % half
    obs_to = jnp.where(live, obs_at, obs_rows)
    tile_to = jnp.where(live, tile_at, tile_count)
    own_rinv = lax.dynamic_slice_in_dim(rinv, corner * quarter, quarter, 0)[:, None, :]
    first_tile = flux_at * tile_count + side * half
    own_nbr = lax.dynamic_slice_in_dim(neighbours, side * half, half, 0)
    nbr = (own_nbr - first_tile + reach).reshape(-1)

    def swap_core(value):
        return exchange(value, lambda i, j: (i ^ 1, j))

    def swap_far(value):
        def partner(i, j):
            to = j - 1 if i % 2 == 0 else j + 1
            return (i ^ 1, to) if 0 <= to < n_flux else None

        return exchange(value, partner)

    def swap_flux(value, bits):
        return exchange(value, lambda i, j: (i, j ^ bits))

    edge = jnp.where(side == 0, probes[:reach], probes[tile_count - reach :])
    beyond = swap_far(edge)
    around = jnp.concatenate([beyond, probes, beyond], axis=0)
    fields = (lax.dynamic_slice_in_dim(around, side * half, 2 * half, 0),)
    for step in range(STEPS):
        spread = spread_tiles(core, nbr, fields, prior_tiles)
        parts = (spread, swap_core(spread))
        pieces = jac_pass(matmul, tile_at, obs_to, parts, blocks, obs_rows, 4, "jac_forward")
        total = pieces[0]
        for bits in range(1, 4):
            total = total + swap_flux(pieces[bits], bits).astype(F32)
        bits = 4
        while bits < n_flux:
            sent = total.astype(HALF)
            total = sent.astype(F32) + swap_flux(sent, bits).astype(F32)
            bits *= 2
        weighted = (total * own_rinv).astype(HALF)
        parts = (weighted,) + tuple(swap_flux(weighted, bits) for bits in range(1, 4))
        mine, theirs = jac_pass(matmul_t, obs_at, tile_to, parts, blocks, tile_count, 2, "jac_adjoint")
        mine = (mine + swap_core(theirs).astype(F32)).astype(HALF)
        bits = 2
        while bits < n_obs:
            other = exchange(mine, lambda i, j, bits=bits: (i ^ bits, j))
            bits *= 2
            if bits < n_obs:
                mine = (mine.astype(F32) + other.astype(F32)).astype(HALF)
        ext, to_core, to_far = gather_tiles(core, nbr, mine, other, prior_tiles)
        fields = (ext, swap_core(to_core), swap_far(to_far))
    ext, from_core, from_far = fields
    low = jnp.where(side == 0, from_far, from_core).astype(F32)
    high = jnp.where(side == 0, from_core, from_far).astype(F32)
    own = (ext + jnp.concatenate([low, high], axis=0))[reach : reach + half].astype(HALF)
    other = swap_core(own)
    first = jnp.where(side == 0, own, other)
    second = jnp.where(side == 0, other, own)
    return jnp.concatenate([first, second], axis=0)


def solution(mesh):
    placed = (
        P("flux", None, None),
        P("flux", None, None, None),
        P("flux", None),
        P("obs", "flux", None, None, None),
        P("obs", "flux", None),
        P("obs", "flux", None),
        P("obs", "flux"),
        P("obs", None),
    )
    return jax.shard_map(
        shards, mesh=mesh, in_specs=placed, out_specs=P("flux", None, None), check_vma=False
    )
```

```python
import functools

import jax
import jax.numpy as jnp
from jax import lax
from jax.experimental import pallas as pl
from jax.experimental.pallas import tpu as pltpu
from jax.sharding import PartitionSpec as P

STEPS = 4
F32 = jnp.float32
HALF = jnp.bfloat16
VMEM_LIMIT = 8 * 2**20
GROUP = 4
ROUND = 24


def matmul(a, b):
    return lax.dot_general(a, b, (((1,), (0,)), ((), ())), preferred_element_type=F32)


def matmul_t(a, b):
    return lax.dot_general(a, b, (((1,), (1,)), ((), ())), preferred_element_type=F32)


def chunk_of(count, most):
    return max(c for c in range(1, most + 1) if count % c == 0)


def exchange(value, partner):
    n_obs, n_flux = lax.axis_size("obs"), lax.axis_size("flux")
    route = []
    for i in range(n_obs):
        for j in range(n_flux):
            to = partner(i, j)
            if to is not None:
                route.append((i * n_flux + j, to[0] * n_flux + to[1]))
    return lax.ppermute(value, ("obs", "flux"), route)


def plan_groups(src, dst, src_rows, dst_rows):
    passes, blocks = dst.shape
    groups = blocks // GROUP + dst_rows
    groups += -groups % ROUND
    slots = groups * GROUP
    i32 = jnp.int32
    at = jnp.arange(blocks, dtype=i32)
    rows = jnp.arange(dst_rows, dtype=i32)
    same = (dst[:, :, None] == dst[:, None, :]) & (at[None, :] < at[:, None])
    rank = jnp.sum(same.astype(i32), axis=2)
    member = (dst[:, None, :] == rows[:, None]).astype(i32)
    fills = (jnp.sum(member, axis=2) + GROUP - 1) // GROUP
    begin = jnp.sum(jnp.where(rows[None, :] < rows[:, None], fills[:, None, :], 0), axis=2)
    place = jnp.sum(member * begin[:, :, None], axis=1) * GROUP + rank
    place = jnp.where(dst < dst_rows, place, slots)
    hit = place[:, None, :] == jnp.arange(slots, dtype=i32)[:, None]
    src_of = jnp.sum(jnp.where(hit, (src - src_rows)[:, None, :], 0), axis=2) + src_rows
    block_of = jnp.sum(jnp.where(hit, at, 0), axis=2)
    lead = place[:, None, :] == jnp.arange(groups, dtype=i32)[:, None] * GROUP
    dst_of = jnp.sum(jnp.where(lead, (dst - dst_rows)[:, None, :], 0), axis=2) + dst_rows
    rounds = (jnp.sum(fills, axis=1, keepdims=True) + ROUND - 1) // ROUND
    return jnp.concatenate([src_of, block_of, dst_of, rounds], axis=1)


def grouped_products(transposed, plan, x, blocks, total):
    slots = (plan.shape[0] - 1) // (2 * GROUP + 1) * GROUP
    total[...] = jnp.zeros_like(total)

    def one(c, _):
        products = []
        for u in range(ROUND):
            first = (c * ROUND + u) * GROUP
            rows = [x[plan[first + g]] for g in range(GROUP)]
            tiles = [blocks[plan[slots + first + g]] for g in range(GROUP)]
            left = jnp.concatenate(rows, axis=1)
            if transposed:
                products.append(matmul_t(left, jnp.concatenate(tiles, axis=1)))
            else:
                products.append(matmul(left, jnp.concatenate(tiles, axis=0)))
        for u in range(ROUND):
            total[plan[2 * slots + c * ROUND + u]] += products[u]
        return 0

    lax.fori_loop(0, plan[plan.shape[0] - 1], one, 0)


def jac_kernel(transposed, n_parts, n_outs, plan, *refs):
    parts = refs[:n_parts]
    jac = refs[n_parts]
    outs = refs[n_parts + 1 : n_parts + 1 + n_outs]
    x, total = refs[n_parts + 1 + n_outs :]
    rows = parts[0].shape[0]
    for k, part in enumerate(parts):
        x[k * rows : (k + 1) * rows] = part[...]
    for r in range(n_parts * rows, x.shape[0]):
        x[r] = jnp.zeros(x.shape[1:], HALF)
    grouped_products(transposed, plan, x, jac, total)
    rows = outs[0].shape[0]
    for k, out in enumerate(outs):
        out[...] = total[k * rows : (k + 1) * rows].astype(out.dtype)


def jac_pass(transposed, plan, parts, jac, src_rows, dst_rows, out_rows, n_outs, name):
    probes, width = parts[0].shape[1:]
    smem = pl.BlockSpec(memory_space=pltpu.SMEM)
    vmem = pl.BlockSpec(memory_space=pltpu.VMEM)
    out = (out_rows // n_outs, probes, width)
    return pl.pallas_call(
        functools.partial(jac_kernel, transposed, len(parts), n_outs),
        in_specs=[smem] + [vmem] * len(parts) + [vmem],
        out_specs=[vmem] * n_outs,
        out_shape=[jax.ShapeDtypeStruct(out, F32 if k == 0 else HALF) for k in range(n_outs)],
        scratch_shapes=[
            pltpu.VMEM((src_rows + 1, probes, width), HALF),
            pltpu.VMEM((dst_rows + 1, probes, width), F32),
        ],
        compiler_params=pltpu.CompilerParams(vmem_limit_bytes=VMEM_LIMIT),
        name=name,
    )(plan, *parts, jac)


def gather_kernel(src_rows, core, plan, mine, other, prior, ext, to_core, to_far, x, total):
    half = mine.shape[0]
    side = core[0]
    x[:half] = (mine[...].astype(F32) + other[...].astype(F32)).astype(HALF)
    x[src_rows] = jnp.zeros(x.shape[1:], HALF)
    grouped_products(True, plan, x, prior, total)
    ext[...] = total[: 2 * half]
    to_core[...] = total[pl.ds(half * (1 - side), half)].astype(HALF)
    to_far[...] = total[pl.ds(half * side, half)].astype(HALF)


def gather_tiles(core, plan, mine, other, prior, src_rows, dst_rows):
    tiles, probes, width = mine.shape
    smem = pl.BlockSpec(memory_space=pltpu.SMEM)
    vmem = pl.BlockSpec(memory_space=pltpu.VMEM)
    return pl.pallas_call(
        functools.partial(gather_kernel, src_rows),
        in_specs=[smem, smem, vmem, vmem, vmem],
        out_specs=[vmem] * 3,
        out_shape=[
            jax.ShapeDtypeStruct((2 * tiles, probes, width), F32),
            jax.ShapeDtypeStruct((tiles, probes, width), HALF),
            jax.ShapeDtypeStruct((tiles, probes, width), HALF),
        ],
        scratch_shapes=[
            pltpu.VMEM((src_rows + 1, probes, width), HALF),
            pltpu.VMEM((dst_rows + 1, probes, width), F32),
        ],
        compiler_params=pltpu.CompilerParams(vmem_limit_bytes=VMEM_LIMIT),
        name="prior_adjoint",
    )(core, plan, mine, other, prior)


def spread_kernel(summed, fan, core, nbr, *refs):
    if summed:
        ext, from_core, from_far, prior, out, field = refs
    else:
        field, prior, out = refs
    tiles = out.shape[0]
    chunk = chunk_of(tiles, 12)
    side = core[0]
    if summed:
        for begin, update in ((tiles * (1 - side), from_core), (tiles * side, from_far)):
            at = pl.ds(begin, tiles)
            field[at] = (ext[at] + update[...].astype(F32)).astype(HALF)

    def one(c, _):
        first = c * chunk
        for u in range(chunk):
            row = [field[nbr[(first + u) * fan + k]] for k in range(fan)]
            tile = prior[pl.ds((side * tiles + first + u) * fan, fan)]
            tile = tile.reshape(fan * tile.shape[1], tile.shape[2])
            out[first + u] = matmul(jnp.concatenate(row, axis=1), tile).astype(HALF)
        return 0

    lax.fori_loop(0, tiles // chunk, one, 0)


def spread_tiles(core, nbr, fields, prior):
    summed = len(fields) > 1
    ext_tiles, probes, width = fields[0].shape
    tiles = ext_tiles // 2
    smem = pl.BlockSpec(memory_space=pltpu.SMEM)
    vmem = pl.BlockSpec(memory_space=pltpu.VMEM)
    return pl.pallas_call(
        functools.partial(spread_kernel, summed, nbr.shape[0] // tiles),
        in_specs=[smem, smem] + [vmem] * len(fields) + [vmem],
        out_specs=vmem,
        out_shape=jax.ShapeDtypeStruct((tiles, probes, width), HALF),
        scratch_shapes=[pltpu.VMEM(fields[0].shape, HALF)] if summed else [],
        compiler_params=pltpu.CompilerParams(vmem_limit_bytes=VMEM_LIMIT),
        name="prior_spread",
    )(core, nbr, *fields, prior)


def shards(probes, prior_tiles, neighbours, jac, jac_obs, jac_flux, counts, rinv):
    n_obs, n_flux = lax.axis_size("obs"), lax.axis_size("flux")
    tile_count = probes.shape[0]
    half = tile_count // 2
    reach = tile_count // 4
    obs_rows = rinv.shape[0]
    quarter = obs_rows // 4
    blocks = jac[0, 0]
    flux_at = lax.axis_index("flux")
    side = lax.rem(lax.axis_index("obs"), 2)
    corner = lax.rem(flux_at, 4)
    core = side.reshape(1)

    live = jnp.arange(blocks.shape[0], dtype=jnp.int32) < counts[0, 0]
    obs_all, flux_all = jac_obs[0, 0], jac_flux[0, 0]
    obs_at = ((obs_all // quarter) ^ corner) * quarter + obs_all % quarter
    tile_at = ((flux_all // half) ^ side) * half + flux_all % half
    own_rinv = lax.dynamic_slice_in_dim(rinv, corner * quarter, quarter, 0)[:, None, :]
    first_tile = flux_at * tile_count + side * half
    own_nbr = lax.dynamic_slice_in_dim(neighbours, side * half, half, 0)
    nbr = (own_nbr - first_tile + reach).reshape(-1)
    fan = neighbours.shape[1]
    prior = prior_tiles.reshape((tile_count * fan,) + prior_tiles.shape[2:])

    rows = max(obs_rows, tile_count, 2 * half)
    count = max(blocks.shape[0], prior.shape[0])
    fill = lambda value, more: jnp.pad(value, (0, count - value.shape[0]), constant_values=more)
    prior_at = jnp.arange(prior.shape[0], dtype=jnp.int32)
    own = prior_at // (half * fan) == side
    prior_src = prior_at // fan - side * half
    prior_dst = jnp.where(own, jnp.tile(nbr, 2), rows)
    plans = plan_groups(
        jnp.stack([fill(tile_at, 0), fill(obs_at, 0), fill(prior_src, 0)]),
        jnp.stack(
            [
                fill(jnp.where(live, obs_at, rows), rows),
                fill(jnp.where(live, tile_at, rows), rows),
                fill(prior_dst, rows),
            ]
        ),
        rows,
        rows,
    )
    obs_plan, tile_plan, prior_plan = plans[0], plans[1], plans[2]

    def swap_core(value):
        return exchange(value, lambda i, j: (i ^ 1, j))

    def swap_far(value):
        def partner(i, j):
            to = j - 1 if i % 2 == 0 else j + 1
            return (i ^ 1, to) if 0 <= to < n_flux else None

        return exchange(value, partner)

    def swap_flux(value, bits):
        return exchange(value, lambda i, j: (i, j ^ bits))

    edge = jnp.where(side == 0, probes[:reach], probes[tile_count - reach :])
    beyond = swap_far(edge)
    around = jnp.concatenate([beyond, probes, beyond], axis=0)
    fields = (lax.dynamic_slice_in_dim(around, side * half, 2 * half, 0),)
    for step in range(STEPS):
        spread = spread_tiles(core, nbr, fields, prior)
        parts = (spread, swap_core(spread))
        pieces = jac_pass(False, obs_plan, parts, blocks, rows, rows, obs_rows, 4, "jac_forward")
        total = pieces[0]
        for bits in range(1, 4):
            total = total + swap_flux(pieces[bits], bits).astype(F32)
        bits = 4
        while bits < n_flux:
            sent = total.astype(HALF)
            total = sent.astype(F32) + swap_flux(sent, bits).astype(F32)
            bits *= 2
        weighted = (total * own_rinv).astype(HALF)
        parts = (weighted,) + tuple(swap_flux(weighted, bits) for bits in range(1, 4))
        mine, theirs = jac_pass(True, tile_plan, parts, blocks, rows, rows, tile_count, 2, "jac_adjoint")
        mine = (mine + swap_core(theirs).astype(F32)).astype(HALF)
        bits = 2
        while bits < n_obs:
            other = exchange(mine, lambda i, j, bits=bits: (i ^ bits, j))
            bits *= 2
            if bits < n_obs:
                mine = (mine.astype(F32) + other.astype(F32)).astype(HALF)
        ext, to_core, to_far = gather_tiles(core, prior_plan, mine, other, prior, rows, rows)
        fields = (ext, swap_core(to_core), swap_far(to_far))
    ext, from_core, from_far = fields
    low = jnp.where(side == 0, from_far, from_core).astype(F32)
    high = jnp.where(side == 0, from_core, from_far).astype(F32)
    own = (ext + jnp.concatenate([low, high], axis=0))[reach : reach + half].astype(HALF)
    other = swap_core(own)
    first = jnp.where(side == 0, own, other)
    second = jnp.where(side == 0, other, own)
    return jnp.concatenate([first, second], axis=0)


def solution(mesh):
    placed = (
        P("flux", None, None),
        P("flux", None, None, None),
        P("flux", None),
        P("obs", "flux", None, None, None),
        P("obs", "flux", None),
        P("obs", "flux", None),
        P("obs", "flux"),
        P("obs", None),
    )
    return jax.shard_map(
        shards, mesh=mesh, in_specs=placed, out_specs=P("flux", None, None), check_vma=False
    )
```

```python
import functools

import jax
import jax.numpy as jnp
from jax import lax
from jax.experimental import pallas as pl
from jax.experimental.pallas import tpu as pltpu
from jax.sharding import PartitionSpec as P

STEPS = 4
F32 = jnp.float32
HALF = jnp.bfloat16
VMEM_LIMIT = 8 * 2**20
GROUP = 4
ROUND = 24


def matmul(a, b):
    return lax.dot_general(a, b, (((1,), (0,)), ((), ())), preferred_element_type=F32)


def chunk_of(count, most):
    return max(c for c in range(1, most + 1) if count % c == 0)


def exchange(value, partner):
    n_obs, n_flux = lax.axis_size("obs"), lax.axis_size("flux")
    route = []
    for i in range(n_obs):
        for j in range(n_flux):
            to = partner(i, j)
            if to is not None:
                route.append((i * n_flux + j, to[0] * n_flux + to[1]))
    return lax.ppermute(value, ("obs", "flux"), route)


def plan_groups(src, dst, src_rows, dst_rows):
    passes, blocks = dst.shape
    groups = blocks // GROUP + dst_rows
    groups += -groups % ROUND
    slots = groups * GROUP
    i32 = jnp.int32
    at = jnp.arange(blocks, dtype=i32)
    rows = jnp.arange(dst_rows, dtype=i32)
    same = (dst[:, :, None] == dst[:, None, :]) & (at[None, :] < at[:, None])
    rank = jnp.sum(same.astype(i32), axis=2)
    member = (dst[:, None, :] == rows[:, None]).astype(i32)
    fills = (jnp.sum(member, axis=2) + GROUP - 1) // GROUP
    begin = jnp.sum(jnp.where(rows[None, :] < rows[:, None], fills[:, None, :], 0), axis=2)
    place = jnp.sum(member * begin[:, :, None], axis=1) * GROUP + rank
    place = jnp.where(dst < dst_rows, place, slots)
    hit = place[:, None, :] == jnp.arange(slots, dtype=i32)[:, None]
    src_of = jnp.sum(jnp.where(hit, (src - src_rows)[:, None, :], 0), axis=2) + src_rows
    block_of = jnp.sum(jnp.where(hit, at, 0), axis=2)
    lead = place[:, None, :] == jnp.arange(groups, dtype=i32)[:, None] * GROUP
    dst_of = jnp.sum(jnp.where(lead, (dst - dst_rows)[:, None, :], 0), axis=2) + dst_rows
    rounds = (jnp.sum(fills, axis=1, keepdims=True) + ROUND - 1) // ROUND
    return jnp.concatenate([src_of, block_of, dst_of, rounds], axis=1)


def setup_kernel(chunk, first, source, plain, turned, sems):
    begin = first[0]

    def copy(c):
        at = pl.ds(c * chunk, chunk)
        rows = pl.ds(begin + c * chunk, chunk)
        return pltpu.make_async_copy(source.at[rows], plain.at[at], sems.at[c])

    def start(c, _):
        copy(c).start()
        return 0

    def turn(c, _):
        copy(c).wait()
        for u in range(chunk):
            turned[c * chunk + u] = plain[c * chunk + u].T
        return 0

    lax.fori_loop(0, plain.shape[0] // chunk, start, 0)
    lax.fori_loop(0, plain.shape[0] // chunk, turn, 0)


def setup_blocks(first, count, source, name):
    shape = (count,) + source.shape[1:]
    chunk = chunk_of(count, 24)
    vmem = pl.BlockSpec(memory_space=pltpu.VMEM)
    return pl.pallas_call(
        functools.partial(setup_kernel, chunk),
        in_specs=[pl.BlockSpec(memory_space=pltpu.SMEM), pl.BlockSpec(memory_space=pl.ANY)],
        out_specs=[vmem, vmem],
        out_shape=[pltpu.VMEM(shape, HALF), pltpu.VMEM(shape, HALF)],
        scratch_shapes=[pltpu.SemaphoreType.DMA((count // chunk,))],
        compiler_params=pltpu.CompilerParams(vmem_limit_bytes=VMEM_LIMIT),
        name=name,
    )(first, pltpu.with_memory_space_constraint(source, pltpu.HBM))


def grouped_products(plan, x, blocks, total):
    slots = (plan.shape[0] - 1) // (2 * GROUP + 1) * GROUP
    total[...] = jnp.zeros_like(total)

    def one(c, _):
        products = []
        for u in range(ROUND):
            first = (c * ROUND + u) * GROUP
            rows = [x[plan[first + g]] for g in range(GROUP)]
            tiles = [blocks[plan[slots + first + g]] for g in range(GROUP)]
            left = jnp.concatenate(rows, axis=1)
            products.append(matmul(left, jnp.concatenate(tiles, axis=0)))
        for u in range(ROUND):
            total[plan[2 * slots + c * ROUND + u]] += products[u]
        return 0

    lax.fori_loop(0, plan[plan.shape[0] - 1], one, 0)


def jac_kernel(n_parts, n_outs, plan, *refs):
    parts = refs[:n_parts]
    jac = refs[n_parts]
    outs = refs[n_parts + 1 : n_parts + 1 + n_outs]
    x, total = refs[n_parts + 1 + n_outs :]
    rows = parts[0].shape[0]
    for k, part in enumerate(parts):
        x[k * rows : (k + 1) * rows] = part[...]
    for r in range(n_parts * rows, x.shape[0]):
        x[r] = jnp.zeros(x.shape[1:], HALF)
    grouped_products(plan, x, jac, total)
    rows = outs[0].shape[0]
    for k, out in enumerate(outs):
        out[...] = total[k * rows : (k + 1) * rows].astype(out.dtype)


def jac_pass(plan, parts, jac, src_rows, dst_rows, out_rows, n_outs, name):
    probes, width = parts[0].shape[1:]
    smem = pl.BlockSpec(memory_space=pltpu.SMEM)
    vmem = pl.BlockSpec(memory_space=pltpu.VMEM)
    out = (out_rows // n_outs, probes, width)
    return pl.pallas_call(
        functools.partial(jac_kernel, len(parts), n_outs),
        in_specs=[smem] + [vmem] * len(parts) + [vmem],
        out_specs=[vmem] * n_outs,
        out_shape=[jax.ShapeDtypeStruct(out, F32 if k == 0 else HALF) for k in range(n_outs)],
        scratch_shapes=[
            pltpu.VMEM((src_rows + 1, probes, width), HALF),
            pltpu.VMEM((dst_rows + 1, probes, width), F32),
        ],
        compiler_params=pltpu.CompilerParams(vmem_limit_bytes=VMEM_LIMIT),
        name=name,
    )(plan, *parts, jac)


def gather_kernel(src_rows, core, plan, mine, other, prior, ext, to_core, to_far, x, total):
    half = mine.shape[0]
    side = core[0]
    x[:half] = (mine[...].astype(F32) + other[...].astype(F32)).astype(HALF)
    x[src_rows] = jnp.zeros(x.shape[1:], HALF)
    grouped_products(plan, x, prior, total)
    ext[...] = total[: 2 * half]
    to_core[...] = total[pl.ds(half * (1 - side), half)].astype(HALF)
    to_far[...] = total[pl.ds(half * side, half)].astype(HALF)


def gather_tiles(core, plan, mine, other, prior, src_rows, dst_rows):
    tiles, probes, width = mine.shape
    smem = pl.BlockSpec(memory_space=pltpu.SMEM)
    vmem = pl.BlockSpec(memory_space=pltpu.VMEM)
    return pl.pallas_call(
        functools.partial(gather_kernel, src_rows),
        in_specs=[smem, smem, vmem, vmem, vmem],
        out_specs=[vmem] * 3,
        out_shape=[
            jax.ShapeDtypeStruct((2 * tiles, probes, width), F32),
            jax.ShapeDtypeStruct((tiles, probes, width), HALF),
            jax.ShapeDtypeStruct((tiles, probes, width), HALF),
        ],
        scratch_shapes=[
            pltpu.VMEM((src_rows + 1, probes, width), HALF),
            pltpu.VMEM((dst_rows + 1, probes, width), F32),
        ],
        compiler_params=pltpu.CompilerParams(vmem_limit_bytes=VMEM_LIMIT),
        name="prior_adjoint",
    )(core, plan, mine, other, prior)


def spread_kernel(summed, fan, core, nbr, *refs):
    if summed:
        ext, from_core, from_far, prior, out, field = refs
    else:
        field, prior, out = refs
    tiles = out.shape[0]
    chunk = chunk_of(tiles, 12)
    side = core[0]
    if summed:
        for begin, update in ((tiles * (1 - side), from_core), (tiles * side, from_far)):
            at = pl.ds(begin, tiles)
            field[at] = (ext[at] + update[...].astype(F32)).astype(HALF)

    def one(c, _):
        first = c * chunk
        for u in range(chunk):
            row = [field[nbr[(first + u) * fan + k]] for k in range(fan)]
            tile = prior[pl.ds((first + u) * fan, fan)]
            tile = tile.reshape(fan * tile.shape[1], tile.shape[2])
            out[first + u] = matmul(jnp.concatenate(row, axis=1), tile).astype(HALF)
        return 0

    lax.fori_loop(0, tiles // chunk, one, 0)


def spread_tiles(core, nbr, fields, prior):
    summed = len(fields) > 1
    ext_tiles, probes, width = fields[0].shape
    tiles = ext_tiles // 2
    smem = pl.BlockSpec(memory_space=pltpu.SMEM)
    vmem = pl.BlockSpec(memory_space=pltpu.VMEM)
    return pl.pallas_call(
        functools.partial(spread_kernel, summed, nbr.shape[0] // tiles),
        in_specs=[smem, smem] + [vmem] * len(fields) + [vmem],
        out_specs=vmem,
        out_shape=jax.ShapeDtypeStruct((tiles, probes, width), HALF),
        scratch_shapes=[pltpu.VMEM(fields[0].shape, HALF)] if summed else [],
        compiler_params=pltpu.CompilerParams(vmem_limit_bytes=VMEM_LIMIT),
        name="prior_spread",
    )(core, nbr, *fields, prior)


def shards(probes, prior_tiles, neighbours, jac, jac_obs, jac_flux, counts, rinv):
    n_obs, n_flux = lax.axis_size("obs"), lax.axis_size("flux")
    tile_count = probes.shape[0]
    half = tile_count // 2
    reach = tile_count // 4
    obs_rows = rinv.shape[0]
    quarter = obs_rows // 4
    blocks = jac[0, 0]
    flux_at = lax.axis_index("flux")
    side = lax.rem(lax.axis_index("obs"), 2)
    corner = lax.rem(flux_at, 4)
    core = side.reshape(1)

    live = jnp.arange(blocks.shape[0], dtype=jnp.int32) < counts[0, 0]
    obs_all, flux_all = jac_obs[0, 0], jac_flux[0, 0]
    obs_at = ((obs_all // quarter) ^ corner) * quarter + obs_all % quarter
    tile_at = ((flux_all // half) ^ side) * half + flux_all % half
    own_rinv = lax.dynamic_slice_in_dim(rinv, corner * quarter, quarter, 0)[:, None, :]
    first_tile = flux_at * tile_count + side * half
    own_nbr = lax.dynamic_slice_in_dim(neighbours, side * half, half, 0)
    nbr = (own_nbr - first_tile + reach).reshape(-1)
    fan = neighbours.shape[1]
    prior = prior_tiles.reshape((tile_count * fan,) + prior_tiles.shape[2:])

    prior_plain, prior_turned = setup_blocks(core * (half * fan), half * fan, prior, "prior_setup")
    jac_plain, jac_turned = setup_blocks(jnp.zeros((1,), jnp.int32), blocks.shape[0], blocks, "jac_setup")

    rows = max(obs_rows, tile_count)
    count = max(blocks.shape[0], half * fan)

    def fill(value, more):
        return jnp.pad(value, (0, count - value.shape[0]), constant_values=more)

    prior_src = jnp.arange(half * fan, dtype=jnp.int32) // fan
    plans = plan_groups(
        jnp.stack([fill(tile_at, 0), fill(obs_at, 0), fill(prior_src, 0)]),
        jnp.stack(
            [
                fill(jnp.where(live, obs_at, rows), rows),
                fill(jnp.where(live, tile_at, rows), rows),
                fill(nbr, rows),
            ]
        ),
        rows,
        rows,
    )
    obs_plan, tile_plan, prior_plan = plans[0], plans[1], plans[2]

    def swap_core(value):
        return exchange(value, lambda i, j: (i ^ 1, j))

    def swap_far(value):
        def partner(i, j):
            to = j - 1 if i % 2 == 0 else j + 1
            return (i ^ 1, to) if 0 <= to < n_flux else None

        return exchange(value, partner)

    def swap_flux(value, bits):
        return exchange(value, lambda i, j: (i, j ^ bits))

    edge = jnp.where(side == 0, probes[:reach], probes[tile_count - reach :])
    beyond = swap_far(edge)
    around = jnp.concatenate([beyond, probes, beyond], axis=0)
    fields = (lax.dynamic_slice_in_dim(around, side * half, 2 * half, 0),)
    for step in range(STEPS):
        spread = spread_tiles(core, nbr, fields, prior_plain)
        parts = (spread, swap_core(spread))
        pieces = jac_pass(obs_plan, parts, jac_plain, rows, rows, obs_rows, 4, "jac_forward")
        total = pieces[0]
        for bits in range(1, 4):
            total = total + swap_flux(pieces[bits], bits).astype(F32)
        bits = 4
        while bits < n_flux:
            sent = total.astype(HALF)
            total = sent.astype(F32) + swap_flux(sent, bits).astype(F32)
            bits *= 2
        weighted = (total * own_rinv).astype(HALF)
        parts = (weighted,) + tuple(swap_flux(weighted, bits) for bits in range(1, 4))
        mine, theirs = jac_pass(tile_plan, parts, jac_turned, rows, rows, tile_count, 2, "jac_adjoint")
        mine = (mine + swap_core(theirs).astype(F32)).astype(HALF)
        bits = 2
        while bits < n_obs:
            other = exchange(mine, lambda i, j, bits=bits: (i ^ bits, j))
            bits *= 2
            if bits < n_obs:
                mine = (mine.astype(F32) + other.astype(F32)).astype(HALF)
        ext, to_core, to_far = gather_tiles(core, prior_plan, mine, other, prior_turned, rows, rows)
        fields = (ext, swap_core(to_core), swap_far(to_far))
    ext, from_core, from_far = fields
    low = jnp.where(side == 0, from_far, from_core).astype(F32)
    high = jnp.where(side == 0, from_core, from_far).astype(F32)
    own = (ext + jnp.concatenate([low, high], axis=0))[reach : reach + half].astype(HALF)
    other = swap_core(own)
    first = jnp.where(side == 0, own, other)
    second = jnp.where(side == 0, other, own)
    return jnp.concatenate([first, second], axis=0)


def solution(mesh):
    placed = (
        P("flux", None, None),
        P("flux", None, None, None),
        P("flux", None),
        P("obs", "flux", None, None, None),
        P("obs", "flux", None),
        P("obs", "flux", None),
        P("obs", "flux"),
        P("obs", None),
    )
    return jax.shard_map(
        shards, mesh=mesh, in_specs=placed, out_specs=P("flux", None, None), check_vma=False
    )
```

```python
import functools

import jax
import jax.numpy as jnp
from jax import lax
from jax.experimental import pallas as pl
from jax.experimental.pallas import tpu as pltpu
from jax.sharding import PartitionSpec as P

STEPS = 4
F32 = jnp.float32
HALF = jnp.bfloat16
VMEM_LIMIT = 8 * 2**20
GROUP = 4
ROUND = 24


def matmul(a, b):
    return lax.dot_general(a, b, (((1,), (0,)), ((), ())), preferred_element_type=F32)


def chunk_of(count, most):
    return max(c for c in range(1, most + 1) if count % c == 0)


def exchange(value, partner):
    n_obs, n_flux = lax.axis_size("obs"), lax.axis_size("flux")
    route = []
    for i in range(n_obs):
        for j in range(n_flux):
            to = partner(i, j)
            if to is not None:
                route.append((i * n_flux + j, to[0] * n_flux + to[1]))
    return lax.ppermute(value, ("obs", "flux"), route)


def plan_groups(src, dst, src_rows, dst_rows):
    passes, blocks = dst.shape
    groups = blocks // GROUP + dst_rows
    groups += -groups % ROUND
    slots = groups * GROUP
    i32 = jnp.int32
    at = jnp.arange(blocks, dtype=i32)
    rows = jnp.arange(dst_rows, dtype=i32)
    same = (dst[:, :, None] == dst[:, None, :]) & (at[None, :] < at[:, None])
    rank = jnp.sum(same.astype(i32), axis=2)
    member = (dst[:, None, :] == rows[:, None]).astype(i32)
    fills = (jnp.sum(member, axis=2) + GROUP - 1) // GROUP
    begin = jnp.sum(jnp.where(rows[None, :] < rows[:, None], fills[:, None, :], 0), axis=2)
    place = jnp.sum(member * begin[:, :, None], axis=1) * GROUP + rank
    place = jnp.where(dst < dst_rows, place, slots)
    hit = place[:, None, :] == jnp.arange(slots, dtype=i32)[:, None]
    src_of = jnp.sum(jnp.where(hit, (src - src_rows)[:, None, :], 0), axis=2) + src_rows
    block_of = jnp.sum(jnp.where(hit, at, 0), axis=2)
    lead = place[:, None, :] == jnp.arange(groups, dtype=i32)[:, None] * GROUP
    dst_of = jnp.sum(jnp.where(lead, (dst - dst_rows)[:, None, :], 0), axis=2) + dst_rows
    rounds = (jnp.sum(fills, axis=1, keepdims=True) + ROUND - 1) // ROUND
    return jnp.concatenate([src_of, block_of, dst_of, rounds], axis=1)


def setup_kernel(chunk, first, source, plain, turned, sems):
    begin = first[0]

    def copy(c):
        at = pl.ds(c * chunk, chunk)
        rows = pl.ds(begin + c * chunk, chunk)
        return pltpu.make_async_copy(source.at[rows], plain.at[at], sems.at[c])

    def start(c, _):
        copy(c).start()
        return 0

    def turn(c, _):
        copy(c).wait()
        for u in range(chunk):
            turned[c * chunk + u] = plain[c * chunk + u].T
        return 0

    lax.fori_loop(0, plain.shape[0] // chunk, start, 0)
    lax.fori_loop(0, plain.shape[0] // chunk, turn, 0)


def setup_blocks(first, count, source, name):
    shape = (count,) + source.shape[1:]
    chunk = chunk_of(count, 24)
    vmem = pl.BlockSpec(memory_space=pltpu.VMEM)
    return pl.pallas_call(
        functools.partial(setup_kernel, chunk),
        in_specs=[pl.BlockSpec(memory_space=pltpu.SMEM), pl.BlockSpec(memory_space=pl.ANY)],
        out_specs=[vmem, vmem],
        out_shape=[pltpu.VMEM(shape, HALF), pltpu.VMEM(shape, HALF)],
        scratch_shapes=[pltpu.SemaphoreType.DMA((count // chunk,))],
        compiler_params=pltpu.CompilerParams(vmem_limit_bytes=VMEM_LIMIT),
        name=name,
    )(first, pltpu.with_memory_space_constraint(source, pltpu.HBM))


def grouped_products(plan, x, blocks, total):
    slots = (plan.shape[0] - 1) // (2 * GROUP + 1) * GROUP
    total[...] = jnp.zeros_like(total)

    def one(c, _):
        products = []
        for u in range(ROUND):
            first = (c * ROUND + u) * GROUP
            rows = [x[plan[first + g]] for g in range(GROUP)]
            tiles = [blocks[plan[slots + first + g]] for g in range(GROUP)]
            left = jnp.concatenate(rows, axis=1)
            products.append(matmul(left, jnp.concatenate(tiles, axis=0)))
        for u in range(ROUND):
            total[plan[2 * slots + c * ROUND + u]] += products[u]
        return 0

    lax.fori_loop(0, plan[plan.shape[0] - 1], one, 0)


def jac_kernel(n_parts, n_outs, plan, *refs):
    parts = refs[:n_parts]
    jac = refs[n_parts]
    outs = refs[n_parts + 1 : n_parts + 1 + n_outs]
    x, total = refs[n_parts + 1 + n_outs :]
    rows = parts[0].shape[0]
    for k, part in enumerate(parts):
        x[k * rows : (k + 1) * rows] = part[...]
    for r in range(n_parts * rows, x.shape[0]):
        x[r] = jnp.zeros(x.shape[1:], HALF)
    grouped_products(plan, x, jac, total)
    rows = outs[0].shape[0]
    for k, out in enumerate(outs):
        out[...] = total[k * rows : (k + 1) * rows].astype(out.dtype)


def jac_pass(plan, parts, jac, src_rows, dst_rows, out_rows, n_outs, name):
    probes, width = parts[0].shape[1:]
    smem = pl.BlockSpec(memory_space=pltpu.SMEM)
    vmem = pl.BlockSpec(memory_space=pltpu.VMEM)
    out = (out_rows // n_outs, probes, width)
    return pl.pallas_call(
        functools.partial(jac_kernel, len(parts), n_outs),
        in_specs=[smem] + [vmem] * len(parts) + [vmem],
        out_specs=[vmem] * n_outs,
        out_shape=[jax.ShapeDtypeStruct(out, F32 if k == 0 else HALF) for k in range(n_outs)],
        scratch_shapes=[
            pltpu.VMEM((src_rows + 1, probes, width), HALF),
            pltpu.VMEM((dst_rows + 1, probes, width), F32),
        ],
        compiler_params=pltpu.CompilerParams(vmem_limit_bytes=VMEM_LIMIT),
        name=name,
    )(plan, *parts, jac)


def gather_kernel(src_rows, core, plan, mine, other, prior, ext, to_core, to_far, x, total):
    half = mine.shape[0]
    side = core[0]
    x[:half] = (mine[...].astype(F32) + other[...].astype(F32)).astype(HALF)
    x[src_rows] = jnp.zeros(x.shape[1:], HALF)
    grouped_products(plan, x, prior, total)
    ext[...] = total[: 2 * half]
    to_core[...] = total[pl.ds(half * (1 - side), half)].astype(HALF)
    to_far[...] = total[pl.ds(half * side, half)].astype(HALF)


def gather_tiles(core, plan, mine, other, prior, src_rows, dst_rows):
    tiles, probes, width = mine.shape
    smem = pl.BlockSpec(memory_space=pltpu.SMEM)
    vmem = pl.BlockSpec(memory_space=pltpu.VMEM)
    return pl.pallas_call(
        functools.partial(gather_kernel, src_rows),
        in_specs=[smem, smem, vmem, vmem, vmem],
        out_specs=[vmem] * 3,
        out_shape=[
            jax.ShapeDtypeStruct((2 * tiles, probes, width), F32),
            jax.ShapeDtypeStruct((tiles, probes, width), HALF),
            jax.ShapeDtypeStruct((tiles, probes, width), HALF),
        ],
        scratch_shapes=[
            pltpu.VMEM((src_rows + 1, probes, width), HALF),
            pltpu.VMEM((dst_rows + 1, probes, width), F32),
        ],
        compiler_params=pltpu.CompilerParams(vmem_limit_bytes=VMEM_LIMIT),
        name="prior_adjoint",
    )(core, plan, mine, other, prior)


def spread_kernel(summed, fan, core, nbr, *refs):
    if summed:
        ext, from_core, from_far, prior, out, field = refs
    else:
        field, prior, out = refs
    tiles = out.shape[0]
    chunk = chunk_of(tiles, 12)
    side = core[0]
    if summed:
        for begin, update in ((tiles * (1 - side), from_core), (tiles * side, from_far)):
            at = pl.ds(begin, tiles)
            field[at] = (ext[at] + update[...].astype(F32)).astype(HALF)

    def one(c, _):
        first = c * chunk
        for u in range(chunk):
            row = [field[nbr[(first + u) * fan + k]] for k in range(fan)]
            tile = prior[pl.ds((first + u) * fan, fan)]
            tile = tile.reshape(fan * tile.shape[1], tile.shape[2])
            out[first + u] = matmul(jnp.concatenate(row, axis=1), tile).astype(HALF)
        return 0

    lax.fori_loop(0, tiles // chunk, one, 0)


def spread_tiles(core, nbr, fields, prior):
    summed = len(fields) > 1
    ext_tiles, probes, width = fields[0].shape
    tiles = ext_tiles // 2
    smem = pl.BlockSpec(memory_space=pltpu.SMEM)
    vmem = pl.BlockSpec(memory_space=pltpu.VMEM)
    return pl.pallas_call(
        functools.partial(spread_kernel, summed, nbr.shape[0] // tiles),
        in_specs=[smem, smem] + [vmem] * len(fields) + [vmem],
        out_specs=vmem,
        out_shape=jax.ShapeDtypeStruct((tiles, probes, width), HALF),
        scratch_shapes=[pltpu.VMEM(fields[0].shape, HALF)] if summed else [],
        compiler_params=pltpu.CompilerParams(vmem_limit_bytes=VMEM_LIMIT),
        name="prior_spread",
    )(core, nbr, *fields, prior)


def shards(probes, prior_tiles, neighbours, jac, jac_obs, jac_flux, counts, rinv):
    n_obs, n_flux = lax.axis_size("obs"), lax.axis_size("flux")
    tile_count = probes.shape[0]
    half = tile_count // 2
    reach = tile_count // 4
    obs_rows = rinv.shape[0]
    quarter = obs_rows // 4
    blocks = jac[0, 0]
    flux_at = lax.axis_index("flux")
    side = lax.rem(lax.axis_index("obs"), 2)
    corner = lax.rem(flux_at, 4)
    core = side.reshape(1)

    live = jnp.arange(blocks.shape[0], dtype=jnp.int32) < counts[0, 0]
    obs_all, flux_all = jac_obs[0, 0], jac_flux[0, 0]
    obs_at = ((obs_all // quarter) ^ corner) * quarter + obs_all % quarter
    tile_at = ((flux_all // half) ^ side) * half + flux_all % half
    own_rinv = lax.dynamic_slice_in_dim(rinv, corner * quarter, quarter, 0)[:, None, :]
    first_tile = flux_at * tile_count + side * half
    own_nbr = lax.dynamic_slice_in_dim(neighbours, side * half, half, 0)
    nbr = (own_nbr - first_tile + reach).reshape(-1)
    fan = neighbours.shape[1]
    prior = prior_tiles.reshape((tile_count * fan,) + prior_tiles.shape[2:])

    rows = max(obs_rows, tile_count)
    count = max(blocks.shape[0], half * fan)

    def fill(value, more):
        return jnp.pad(value, (0, count - value.shape[0]), constant_values=more)

    prior_src = jnp.arange(half * fan, dtype=jnp.int32) // fan
    plans = plan_groups(
        jnp.stack([fill(tile_at, 0), fill(obs_at, 0), fill(prior_src, 0)]),
        jnp.stack(
            [
                fill(jnp.where(live, obs_at, rows), rows),
                fill(jnp.where(live, tile_at, rows), rows),
                fill(nbr, rows),
            ]
        ),
        rows,
        rows,
    )

    def swap_core(value):
        return exchange(value, lambda i, j: (i ^ 1, j))

    def swap_far(value):
        def partner(i, j):
            to = j - 1 if i % 2 == 0 else j + 1
            return (i ^ 1, to) if 0 <= to < n_flux else None

        return exchange(value, partner)

    def swap_flux(value, bits):
        return exchange(value, lambda i, j: (i, j ^ bits))

    edge = jnp.where(side == 0, probes[:reach], probes[tile_count - reach :])
    beyond = swap_far(edge)
    around = jnp.concatenate([beyond, probes, beyond], axis=0)
    field = lax.dynamic_slice_in_dim(around, side * half, 2 * half, 0)

    core, begin, nbr, obs_plan, tile_plan, prior_plan, own_rinv, field, blocks, prior = (
        lax.optimization_barrier(
            (core, core * (half * fan), nbr, plans[0], plans[1], plans[2], own_rinv, field, blocks, prior)
        )
    )
    prior_plain, prior_turned = setup_blocks(begin, half * fan, prior, "prior_setup")
    jac_plain, jac_turned = setup_blocks(begin * 0, blocks.shape[0], blocks, "jac_setup")
    fields = (field,)
    for step in range(STEPS):
        spread = spread_tiles(core, nbr, fields, prior_plain)
        parts = (spread, swap_core(spread))
        pieces = jac_pass(obs_plan, parts, jac_plain, rows, rows, obs_rows, 4, "jac_forward")
        total = pieces[0]
        for bits in range(1, 4):
            total = total + swap_flux(pieces[bits], bits).astype(F32)
        bits = 4
        while bits < n_flux:
            sent = total.astype(HALF)
            total = sent.astype(F32) + swap_flux(sent, bits).astype(F32)
            bits *= 2
        weighted = (total * own_rinv).astype(HALF)
        parts = (weighted,) + tuple(swap_flux(weighted, bits) for bits in range(1, 4))
        mine, theirs = jac_pass(tile_plan, parts, jac_turned, rows, rows, tile_count, 2, "jac_adjoint")
        mine = (mine + swap_core(theirs).astype(F32)).astype(HALF)
        bits = 2
        while bits < n_obs:
            other = exchange(mine, lambda i, j, bits=bits: (i ^ bits, j))
            bits *= 2
            if bits < n_obs:
                mine = (mine.astype(F32) + other.astype(F32)).astype(HALF)
        ext, to_core, to_far = gather_tiles(core, prior_plan, mine, other, prior_turned, rows, rows)
        fields = (ext, swap_core(to_core), swap_far(to_far))
    ext, from_core, from_far = fields
    low = jnp.where(side == 0, from_far, from_core).astype(F32)
    high = jnp.where(side == 0, from_core, from_far).astype(F32)
    own = (ext + jnp.concatenate([low, high], axis=0))[reach : reach + half].astype(HALF)
    other = swap_core(own)
    first = jnp.where(side == 0, own, other)
    second = jnp.where(side == 0, other, own)
    return jnp.concatenate([first, second], axis=0)


def solution(mesh):
    placed = (
        P("flux", None, None),
        P("flux", None, None, None),
        P("flux", None),
        P("obs", "flux", None, None, None),
        P("obs", "flux", None),
        P("obs", "flux", None),
        P("obs", "flux"),
        P("obs", None),
    )
    return jax.shard_map(
        shards, mesh=mesh, in_specs=placed, out_specs=P("flux", None, None), check_vma=False
    )
```

```python
import functools
import math

import jax
import jax.numpy as jnp
from jax import lax
from jax.experimental import pallas as pl
from jax.experimental.pallas import tpu as pltpu
from jax.sharding import PartitionSpec as P

STEPS = 4
F32 = jnp.float32
HALF = jnp.bfloat16
VMEM_LIMIT = 8 * 2**20
GROUP = 4
ROUND = 24
LANES = 128


def matmul(a, b):
    return lax.dot_general(a, b, (((1,), (0,)), ((), ())), preferred_element_type=F32)


def chunk_of(count, most):
    return max(c for c in range(1, most + 1) if count % c == 0)


def exchange(value, partner):
    n_obs, n_flux = lax.axis_size("obs"), lax.axis_size("flux")
    route = []
    for i in range(n_obs):
        for j in range(n_flux):
            to = partner(i, j)
            if to is not None:
                route.append((i * n_flux + j, to[0] * n_flux + to[1]))
    return lax.ppermute(value, ("obs", "flux"), route)


def plan_sizes(blocks, dst_rows):
    groups = (blocks + -blocks % LANES) // GROUP + dst_rows
    groups += -groups % ROUND
    slots = groups * GROUP
    return slots + -slots % LANES, groups + 1 + -(groups + 1) % LANES


def columns(row):
    parts = [
        jnp.broadcast_to(row[:, k : k + LANES], (LANES, LANES)).T for k in range(0, row.shape[1], LANES)
    ]
    return jnp.concatenate(parts, axis=0)


def plan_groups(src, dst, rows, out):
    blocks = dst.shape[1]
    slots, groups = plan_sizes(blocks, rows)
    i32 = jnp.int32
    lane = lax.broadcasted_iota(i32, (blocks, LANES), 1)
    at = lax.broadcasted_iota(i32, (blocks, LANES), 0)
    src_at, dst_at = columns(src), columns(dst)
    rank = jnp.zeros((blocks, LANES), F32)
    for k in range(0, blocks, LANES):
        same = (dst_at == dst[:, k : k + LANES]) & (lane + k < at)
        rank += same.astype(F32)
    rank = jnp.sum(rank, axis=1, keepdims=True)
    fills = jnp.sum((dst_at == lane).astype(F32), axis=0, keepdims=True)
    sizes = jnp.where(lane[:1] < rows, jnp.floor((fills + (GROUP - 1)) * (1.0 / GROUP)), 0.0)
    begin = jnp.sum(jnp.where(lane < dst_at, sizes, 0.0), axis=1, keepdims=True)
    place = (begin * GROUP + rank).astype(i32)
    place = jnp.where(dst_at < rows, place, slots)
    for k in range(0, slots, LANES):
        hit = place == lane + k
        of = jnp.sum(jnp.where(hit, (src_at - rows).astype(F32), 0.0), axis=0, keepdims=True)
        out[:, k : k + LANES] = of.astype(i32) + rows
        of = jnp.sum(jnp.where(hit, at.astype(F32), 0.0), axis=0, keepdims=True)
        out[:, slots + k : slots + k + LANES] = of.astype(i32)
    full = jnp.sum(sizes, axis=1, keepdims=True)
    rounds = jnp.sum((lane[:1].astype(F32) * ROUND < full).astype(F32), axis=1, keepdims=True)
    for k in range(0, groups, LANES):
        lead = place == (lane + k) * GROUP
        of = jnp.sum(jnp.where(lead, (dst_at - rows).astype(F32), 0.0), axis=0, keepdims=True)
        of = jnp.where(lane[:1] + k == groups - 1, rounds, of + rows)
        out[:, 2 * slots + k : 2 * slots + k + LANES] = of.astype(i32)


def setup_kernel(
    rows, chunk, where, obs, flux, nbr, prior, jac,
    prior_plain, prior_turned, jac_plain, jac_turned, obs_plan, tile_plan, prior_plan, sems
):
    side, corner, count = where[0], where[1], where[2]
    begin = side * prior_plain.shape[0]
    rounds = (prior_plain.shape[0] // chunk, jac_plain.shape[0] // chunk)

    def copy(c, first, source, plain, offset):
        to = pl.ds(c * chunk, chunk)
        return pltpu.make_async_copy(source.at[pl.ds(first + c * chunk, chunk)], plain.at[to], sems.at[offset + c])

    def start(first, source, plain, offset):
        def one(c, _):
            copy(c, first, source, plain, offset).start()
            return 0

        return one

    def turn(first, source, plain, turned, offset):
        def one(c, _):
            copy(c, first, source, plain, offset).wait()
            for u in range(chunk):
                turned[c * chunk + u] = plain[c * chunk + u].T
            return 0

        return one

    lax.fori_loop(0, rounds[0], start(begin, prior, prior_plain, 0), 0)
    lax.fori_loop(0, rounds[1], start(0, jac, jac_plain, rounds[0]), 0)

    blocks = obs.shape[1]
    obs_rows, tile_rows, fan = rows
    half = tile_rows // 2
    quarter = obs_rows // 4
    most = max(obs_rows, tile_rows)
    i32 = jnp.int32
    at = lax.broadcasted_iota(i32, (1, blocks), 1)
    live = at < count
    block = sum((obs[...] >= k * quarter).astype(i32) for k in range(1, 4))
    obs_at = (block ^ corner) * quarter + obs[...] - block * quarter
    block = (flux[...] >= half).astype(i32)
    tile_at = (block ^ side) * half + flux[...] - block * half
    plan_groups(tile_at, jnp.where(live, obs_at, most), most, obs_plan)
    plan_groups(obs_at, jnp.where(live, tile_at, most), most, tile_plan)
    at = lax.broadcasted_iota(i32, nbr.shape, 1)
    tile = sum((at >= k * fan).astype(i32) for k in range(1, half))
    plan_groups(tile, nbr[...], most, prior_plan)

    lax.fori_loop(0, rounds[0], turn(begin, prior, prior_plain, prior_turned, 0), 0)
    lax.fori_loop(0, rounds[1], turn(0, jac, jac_plain, jac_turned, rounds[0]), 0)


def setup(where, obs, flux, nbr, prior, jac, rows):
    most = max(rows[:2])
    tiles = rows[1] // 2 * rows[2]
    chunk = chunk_of(math.gcd(tiles, jac.shape[0]), 24)
    smem = pl.BlockSpec(memory_space=pltpu.SMEM)
    vmem = pl.BlockSpec(memory_space=pltpu.VMEM)
    hbm = pl.BlockSpec(memory_space=pl.ANY)
    own = pltpu.VMEM((tiles,) + prior.shape[1:], HALF)
    all_blocks = pltpu.VMEM(jac.shape, HALF)
    plans = []
    for width in (obs.shape[1], obs.shape[1], nbr.shape[1]):
        slots, groups = plan_sizes(width, most)
        plans.append(jax.ShapeDtypeStruct((1, 2 * slots + groups), jnp.int32))
    return pl.pallas_call(
        functools.partial(setup_kernel, rows, chunk),
        in_specs=[smem, vmem, vmem, vmem, hbm, hbm],
        out_specs=[vmem] * 7,
        out_shape=[own, own, all_blocks, all_blocks] + plans,
        scratch_shapes=[pltpu.SemaphoreType.DMA(((tiles + jac.shape[0]) // chunk,))],
        compiler_params=pltpu.CompilerParams(vmem_limit_bytes=VMEM_LIMIT),
        name="setup",
    )(
        where,
        obs,
        flux,
        nbr,
        pltpu.with_memory_space_constraint(prior, pltpu.HBM),
        pltpu.with_memory_space_constraint(jac, pltpu.HBM),
    )


def grouped_products(plan, x, blocks, total):
    slots, groups = plan_sizes(blocks.shape[0], x.shape[0] - 1)
    total[...] = jnp.zeros_like(total)

    def one(c, _):
        products = []
        for u in range(ROUND):
            first = (c * ROUND + u) * GROUP
            rows = [x[plan[0, first + g]] for g in range(GROUP)]
            tiles = [blocks[plan[0, slots + first + g]] for g in range(GROUP)]
            left = jnp.concatenate(rows, axis=1)
            products.append(matmul(left, jnp.concatenate(tiles, axis=0)))
        for u in range(ROUND):
            total[plan[0, 2 * slots + c * ROUND + u]] += products[u]
        return 0

    lax.fori_loop(0, plan[0, 2 * slots + groups - 1], one, 0)


def jac_kernel(n_parts, n_outs, plan, *refs):
    parts = refs[:n_parts]
    jac = refs[n_parts]
    outs = refs[n_parts + 1 : n_parts + 1 + n_outs]
    x, total = refs[n_parts + 1 + n_outs :]
    rows = parts[0].shape[0]
    for k, part in enumerate(parts):
        x[k * rows : (k + 1) * rows] = part[...]
    for r in range(n_parts * rows, x.shape[0]):
        x[r] = jnp.zeros(x.shape[1:], HALF)
    grouped_products(plan, x, jac, total)
    rows = outs[0].shape[0]
    for k, out in enumerate(outs):
        out[...] = total[k * rows : (k + 1) * rows].astype(out.dtype)


def jac_pass(plan, parts, jac, src_rows, dst_rows, out_rows, n_outs, name):
    probes, width = parts[0].shape[1:]
    smem = pl.BlockSpec(memory_space=pltpu.SMEM)
    vmem = pl.BlockSpec(memory_space=pltpu.VMEM)
    out = (out_rows // n_outs, probes, width)
    return pl.pallas_call(
        functools.partial(jac_kernel, len(parts), n_outs),
        in_specs=[smem] + [vmem] * len(parts) + [vmem],
        out_specs=[vmem] * n_outs,
        out_shape=[jax.ShapeDtypeStruct(out, F32 if k == 0 else HALF) for k in range(n_outs)],
        scratch_shapes=[
            pltpu.VMEM((src_rows + 1, probes, width), HALF),
            pltpu.VMEM((dst_rows + 1, probes, width), F32),
        ],
        compiler_params=pltpu.CompilerParams(vmem_limit_bytes=VMEM_LIMIT),
        name=name,
    )(plan, *parts, jac)


def gather_kernel(src_rows, core, plan, mine, other, prior, ext, to_core, to_far, x, total):
    half = mine.shape[0]
    side = core[0]
    x[:half] = (mine[...].astype(F32) + other[...].astype(F32)).astype(HALF)
    x[src_rows] = jnp.zeros(x.shape[1:], HALF)
    grouped_products(plan, x, prior, total)
    ext[...] = total[: 2 * half]
    to_core[...] = total[pl.ds(half * (1 - side), half)].astype(HALF)
    to_far[...] = total[pl.ds(half * side, half)].astype(HALF)


def gather_tiles(core, plan, mine, other, prior, src_rows, dst_rows):
    tiles, probes, width = mine.shape
    smem = pl.BlockSpec(memory_space=pltpu.SMEM)
    vmem = pl.BlockSpec(memory_space=pltpu.VMEM)
    return pl.pallas_call(
        functools.partial(gather_kernel, src_rows),
        in_specs=[smem, smem, vmem, vmem, vmem],
        out_specs=[vmem] * 3,
        out_shape=[
            jax.ShapeDtypeStruct((2 * tiles, probes, width), F32),
            jax.ShapeDtypeStruct((tiles, probes, width), HALF),
            jax.ShapeDtypeStruct((tiles, probes, width), HALF),
        ],
        scratch_shapes=[
            pltpu.VMEM((src_rows + 1, probes, width), HALF),
            pltpu.VMEM((dst_rows + 1, probes, width), F32),
        ],
        compiler_params=pltpu.CompilerParams(vmem_limit_bytes=VMEM_LIMIT),
        name="prior_adjoint",
    )(core, plan, mine, other, prior)


def spread_kernel(summed, fan, core, nbr, *refs):
    if summed:
        ext, from_core, from_far, prior, out, field = refs
    else:
        field, prior, out = refs
    tiles = out.shape[0]
    chunk = chunk_of(tiles, 12)
    side = core[0]
    if summed:
        for begin, update in ((tiles * (1 - side), from_core), (tiles * side, from_far)):
            at = pl.ds(begin, tiles)
            field[at] = (ext[at] + update[...].astype(F32)).astype(HALF)

    def one(c, _):
        first = c * chunk
        for u in range(chunk):
            row = [field[nbr[(first + u) * fan + k]] for k in range(fan)]
            tile = prior[pl.ds((first + u) * fan, fan)]
            tile = tile.reshape(fan * tile.shape[1], tile.shape[2])
            out[first + u] = matmul(jnp.concatenate(row, axis=1), tile).astype(HALF)
        return 0

    lax.fori_loop(0, tiles // chunk, one, 0)


def spread_tiles(core, nbr, fields, prior):
    summed = len(fields) > 1
    ext_tiles, probes, width = fields[0].shape
    tiles = ext_tiles // 2
    smem = pl.BlockSpec(memory_space=pltpu.SMEM)
    vmem = pl.BlockSpec(memory_space=pltpu.VMEM)
    return pl.pallas_call(
        functools.partial(spread_kernel, summed, nbr.shape[0] // tiles),
        in_specs=[smem, smem] + [vmem] * len(fields) + [vmem],
        out_specs=vmem,
        out_shape=jax.ShapeDtypeStruct((tiles, probes, width), HALF),
        scratch_shapes=[pltpu.VMEM(fields[0].shape, HALF)] if summed else [],
        compiler_params=pltpu.CompilerParams(vmem_limit_bytes=VMEM_LIMIT),
        name="prior_spread",
    )(core, nbr, *fields, prior)


def shards(probes, prior_tiles, neighbours, jac, jac_obs, jac_flux, counts, rinv):
    n_obs, n_flux = lax.axis_size("obs"), lax.axis_size("flux")
    tile_count = probes.shape[0]
    half = tile_count // 2
    reach = tile_count // 4
    obs_rows = rinv.shape[0]
    quarter = obs_rows // 4
    blocks = jac[0, 0]
    flux_at = lax.axis_index("flux")
    side = lax.rem(lax.axis_index("obs"), 2)
    corner = lax.rem(flux_at, 4)
    core = side.reshape(1)

    own_rinv = lax.dynamic_slice_in_dim(rinv, corner * quarter, quarter, 0)[:, None, :]
    first_tile = flux_at * tile_count + side * half
    own_nbr = lax.dynamic_slice_in_dim(neighbours, side * half, half, 0)
    nbr = (own_nbr - first_tile + reach).reshape(-1)
    fan = neighbours.shape[1]
    prior = prior_tiles.reshape((tile_count * fan,) + prior_tiles.shape[2:])

    rows = max(obs_rows, tile_count)

    def swap_core(value):
        return exchange(value, lambda i, j: (i ^ 1, j))

    def swap_far(value):
        def partner(i, j):
            to = j - 1 if i % 2 == 0 else j + 1
            return (i ^ 1, to) if 0 <= to < n_flux else None

        return exchange(value, partner)

    def swap_flux(value, bits):
        return exchange(value, lambda i, j: (i, j ^ bits))

    edge = jnp.where(side == 0, probes[:reach], probes[tile_count - reach :])
    beyond = swap_far(edge)
    around = jnp.concatenate([beyond, probes, beyond], axis=0)
    field = lax.dynamic_slice_in_dim(around, side * half, 2 * half, 0)

    where = jnp.stack([side, corner, counts[0, 0]])
    width = nbr.shape[0] + -nbr.shape[0] % LANES
    nbr_row = jnp.pad(nbr, (0, width - nbr.shape[0]), constant_values=rows).reshape(1, width)
    sizes = (obs_rows, tile_count, fan)

    core, nbr, nbr_row, where, own_rinv, field, prior, blocks = lax.optimization_barrier(
        (core, nbr, nbr_row, where, own_rinv, field, prior, blocks)
    )
    prior_plain, prior_turned, jac_plain, jac_turned, obs_plan, tile_plan, prior_plan = setup(
        where, jac_obs[0], jac_flux[0], nbr_row, prior, blocks, sizes
    )
    fields = (field,)
    for step in range(STEPS):
        spread = spread_tiles(core, nbr, fields, prior_plain)
        parts = (spread, swap_core(spread))
        pieces = jac_pass(obs_plan, parts, jac_plain, rows, rows, obs_rows, 4, "jac_forward")
        total = pieces[0]
        for bits in range(1, 4):
            total = total + swap_flux(pieces[bits], bits).astype(F32)
        bits = 4
        while bits < n_flux:
            sent = total.astype(HALF)
            total = sent.astype(F32) + swap_flux(sent, bits).astype(F32)
            bits *= 2
        weighted = (total * own_rinv).astype(HALF)
        parts = (weighted,) + tuple(swap_flux(weighted, bits) for bits in range(1, 4))
        mine, theirs = jac_pass(tile_plan, parts, jac_turned, rows, rows, tile_count, 2, "jac_adjoint")
        mine = (mine + swap_core(theirs).astype(F32)).astype(HALF)
        bits = 2
        while bits < n_obs:
            other = exchange(mine, lambda i, j, bits=bits: (i ^ bits, j))
            bits *= 2
            if bits < n_obs:
                mine = (mine.astype(F32) + other.astype(F32)).astype(HALF)
        ext, to_core, to_far = gather_tiles(core, prior_plan, mine, other, prior_turned, rows, rows)
        if step < STEPS - 1:
            fields = (ext, swap_core(to_core), swap_far(to_far))
    lower = side == 0
    from_core = swap_core(jnp.where(lower, to_core[half - reach :], to_core[:reach])).astype(F32)
    from_far = swap_far(jnp.where(lower, to_far[:reach], to_far[half - reach :])).astype(F32)
    low = jnp.where(lower, from_far, from_core)
    high = jnp.where(lower, from_core, from_far)
    own = (ext[reach : reach + half] + jnp.concatenate([low, high], axis=0)).astype(HALF)
    other = swap_core(own)
    first = jnp.where(side == 0, own, other)
    second = jnp.where(side == 0, other, own)
    return jnp.concatenate([first, second], axis=0)


def solution(mesh):
    placed = (
        P("flux", None, None),
        P("flux", None, None, None),
        P("flux", None),
        P("obs", "flux", None, None, None),
        P("obs", "flux", None),
        P("obs", "flux", None),
        P("obs", "flux"),
        P("obs", None),
    )
    return jax.shard_map(
        shards, mesh=mesh, in_specs=placed, out_specs=P("flux", None, None), check_vma=False
    )
```

```python
import functools
import math

import jax
import jax.numpy as jnp
from jax import lax
from jax.experimental import pallas as pl
from jax.experimental.pallas import tpu as pltpu
from jax.sharding import PartitionSpec as P

STEPS = 4
F32 = jnp.float32
HALF = jnp.bfloat16
VMEM_LIMIT = 8 * 2**20
LANES = 128
OBS_PLAN = (4, 57)
TILE_PLAN = (4, 60)
PRIOR_PLAN = (2, 56)


def matmul(a, b):
    return lax.dot_general(a, b, (((1,), (0,)), ((), ())), preferred_element_type=F32)


def chunk_of(count, most):
    return max(c for c in range(1, most + 1) if count % c == 0)


def exchange(value, partner):
    n_obs, n_flux = lax.axis_size("obs"), lax.axis_size("flux")
    route = []
    for i in range(n_obs):
        for j in range(n_flux):
            to = partner(i, j)
            if to is not None:
                route.append((i * n_flux + j, to[0] * n_flux + to[1]))
    return lax.ppermute(value, ("obs", "flux"), route)


def plan_sizes(plan, blocks, dst_rows):
    group, per_round = plan
    groups = blocks // group + dst_rows
    groups += -groups % per_round
    slots = groups * group
    return slots + -slots % LANES, groups + 1 + -(groups + 1) % LANES


def columns(row):
    parts = [
        jnp.broadcast_to(row[:, k : k + LANES], (LANES, LANES)).T for k in range(0, row.shape[1], LANES)
    ]
    return jnp.concatenate(parts, axis=0)


def plan_groups(plan, src, dst, first, rows, out):
    group, per_round = plan
    blocks = dst.shape[1]
    slots, groups = plan_sizes(plan, blocks, rows)
    i32 = jnp.int32
    lane = lax.broadcasted_iota(i32, (blocks, LANES), 1)
    at = lax.broadcasted_iota(i32, (blocks, LANES), 0)
    src_at, dst_at = columns(src), columns(dst)
    rank = jnp.zeros((blocks, LANES), F32)
    for k in range(0, blocks, LANES):
        same = (dst_at == dst[:, k : k + LANES]) & (lane + k < at)
        rank += same.astype(F32)
    rank = jnp.sum(rank, axis=1, keepdims=True)
    fills = jnp.sum((dst_at == lane).astype(F32), axis=0, keepdims=True)
    sizes = jnp.where(lane[:1] < rows, jnp.floor((fills + (group - 1)) * (1.0 / group)), 0.0)
    begin = jnp.sum(jnp.where(lane < dst_at, sizes, 0.0), axis=1, keepdims=True)
    place = (begin * group + rank).astype(i32)
    place = jnp.where(dst_at < rows, place, slots)
    for k in range(0, slots, LANES):
        hit = place == lane + k
        of = jnp.sum(jnp.where(hit, (src_at - rows).astype(F32), 0.0), axis=0, keepdims=True)
        out[:, k : k + LANES] = of.astype(i32) + rows
        of = jnp.sum(jnp.where(hit, (at - first).astype(F32), 0.0), axis=0, keepdims=True)
        out[:, slots + k : slots + k + LANES] = of.astype(i32)
    full = jnp.sum(sizes, axis=1, keepdims=True)
    rounds = jnp.sum((lane[:1].astype(F32) * per_round < full).astype(F32), axis=1, keepdims=True)
    for k in range(0, groups, LANES):
        lead = place == (lane + k) * group
        of = jnp.sum(jnp.where(lead, (dst_at - rows).astype(F32), 0.0), axis=0, keepdims=True)
        of = jnp.where(lane[:1] + k == groups - 1, rounds, of + rows)
        out[:, 2 * slots + k : 2 * slots + k + LANES] = of.astype(i32)


def setup_kernel(
    rows, chunk, where, obs, flux, nbr, prior, jac,
    prior_plain, prior_turned, jac_plain, jac_turned, obs_plan, tile_plan, prior_plan, nbr_list,
    obs_in, flux_in, nbr_in, obs_out, tile_out, prior_out, nbr_out, small_sems, sems
):
    side, corner, count, first_tile = where[0], where[1], where[2], where[3]
    owned = prior_plain.shape[0]
    begin = side * owned
    rounds = (owned // chunk, jac_plain.shape[0] // chunk)

    def copy(c, first, source, plain, offset):
        to = pl.ds(c * chunk, chunk)
        return pltpu.make_async_copy(source.at[pl.ds(first + c * chunk, chunk)], plain.at[to], sems.at[offset + c])

    def start(first, source, plain, offset):
        def one(c, _):
            copy(c, first, source, plain, offset).start()
            return 0

        return one

    def turn(first, source, plain, turned, offset):
        def one(c, _):
            copy(c, first, source, plain, offset).wait()
            for u in range(chunk):
                turned[c * chunk + u] = plain[c * chunk + u].T
            return 0

        return one

    small = ((obs, obs_in), (flux, flux_in), (nbr, nbr_in))
    small = [pltpu.make_async_copy(src, dst, small_sems.at[k]) for k, (src, dst) in enumerate(small)]
    for one in small:
        one.start()
    lax.fori_loop(0, rounds[0], start(begin, prior, prior_plain, 0), 0)
    lax.fori_loop(0, rounds[1], start(0, jac, jac_plain, rounds[0]), 0)
    for one in small:
        one.wait()

    obs_rows, tile_rows, fan = rows
    half = tile_rows // 2
    reach = tile_rows // 4
    quarter = obs_rows // 4
    most = max(obs_rows, tile_rows)
    i32 = jnp.int32
    at = lax.broadcasted_iota(i32, obs_in.shape, 1)
    live = at < count
    block = sum((obs_in[...] >= k * quarter).astype(i32) for k in range(1, 4))
    obs_at = (block ^ corner) * quarter + obs_in[...] - block * quarter
    block = (flux_in[...] >= half).astype(i32)
    tile_at = (block ^ side) * half + flux_in[...] - block * half
    plan_groups(OBS_PLAN, tile_at, jnp.where(live, obs_at, most), 0, most, obs_out)
    plan_groups(TILE_PLAN, obs_at, jnp.where(live, tile_at, most), 0, most, tile_out)
    at = lax.broadcasted_iota(i32, nbr_in.shape, 1)
    tile = sum((at >= k * fan).astype(i32) for k in range(1, tile_rows)) - side * half
    owns = (tile >= 0) & (tile < half)
    ext = nbr_in[...] - first_tile + reach
    plan_groups(PRIOR_PLAN, jnp.where(owns, tile, 0), jnp.where(owns, ext, most), begin, most, prior_out)
    nbr_out[:, : ext.shape[1]] = ext
    nbr_out[:, ext.shape[1] :] = jnp.zeros((1, LANES), i32) + side
    lists = ((obs_out, obs_plan), (tile_out, tile_plan), (prior_out, prior_plan), (nbr_out, nbr_list))
    lists = [pltpu.make_async_copy(src, dst, small_sems.at[3 + k]) for k, (src, dst) in enumerate(lists)]
    for one in lists:
        one.start()

    lax.fori_loop(0, rounds[0], turn(begin, prior, prior_plain, prior_turned, 0), 0)
    lax.fori_loop(0, rounds[1], turn(0, jac, jac_plain, jac_turned, rounds[0]), 0)
    for one in lists:
        one.wait()


def setup(where, obs, flux, nbr, prior, jac, rows):
    most = max(rows[:2])
    owned = rows[1] // 2 * rows[2]
    chunk = chunk_of(math.gcd(owned, jac.shape[0]), 24)
    smem = pl.BlockSpec(memory_space=pltpu.SMEM)
    vmem = pl.BlockSpec(memory_space=pltpu.VMEM)
    hbm = pl.BlockSpec(memory_space=pl.ANY)
    own = pltpu.VMEM((owned,) + prior.shape[1:], HALF)
    all_blocks = pltpu.VMEM(jac.shape, HALF)
    i32 = jnp.int32
    lengths = []
    for plan, width in ((OBS_PLAN, obs), (TILE_PLAN, obs), (PRIOR_PLAN, nbr)):
        slots, groups = plan_sizes(plan, width.shape[1], most)
        lengths.append(2 * slots + groups)
    lengths.append(nbr.shape[1] + LANES)
    return pl.pallas_call(
        functools.partial(setup_kernel, rows, chunk),
        in_specs=[smem] + [hbm] * 5,
        out_specs=[vmem] * 4 + [smem] * 4,
        out_shape=[own, own, all_blocks, all_blocks] + [pltpu.SMEM((1, n), i32) for n in lengths],
        scratch_shapes=[pltpu.VMEM(v.shape, i32) for v in (obs, flux, nbr)]
        + [pltpu.VMEM((1, n), i32) for n in lengths]
        + [
            pltpu.SemaphoreType.DMA((7,)),
            pltpu.SemaphoreType.DMA(((owned + jac.shape[0]) // chunk,)),
        ],
        compiler_params=pltpu.CompilerParams(vmem_limit_bytes=VMEM_LIMIT),
        name="setup",
    )(where, *(pltpu.with_memory_space_constraint(v, pltpu.HBM) for v in (obs, flux, nbr, prior, jac)))


def grouped_products(plan, sizes, lists, x, blocks, total):
    group, per_round = plan
    slots, groups = sizes
    total[...] = jnp.zeros_like(total)

    def one(c, _):
        products = []
        for u in range(per_round):
            first = (c * per_round + u) * group
            rows = [x[lists[0, first + g]] for g in range(group)]
            tiles = [blocks[lists[0, slots + first + g]] for g in range(group)]
            products.append(matmul(jnp.concatenate(rows, axis=1), jnp.concatenate(tiles, axis=0)))
        for u in range(per_round):
            total[lists[0, 2 * slots + c * per_round + u]] += products[u]
        return 0

    lax.fori_loop(0, lists[0, 2 * slots + groups - 1], one, 0)


def jac_kernel(plan, sizes, n_parts, n_outs, lists, *refs):
    parts = refs[:n_parts]
    jac = refs[n_parts]
    outs = refs[n_parts + 1 : n_parts + 1 + n_outs]
    x, total = refs[n_parts + 1 + n_outs :]
    rows = parts[0].shape[0]
    for k, part in enumerate(parts):
        x[k * rows : (k + 1) * rows] = part[...]
    for r in range(n_parts * rows, x.shape[0]):
        x[r] = jnp.zeros(x.shape[1:], HALF)
    grouped_products(plan, sizes, lists, x, jac, total)
    rows = outs[0].shape[0]
    for k, out in enumerate(outs):
        out[...] = total[k * rows : (k + 1) * rows].astype(out.dtype)


def jac_pass(plan, lists, parts, jac, rows, out_rows, n_outs, name):
    probes, width = parts[0].shape[1:]
    smem = pl.BlockSpec(memory_space=pltpu.SMEM)
    vmem = pl.BlockSpec(memory_space=pltpu.VMEM)
    out = (out_rows // n_outs, probes, width)
    return pl.pallas_call(
        functools.partial(jac_kernel, plan, plan_sizes(plan, jac.shape[0], rows), len(parts), n_outs),
        in_specs=[smem] + [vmem] * len(parts) + [vmem],
        out_specs=[vmem] * n_outs,
        out_shape=[jax.ShapeDtypeStruct(out, F32 if k == 0 else HALF) for k in range(n_outs)],
        scratch_shapes=[
            pltpu.VMEM((rows + 1, probes, width), HALF),
            pltpu.VMEM((rows + 1, probes, width), F32),
        ],
        compiler_params=pltpu.CompilerParams(vmem_limit_bytes=VMEM_LIMIT),
        name=name,
    )(lists, *parts, jac)


def gather_kernel(rows, sizes, nbr, lists, mine, other, prior, ext, to_core, to_far, x, total):
    half = mine.shape[0]
    side = nbr[0, nbr.shape[1] - 1]
    x[:half] = (mine[...].astype(F32) + other[...].astype(F32)).astype(HALF)
    x[rows] = jnp.zeros(x.shape[1:], HALF)
    grouped_products(PRIOR_PLAN, sizes, lists, x, prior, total)
    ext[...] = total[: 2 * half]
    to_core[...] = total[pl.ds(half * (1 - side), half)].astype(HALF)
    to_far[...] = total[pl.ds(half * side, half)].astype(HALF)


def gather_tiles(nbr, lists, mine, other, prior, rows):
    tiles, probes, width = mine.shape
    smem = pl.BlockSpec(memory_space=pltpu.SMEM)
    vmem = pl.BlockSpec(memory_space=pltpu.VMEM)
    return pl.pallas_call(
        functools.partial(gather_kernel, rows, plan_sizes(PRIOR_PLAN, nbr.shape[1] - LANES, rows)),
        in_specs=[smem, smem, vmem, vmem, vmem],
        out_specs=[vmem] * 3,
        out_shape=[
            jax.ShapeDtypeStruct((2 * tiles, probes, width), F32),
            jax.ShapeDtypeStruct((tiles, probes, width), HALF),
            jax.ShapeDtypeStruct((tiles, probes, width), HALF),
        ],
        scratch_shapes=[
            pltpu.VMEM((rows + 1, probes, width), HALF),
            pltpu.VMEM((rows + 1, probes, width), F32),
        ],
        compiler_params=pltpu.CompilerParams(vmem_limit_bytes=VMEM_LIMIT),
        name="prior_adjoint",
    )(nbr, lists, mine, other, prior)


def spread_kernel(first, fan, nbr, *refs):
    prior, out, field = refs[-3:]
    tiles = out.shape[0]
    chunk = chunk_of(tiles, 24)
    side = nbr[0, nbr.shape[1] - 1]
    if first:
        probes, beyond = refs[:2]
        reach = beyond.shape[0]
        inner = 2 * tiles - reach
        field[pl.ds(reach * (1 - side), inner)] = probes[pl.ds(reach * side, inner)]
        field[pl.ds(inner * side, reach)] = beyond[...]
    else:
        ext, from_core, from_far = refs[:3]
        for begin, update in ((tiles * (1 - side), from_core), (tiles * side, from_far)):
            at = pl.ds(begin, tiles)
            field[at] = (ext[at] + update[...].astype(F32)).astype(HALF)

    def one(c, _):
        for u in range(chunk):
            t = c * chunk + u
            row = [field[nbr[0, (side * tiles + t) * fan + k]] for k in range(fan)]
            tile = prior[pl.ds(t * fan, fan)]
            tile = tile.reshape(fan * tile.shape[1], tile.shape[2])
            out[t] = matmul(jnp.concatenate(row, axis=1), tile).astype(HALF)
        return 0

    lax.fori_loop(0, tiles // chunk, one, 0)


def spread_tiles(nbr, fields, prior):
    ext_tiles, probes, width = fields[0].shape
    tiles = ext_tiles // 2
    smem = pl.BlockSpec(memory_space=pltpu.SMEM)
    vmem = pl.BlockSpec(memory_space=pltpu.VMEM)
    return pl.pallas_call(
        functools.partial(spread_kernel, len(fields) == 2, prior.shape[0] // tiles),
        in_specs=[smem] + [vmem] * len(fields) + [vmem],
        out_specs=vmem,
        out_shape=jax.ShapeDtypeStruct((tiles, probes, width), HALF),
        scratch_shapes=[pltpu.VMEM(fields[0].shape, HALF)],
        compiler_params=pltpu.CompilerParams(vmem_limit_bytes=VMEM_LIMIT),
        name="prior_spread",
    )(nbr, *fields, prior)


def shards(probes, prior_tiles, neighbours, jac, jac_obs, jac_flux, counts, rinv):
    n_obs, n_flux = lax.axis_size("obs"), lax.axis_size("flux")
    tile_count = probes.shape[0]
    half = tile_count // 2
    reach = tile_count // 4
    obs_rows = rinv.shape[0]
    quarter = obs_rows // 4
    blocks = jac[0, 0]
    flux_at = lax.axis_index("flux")
    side = lax.rem(lax.axis_index("obs"), 2)
    corner = lax.rem(flux_at, 4)
    fan = neighbours.shape[1]
    prior = prior_tiles.reshape((tile_count * fan,) + prior_tiles.shape[2:])
    own_rinv = lax.dynamic_slice_in_dim(rinv, corner * quarter, quarter, 0)[:, None, :]
    rows = max(obs_rows, tile_count)
    sizes = (obs_rows, tile_count, fan)

    def swap_core(value):
        return exchange(value, lambda i, j: (i ^ 1, j))

    def swap_far(value):
        def partner(i, j):
            to = j - 1 if i % 2 == 0 else j + 1
            return (i ^ 1, to) if 0 <= to < n_flux else None

        return exchange(value, partner)

    def swap_flux(value, bits):
        return exchange(value, lambda i, j: (i, j ^ bits))

    edge = jnp.where(side == 0, probes[:reach], probes[tile_count - reach :])
    beyond = swap_far(edge)
    where = jnp.stack([side, corner, counts[0, 0], flux_at * tile_count + side * half])
    nbr = neighbours.reshape(1, tile_count * fan)

    where, own_rinv, nbr, prior, blocks = lax.optimization_barrier((where, own_rinv, nbr, prior, blocks))
    prior_plain, prior_turned, jac_plain, jac_turned, obs_lists, tile_lists, prior_lists, nbr = setup(
        where, jac_obs[0], jac_flux[0], nbr, prior, blocks, sizes
    )
    fields = (probes, beyond)
    for step in range(STEPS):
        spread = spread_tiles(nbr, fields, prior_plain)
        parts = (spread, swap_core(spread))
        pieces = jac_pass(OBS_PLAN, obs_lists, parts, jac_plain, rows, obs_rows, 4, "jac_forward")
        total = pieces[0]
        for bits in range(1, 4):
            total = total + swap_flux(pieces[bits], bits).astype(F32)
        bits = 4
        while bits < n_flux:
            sent = total.astype(HALF)
            total = sent.astype(F32) + swap_flux(sent, bits).astype(F32)
            bits *= 2
        weighted = (total * own_rinv).astype(HALF)
        parts = (weighted,) + tuple(swap_flux(weighted, bits) for bits in range(1, 4))
        mine, theirs = jac_pass(TILE_PLAN, tile_lists, parts, jac_turned, rows, tile_count, 2, "jac_adjoint")
        mine = (mine + swap_core(theirs).astype(F32)).astype(HALF)
        bits = 2
        while bits < n_obs:
            other = exchange(mine, lambda i, j, bits=bits: (i ^ bits, j))
            bits *= 2
            if bits < n_obs:
                mine = (mine.astype(F32) + other.astype(F32)).astype(HALF)
        ext, to_core, to_far = gather_tiles(nbr, prior_lists, mine, other, prior_turned, rows)
        if step < STEPS - 1:
            fields = (ext, swap_core(to_core), swap_far(to_far))
    lower = side == 0
    from_core = swap_core(jnp.where(lower, to_core[half - reach :], to_core[:reach])).astype(F32)
    from_far = swap_far(jnp.where(lower, to_far[:reach], to_far[half - reach :])).astype(F32)
    low = jnp.where(lower, from_far, from_core)
    high = jnp.where(lower, from_core, from_far)
    own = (ext[reach : reach + half] + jnp.concatenate([low, high], axis=0)).astype(HALF)
    other = swap_core(own)
    first = jnp.where(side == 0, own, other)
    second = jnp.where(side == 0, other, own)
    return jnp.concatenate([first, second], axis=0)


def solution(mesh):
    placed = (
        P("flux", None, None),
        P("flux", None, None, None),
        P("flux", None),
        P("obs", "flux", None, None, None),
        P("obs", "flux", None),
        P("obs", "flux", None),
        P("obs", "flux"),
        P("obs", None),
    )
    return jax.shard_map(
        shards, mesh=mesh, in_specs=placed, out_specs=P("flux", None, None), check_vma=False
    )
```

```python
import functools
import math

import jax
import jax.numpy as jnp
from jax import lax
from jax.experimental import pallas as pl
from jax.experimental.pallas import tpu as pltpu
from jax.sharding import PartitionSpec as P

STEPS = 4
F32 = jnp.float32
HALF = jnp.bfloat16
VMEM_LIMIT = 8 * 2**20
LANES = 128
OBS_PLAN = (4, 57)
TILE_PLAN = (4, 60)
PRIOR_PLAN = (2, 56)


def matmul(a, b):
    return lax.dot_general(a, b, (((1,), (0,)), ((), ())), preferred_element_type=F32)


def chunk_of(count, most):
    return max(c for c in range(1, most + 1) if count % c == 0)


def exchange(value, partner):
    n_obs, n_flux = lax.axis_size("obs"), lax.axis_size("flux")
    route = []
    for i in range(n_obs):
        for j in range(n_flux):
            to = partner(i, j)
            if to is not None:
                route.append((i * n_flux + j, to[0] * n_flux + to[1]))
    return lax.ppermute(value, ("obs", "flux"), route)


def plan_sizes(plan, blocks, dst_rows):
    group, per_round = plan
    groups = blocks // group + dst_rows
    groups += -groups % per_round
    slots = groups * group
    return slots + -slots % LANES, groups + 1 + -(groups + 1) % LANES


def columns(row):
    parts = [
        jnp.broadcast_to(row[:, k : k + LANES], (LANES, LANES)).T for k in range(0, row.shape[1], LANES)
    ]
    return jnp.concatenate(parts, axis=0)


def plan_groups(plan, src, dst, first, rows, out):
    group, per_round = plan
    blocks = dst.shape[1]
    slots, groups = plan_sizes(plan, blocks, rows)
    i32 = jnp.int32
    lane = lax.broadcasted_iota(i32, (blocks, LANES), 1)
    at = lax.broadcasted_iota(i32, (blocks, LANES), 0)
    src_at, dst_at = columns(src), columns(dst)
    rank = jnp.zeros((blocks, LANES), F32)
    for k in range(0, blocks, LANES):
        same = (dst_at == dst[:, k : k + LANES]) & (lane + k < at)
        rank += same.astype(F32)
    rank = jnp.sum(rank, axis=1, keepdims=True)
    fills = jnp.sum((dst_at == lane).astype(F32), axis=0, keepdims=True)
    sizes = jnp.where(lane[:1] < rows, jnp.floor((fills + (group - 1)) * (1.0 / group)), 0.0)
    begin = jnp.sum(jnp.where(lane < dst_at, sizes, 0.0), axis=1, keepdims=True)
    place = (begin * group + rank).astype(i32)
    place = jnp.where(dst_at < rows, place, slots)
    for k in range(0, slots, LANES):
        hit = place == lane + k
        of = jnp.sum(jnp.where(hit, (src_at - rows).astype(F32), 0.0), axis=0, keepdims=True)
        out[:, k : k + LANES] = of.astype(i32) + rows
        of = jnp.sum(jnp.where(hit, (at - first).astype(F32), 0.0), axis=0, keepdims=True)
        out[:, slots + k : slots + k + LANES] = of.astype(i32)
    full = jnp.sum(sizes, axis=1, keepdims=True)
    rounds = jnp.sum((lane[:1].astype(F32) * per_round < full).astype(F32), axis=1, keepdims=True)
    for k in range(0, groups, LANES):
        lead = place == (lane + k) * group
        of = jnp.sum(jnp.where(lead, (dst_at - rows).astype(F32), 0.0), axis=0, keepdims=True)
        of = jnp.where(lane[:1] + k == groups - 1, rounds, of + rows)
        out[:, 2 * slots + k : 2 * slots + k + LANES] = of.astype(i32)


def setup_kernel(
    rows, chunk, where, obs, flux, nbr, prior, jac,
    prior_plain, jac_plain, obs_plan, tile_plan, prior_plan, nbr_list,
    obs_in, flux_in, nbr_in, obs_out, tile_out, prior_out, nbr_out, small_sems, sems
):
    side, corner, count, first_tile = where[0], where[1], where[2], where[3]
    owned = prior_plain.shape[0]
    begin = side * owned
    rounds = (owned // chunk, jac_plain.shape[0] // chunk)

    def copy(c, first, source, plain, offset):
        to = pl.ds(c * chunk, chunk)
        return pltpu.make_async_copy(source.at[pl.ds(first + c * chunk, chunk)], plain.at[to], sems.at[offset + c])

    def start(first, source, plain, offset):
        def one(c, _):
            copy(c, first, source, plain, offset).start()
            return 0

        return one

    def wait(first, source, plain, offset):
        def one(c, _):
            copy(c, first, source, plain, offset).wait()
            return 0

        return one

    small = ((obs, obs_in), (flux, flux_in), (nbr, nbr_in))
    small = [pltpu.make_async_copy(src, dst, small_sems.at[k]) for k, (src, dst) in enumerate(small)]
    for one in small:
        one.start()
    lax.fori_loop(0, rounds[0], start(begin, prior, prior_plain, 0), 0)
    lax.fori_loop(0, rounds[1], start(0, jac, jac_plain, rounds[0]), 0)
    for one in small:
        one.wait()

    obs_rows, tile_rows, fan = rows
    half = tile_rows // 2
    reach = tile_rows // 4
    quarter = obs_rows // 4
    most = max(obs_rows, tile_rows)
    i32 = jnp.int32
    at = lax.broadcasted_iota(i32, obs_in.shape, 1)
    live = at < count
    block = sum((obs_in[...] >= k * quarter).astype(i32) for k in range(1, 4))
    obs_at = (block ^ corner) * quarter + obs_in[...] - block * quarter
    block = (flux_in[...] >= half).astype(i32)
    tile_at = (block ^ side) * half + flux_in[...] - block * half
    plan_groups(OBS_PLAN, tile_at, jnp.where(live, obs_at, most), 0, most, obs_out)
    plan_groups(TILE_PLAN, obs_at, jnp.where(live, tile_at, most), 0, most, tile_out)
    at = lax.broadcasted_iota(i32, nbr_in.shape, 1)
    tile = sum((at >= k * fan).astype(i32) for k in range(1, tile_rows)) - side * half
    owns = (tile >= 0) & (tile < half)
    ext = nbr_in[...] - first_tile + reach
    plan_groups(PRIOR_PLAN, jnp.where(owns, tile, 0), jnp.where(owns, ext, most), begin, most, prior_out)
    nbr_out[:, : ext.shape[1]] = ext
    nbr_out[:, ext.shape[1] :] = jnp.zeros((1, LANES), i32) + side
    lists = ((obs_out, obs_plan), (tile_out, tile_plan), (prior_out, prior_plan), (nbr_out, nbr_list))
    lists = [pltpu.make_async_copy(src, dst, small_sems.at[3 + k]) for k, (src, dst) in enumerate(lists)]
    for one in lists:
        one.start()

    lax.fori_loop(0, rounds[0], wait(begin, prior, prior_plain, 0), 0)
    lax.fori_loop(0, rounds[1], wait(0, jac, jac_plain, rounds[0]), 0)
    for one in lists:
        one.wait()


def turn_kernel(chunk, plain, turned):
    def one(c, _):
        for u in range(chunk):
            turned[c * chunk + u] = plain[c * chunk + u].T
        return 0

    lax.fori_loop(0, plain.shape[0] // chunk, one, 0)


def turn_blocks(plain, name):
    vmem = pl.BlockSpec(memory_space=pltpu.VMEM)
    return pl.pallas_call(
        functools.partial(turn_kernel, chunk_of(plain.shape[0], 48)),
        in_specs=[vmem],
        out_specs=vmem,
        out_shape=pltpu.VMEM(plain.shape, HALF),
        compiler_params=pltpu.CompilerParams(vmem_limit_bytes=VMEM_LIMIT),
        cost_estimate=pl.CostEstimate(flops=0, bytes_accessed=2 * plain.size, transcendentals=0),
        name=name,
    )(plain)


def setup(where, obs, flux, nbr, prior, jac, rows):
    most = max(rows[:2])
    owned = rows[1] // 2 * rows[2]
    chunk = chunk_of(math.gcd(owned, jac.shape[0]), 24)
    smem = pl.BlockSpec(memory_space=pltpu.SMEM)
    vmem = pl.BlockSpec(memory_space=pltpu.VMEM)
    hbm = pl.BlockSpec(memory_space=pl.ANY)
    own = pltpu.VMEM((owned,) + prior.shape[1:], HALF)
    all_blocks = pltpu.VMEM(jac.shape, HALF)
    i32 = jnp.int32
    lengths = []
    for plan, width in ((OBS_PLAN, obs), (TILE_PLAN, obs), (PRIOR_PLAN, nbr)):
        slots, groups = plan_sizes(plan, width.shape[1], most)
        lengths.append(2 * slots + groups)
    lengths.append(nbr.shape[1] + LANES)
    return pl.pallas_call(
        functools.partial(setup_kernel, rows, chunk),
        in_specs=[smem] + [hbm] * 5,
        out_specs=[vmem] * 2 + [smem] * 4,
        out_shape=[own, all_blocks] + [pltpu.SMEM((1, n), i32) for n in lengths],
        scratch_shapes=[pltpu.VMEM(v.shape, i32) for v in (obs, flux, nbr)]
        + [pltpu.VMEM((1, n), i32) for n in lengths]
        + [
            pltpu.SemaphoreType.DMA((7,)),
            pltpu.SemaphoreType.DMA(((owned + jac.shape[0]) // chunk,)),
        ],
        compiler_params=pltpu.CompilerParams(vmem_limit_bytes=VMEM_LIMIT),
        name="setup",
    )(where, *(pltpu.with_memory_space_constraint(v, pltpu.HBM) for v in (obs, flux, nbr, prior, jac)))


def grouped_products(plan, sizes, lists, x, blocks, total):
    group, per_round = plan
    slots, groups = sizes
    total[...] = jnp.zeros_like(total)

    def one(c, _):
        products = []
        for u in range(per_round):
            first = (c * per_round + u) * group
            rows = [x[lists[0, first + g]] for g in range(group)]
            tiles = [blocks[lists[0, slots + first + g]] for g in range(group)]
            products.append(matmul(jnp.concatenate(rows, axis=1), jnp.concatenate(tiles, axis=0)))
        for u in range(per_round):
            total[lists[0, 2 * slots + c * per_round + u]] += products[u]
        return 0

    lax.fori_loop(0, lists[0, 2 * slots + groups - 1], one, 0)


def jac_kernel(plan, sizes, n_parts, n_outs, lists, *refs):
    parts = refs[:n_parts]
    jac = refs[n_parts]
    outs = refs[n_parts + 1 : n_parts + 1 + n_outs]
    x, total = refs[n_parts + 1 + n_outs :]
    rows = parts[0].shape[0]
    for k, part in enumerate(parts):
        x[k * rows : (k + 1) * rows] = part[...]
    for r in range(n_parts * rows, x.shape[0]):
        x[r] = jnp.zeros(x.shape[1:], HALF)
    grouped_products(plan, sizes, lists, x, jac, total)
    rows = outs[0].shape[0]
    for k, out in enumerate(outs):
        out[...] = total[k * rows : (k + 1) * rows].astype(out.dtype)


def jac_pass(plan, lists, parts, jac, rows, out_rows, n_outs, name):
    probes, width = parts[0].shape[1:]
    smem = pl.BlockSpec(memory_space=pltpu.SMEM)
    vmem = pl.BlockSpec(memory_space=pltpu.VMEM)
    out = (out_rows // n_outs, probes, width)
    return pl.pallas_call(
        functools.partial(jac_kernel, plan, plan_sizes(plan, jac.shape[0], rows), len(parts), n_outs),
        in_specs=[smem] + [vmem] * len(parts) + [vmem],
        out_specs=[vmem] * n_outs,
        out_shape=[jax.ShapeDtypeStruct(out, F32 if k == 0 else HALF) for k in range(n_outs)],
        scratch_shapes=[
            pltpu.VMEM((rows + 1, probes, width), HALF),
            pltpu.VMEM((rows + 1, probes, width), F32),
        ],
        compiler_params=pltpu.CompilerParams(vmem_limit_bytes=VMEM_LIMIT),
        name=name,
    )(lists, *parts, jac)


def gather_kernel(rows, sizes, nbr, lists, mine, other, prior, ext, to_core, to_far, x, total):
    half = mine.shape[0]
    side = nbr[0, nbr.shape[1] - 1]
    x[:half] = (mine[...].astype(F32) + other[...].astype(F32)).astype(HALF)
    x[rows] = jnp.zeros(x.shape[1:], HALF)
    grouped_products(PRIOR_PLAN, sizes, lists, x, prior, total)
    ext[...] = total[: 2 * half]
    to_core[...] = total[pl.ds(half * (1 - side), half)].astype(HALF)
    to_far[...] = total[pl.ds(half * side, half)].astype(HALF)


def gather_tiles(nbr, lists, mine, other, prior, rows):
    tiles, probes, width = mine.shape
    smem = pl.BlockSpec(memory_space=pltpu.SMEM)
    vmem = pl.BlockSpec(memory_space=pltpu.VMEM)
    return pl.pallas_call(
        functools.partial(gather_kernel, rows, plan_sizes(PRIOR_PLAN, nbr.shape[1] - LANES, rows)),
        in_specs=[smem, smem, vmem, vmem, vmem],
        out_specs=[vmem] * 3,
        out_shape=[
            jax.ShapeDtypeStruct((2 * tiles, probes, width), F32),
            jax.ShapeDtypeStruct((tiles, probes, width), HALF),
            jax.ShapeDtypeStruct((tiles, probes, width), HALF),
        ],
        scratch_shapes=[
            pltpu.VMEM((rows + 1, probes, width), HALF),
            pltpu.VMEM((rows + 1, probes, width), F32),
        ],
        compiler_params=pltpu.CompilerParams(vmem_limit_bytes=VMEM_LIMIT),
        name="prior_adjoint",
    )(nbr, lists, mine, other, prior)


def spread_kernel(first, fan, nbr, *refs):
    prior, out, field = refs[-3:]
    tiles = out.shape[0]
    chunk = chunk_of(tiles, 24)
    side = nbr[0, nbr.shape[1] - 1]
    if first:
        probes, beyond = refs[:2]
        reach = beyond.shape[0]
        inner = 2 * tiles - reach
        field[pl.ds(reach * (1 - side), inner)] = probes[pl.ds(reach * side, inner)]
        field[pl.ds(inner * side, reach)] = beyond[...]
    else:
        ext, from_core, from_far = refs[:3]
        for begin, update in ((tiles * (1 - side), from_core), (tiles * side, from_far)):
            at = pl.ds(begin, tiles)
            field[at] = (ext[at] + update[...].astype(F32)).astype(HALF)

    def one(c, _):
        for u in range(chunk):
            t = c * chunk + u
            row = [field[nbr[0, (side * tiles + t) * fan + k]] for k in range(fan)]
            tile = prior[pl.ds(t * fan, fan)]
            tile = tile.reshape(fan * tile.shape[1], tile.shape[2])
            out[t] = matmul(jnp.concatenate(row, axis=1), tile).astype(HALF)
        return 0

    lax.fori_loop(0, tiles // chunk, one, 0)


def spread_tiles(nbr, fields, prior):
    ext_tiles, probes, width = fields[0].shape
    tiles = ext_tiles // 2
    smem = pl.BlockSpec(memory_space=pltpu.SMEM)
    vmem = pl.BlockSpec(memory_space=pltpu.VMEM)
    return pl.pallas_call(
        functools.partial(spread_kernel, len(fields) == 2, prior.shape[0] // tiles),
        in_specs=[smem] + [vmem] * len(fields) + [vmem],
        out_specs=vmem,
        out_shape=jax.ShapeDtypeStruct((tiles, probes, width), HALF),
        scratch_shapes=[pltpu.VMEM(fields[0].shape, HALF)],
        compiler_params=pltpu.CompilerParams(vmem_limit_bytes=VMEM_LIMIT),
        name="prior_spread",
    )(nbr, *fields, prior)


def shards(probes, prior_tiles, neighbours, jac, jac_obs, jac_flux, counts, rinv):
    n_obs, n_flux = lax.axis_size("obs"), lax.axis_size("flux")
    tile_count = probes.shape[0]
    half = tile_count // 2
    reach = tile_count // 4
    obs_rows = rinv.shape[0]
    quarter = obs_rows // 4
    blocks = jac[0, 0]
    flux_at = lax.axis_index("flux")
    side = lax.rem(lax.axis_index("obs"), 2)
    corner = lax.rem(flux_at, 4)
    fan = neighbours.shape[1]
    prior = prior_tiles.reshape((tile_count * fan,) + prior_tiles.shape[2:])
    own_rinv = lax.dynamic_slice_in_dim(rinv, corner * quarter, quarter, 0)[:, None, :]
    rows = max(obs_rows, tile_count)
    sizes = (obs_rows, tile_count, fan)

    def swap_core(value):
        return exchange(value, lambda i, j: (i ^ 1, j))

    def swap_far(value):
        def partner(i, j):
            to = j - 1 if i % 2 == 0 else j + 1
            return (i ^ 1, to) if 0 <= to < n_flux else None

        return exchange(value, partner)

    def swap_flux(value, bits):
        return exchange(value, lambda i, j: (i, j ^ bits))

    edge = jnp.where(side == 0, probes[:reach], probes[tile_count - reach :])
    beyond = swap_far(edge)
    where = jnp.stack([side, corner, counts[0, 0], flux_at * tile_count + side * half])
    nbr = neighbours.reshape(1, tile_count * fan)

    where, own_rinv, nbr, prior, blocks = lax.optimization_barrier((where, own_rinv, nbr, prior, blocks))
    prior_plain, jac_plain, obs_lists, tile_lists, prior_lists, nbr = setup(
        where, jac_obs[0], jac_flux[0], nbr, prior, blocks, sizes
    )
    fields = (probes, beyond)
    for step in range(STEPS):
        spread = spread_tiles(nbr, fields, prior_plain)
        parts = (spread, swap_core(spread))
        pieces = jac_pass(OBS_PLAN, obs_lists, parts, jac_plain, rows, obs_rows, 4, "jac_forward")
        if step == 0:
            pieces, jac_plain = lax.optimization_barrier((pieces, jac_plain))
            jac_turned = turn_blocks(jac_plain, "jac_turn")
        total = pieces[0]
        for bits in range(1, 4):
            total = total + swap_flux(pieces[bits], bits).astype(F32)
        bits = 4
        while bits < n_flux:
            sent = total.astype(HALF)
            total = sent.astype(F32) + swap_flux(sent, bits).astype(F32)
            bits *= 2
        weighted = (total * own_rinv).astype(HALF)
        parts = (weighted,) + tuple(swap_flux(weighted, bits) for bits in range(1, 4))
        mine, theirs = jac_pass(TILE_PLAN, tile_lists, parts, jac_turned, rows, tile_count, 2, "jac_adjoint")
        mine = (mine + swap_core(theirs).astype(F32)).astype(HALF)
        if step == 0:
            mine, prior_plain = lax.optimization_barrier((mine, prior_plain))
            prior_turned = turn_blocks(prior_plain, "prior_turn")
        bits = 2
        while bits < n_obs:
            other = exchange(mine, lambda i, j, bits=bits: (i ^ bits, j))
            bits *= 2
            if bits < n_obs:
                mine = (mine.astype(F32) + other.astype(F32)).astype(HALF)
        ext, to_core, to_far = gather_tiles(nbr, prior_lists, mine, other, prior_turned, rows)
        if step < STEPS - 1:
            fields = (ext, swap_core(to_core), swap_far(to_far))
    lower = side == 0
    from_core = swap_core(jnp.where(lower, to_core[half - reach :], to_core[:reach])).astype(F32)
    from_far = swap_far(jnp.where(lower, to_far[:reach], to_far[half - reach :])).astype(F32)
    low = jnp.where(lower, from_far, from_core)
    high = jnp.where(lower, from_core, from_far)
    own = (ext[reach : reach + half] + jnp.concatenate([low, high], axis=0)).astype(HALF)
    other = swap_core(own)
    first = jnp.where(side == 0, own, other)
    second = jnp.where(side == 0, other, own)
    return jnp.concatenate([first, second], axis=0)


def solution(mesh):
    placed = (
        P("flux", None, None),
        P("flux", None, None, None),
        P("flux", None),
        P("obs", "flux", None, None, None),
        P("obs", "flux", None),
        P("obs", "flux", None),
        P("obs", "flux"),
        P("obs", None),
    )
    return jax.shard_map(
        shards, mesh=mesh, in_specs=placed, out_specs=P("flux", None, None), check_vma=False
    )
```

```python
import functools
import math

import jax
import jax.numpy as jnp
from jax import lax
from jax.experimental import pallas as pl
from jax.experimental.pallas import tpu as pltpu
from jax.sharding import PartitionSpec as P

STEPS = 4
F32 = jnp.float32
HALF = jnp.bfloat16
VMEM_LIMIT = 8 * 2**20
LANES = 128
FORWARD_PLAN = (2, 56)
NEAR_PLAN = (2, 32)
REST_PLAN = (2, 42)
PRIOR_PLAN = (2, 56)


def matmul(a, b):
    return lax.dot_general(a, b, (((1,), (0,)), ((), ())), preferred_element_type=F32)


def chunk_of(count, most):
    return max(c for c in range(1, most + 1) if count % c == 0)


def exchange(value, partner):
    n_obs, n_flux = lax.axis_size("obs"), lax.axis_size("flux")
    route = []
    for i in range(n_obs):
        for j in range(n_flux):
            to = partner(i, j)
            if to is not None:
                route.append((i * n_flux + j, to[0] * n_flux + to[1]))
    return lax.ppermute(value, ("obs", "flux"), route)


def plan_sizes(plan, blocks, dst_rows):
    group, per_round = plan
    groups = blocks // group + dst_rows
    groups += -groups % per_round
    slots = groups * group
    return slots + -slots % LANES, groups + 1 + -(groups + 1) % LANES


def columns(row):
    parts = [
        jnp.broadcast_to(row[:, k : k + LANES], (LANES, LANES)).T for k in range(0, row.shape[1], LANES)
    ]
    return jnp.concatenate(parts, axis=0)


def plan_groups(plan, src, dst, first, rows, out):
    group, per_round = plan
    blocks = dst.shape[1]
    slots, groups = plan_sizes(plan, blocks, rows)
    i32 = jnp.int32
    lane = lax.broadcasted_iota(i32, (blocks, LANES), 1)
    at = lax.broadcasted_iota(i32, (blocks, LANES), 0)
    src_at, dst_at = columns(src), columns(dst)
    rank = jnp.zeros((blocks, LANES), F32)
    for k in range(0, blocks, LANES):
        same = (dst_at == dst[:, k : k + LANES]) & (lane + k < at)
        rank += same.astype(F32)
    rank = jnp.sum(rank, axis=1, keepdims=True)
    fills = jnp.sum((dst_at == lane).astype(F32), axis=0, keepdims=True)
    sizes = jnp.where(lane[:1] < rows, jnp.floor((fills + (group - 1)) * (1.0 / group)), 0.0)
    begin = jnp.sum(jnp.where(lane < dst_at, sizes, 0.0), axis=1, keepdims=True)
    place = (begin * group + rank).astype(i32)
    place = jnp.where(dst_at < rows, place, slots)
    for k in range(0, slots, LANES):
        hit = place == lane + k
        of = jnp.sum(jnp.where(hit, (src_at - rows).astype(F32), 0.0), axis=0, keepdims=True)
        out[:, k : k + LANES] = of.astype(i32) + rows
        of = jnp.sum(jnp.where(hit, (at - first).astype(F32), 0.0), axis=0, keepdims=True)
        out[:, slots + k : slots + k + LANES] = of.astype(i32)
    full = jnp.sum(sizes, axis=1, keepdims=True)
    rounds = jnp.sum((lane[:1].astype(F32) * per_round < full).astype(F32), axis=1, keepdims=True)
    for k in range(0, groups, LANES):
        lead = place == (lane + k) * group
        of = jnp.sum(jnp.where(lead, (dst_at - rows).astype(F32), 0.0), axis=0, keepdims=True)
        of = jnp.where(lane[:1] + k == groups - 1, rounds, of + rows)
        out[:, 2 * slots + k : 2 * slots + k + LANES] = of.astype(i32)


def setup_kernel(
    rows, chunk, where, obs, flux, nbr, prior, jac,
    prior_plain, jac_plain, *refs
):
    plans, (obs_in, flux_in, nbr_in) = refs[:7], refs[7:10]
    built, (small_sems, sems) = refs[10:17], refs[17:]
    side, corner, count, first_tile = where[0], where[1], where[2], where[3]
    owned = prior_plain.shape[0]
    begin = side * owned
    rounds = (owned // chunk, jac_plain.shape[0] // chunk)

    def copy(c, first, source, plain, offset):
        to = pl.ds(c * chunk, chunk)
        return pltpu.make_async_copy(source.at[pl.ds(first + c * chunk, chunk)], plain.at[to], sems.at[offset + c])

    def start(first, source, plain, offset):
        def one(c, _):
            copy(c, first, source, plain, offset).start()
            return 0

        return one

    def wait(first, source, plain, offset):
        def one(c, _):
            copy(c, first, source, plain, offset).wait()
            return 0

        return one

    small = ((obs, obs_in), (flux, flux_in), (nbr, nbr_in))
    small = [pltpu.make_async_copy(src, dst, small_sems.at[k]) for k, (src, dst) in enumerate(small)]
    for one in small:
        one.start()
    lax.fori_loop(0, rounds[0], start(begin, prior, prior_plain, 0), 0)
    lax.fori_loop(0, rounds[1], start(0, jac, jac_plain, rounds[0]), 0)
    for one in small:
        one.wait()

    obs_rows, tile_rows, fan = rows
    half = tile_rows // 2
    reach = tile_rows // 4
    quarter = obs_rows // 4
    most = max(obs_rows, tile_rows)
    i32 = jnp.int32
    at = lax.broadcasted_iota(i32, obs_in.shape, 1)
    live = at < count
    block = sum((obs_in[...] >= k * quarter).astype(i32) for k in range(1, 4))
    obs_at = (block ^ corner) * quarter + obs_in[...] - block * quarter
    block = (flux_in[...] >= half).astype(i32)
    tile_at = (block ^ side) * half + flux_in[...] - block * half
    own, near = tile_at < half, obs_at < quarter
    for plan, src, dst, use, out in (
        (FORWARD_PLAN, tile_at, obs_at, own, built[0]),
        (FORWARD_PLAN, tile_at - half, obs_at, ~own, built[1]),
        (NEAR_PLAN, obs_at, tile_at, near, built[2]),
        (REST_PLAN, obs_at - quarter, tile_at - half, ~near & ~own, built[3]),
        (REST_PLAN, obs_at - quarter, tile_at, ~near & own, built[4]),
    ):
        use = live & use
        plan_groups(plan, jnp.where(use, src, 0), jnp.where(use, dst, most), 0, most, out)
    at = lax.broadcasted_iota(i32, nbr_in.shape, 1)
    tile = sum((at >= k * fan).astype(i32) for k in range(1, tile_rows)) - side * half
    owns = (tile >= 0) & (tile < half)
    ext = nbr_in[...] - first_tile + reach
    plan_groups(PRIOR_PLAN, jnp.where(owns, tile, 0), jnp.where(owns, ext, most), begin, most, built[5])
    built[6][:, : ext.shape[1]] = ext
    built[6][:, ext.shape[1] :] = jnp.zeros((1, LANES), i32) + side
    lists = [
        pltpu.make_async_copy(src, dst, small_sems.at[3 + k])
        for k, (src, dst) in enumerate(zip(built, plans))
    ]
    for one in lists:
        one.start()

    lax.fori_loop(0, rounds[0], wait(begin, prior, prior_plain, 0), 0)
    lax.fori_loop(0, rounds[1], wait(0, jac, jac_plain, rounds[0]), 0)
    for one in lists:
        one.wait()


def turn_kernel(chunk, plain, turned):
    def one(c, _):
        for u in range(chunk):
            turned[c * chunk + u] = plain[c * chunk + u].T
        return 0

    lax.fori_loop(0, plain.shape[0] // chunk, one, 0)


def turn_blocks(plain, name):
    vmem = pl.BlockSpec(memory_space=pltpu.VMEM)
    return pl.pallas_call(
        functools.partial(turn_kernel, chunk_of(plain.shape[0], 48)),
        in_specs=[vmem],
        out_specs=vmem,
        out_shape=pltpu.VMEM(plain.shape, HALF),
        compiler_params=pltpu.CompilerParams(vmem_limit_bytes=VMEM_LIMIT),
        cost_estimate=pl.CostEstimate(flops=0, bytes_accessed=2 * plain.size, transcendentals=0),
        name=name,
    )(plain)


def setup(where, obs, flux, nbr, prior, jac, rows):
    most = max(rows[:2])
    owned = rows[1] // 2 * rows[2]
    chunk = chunk_of(math.gcd(owned, jac.shape[0]), 24)
    smem = pl.BlockSpec(memory_space=pltpu.SMEM)
    vmem = pl.BlockSpec(memory_space=pltpu.VMEM)
    hbm = pl.BlockSpec(memory_space=pl.ANY)
    own = pltpu.VMEM((owned,) + prior.shape[1:], HALF)
    all_blocks = pltpu.VMEM(jac.shape, HALF)
    i32 = jnp.int32
    lengths = []
    used = (FORWARD_PLAN, FORWARD_PLAN, NEAR_PLAN, REST_PLAN, REST_PLAN, PRIOR_PLAN)
    for plan in used:
        slots, groups = plan_sizes(plan, (nbr if plan is used[-1] else obs).shape[1], most)
        lengths.append(2 * slots + groups)
    lengths.append(nbr.shape[1] + LANES)
    return pl.pallas_call(
        functools.partial(setup_kernel, rows, chunk),
        in_specs=[smem] + [hbm] * 5,
        out_specs=[vmem] * 2 + [smem] * 7,
        out_shape=[own, all_blocks] + [pltpu.SMEM((1, n), i32) for n in lengths],
        scratch_shapes=[pltpu.VMEM(v.shape, i32) for v in (obs, flux, nbr)]
        + [pltpu.VMEM((1, n), i32) for n in lengths]
        + [
            pltpu.SemaphoreType.DMA((10,)),
            pltpu.SemaphoreType.DMA(((owned + jac.shape[0]) // chunk,)),
        ],
        compiler_params=pltpu.CompilerParams(vmem_limit_bytes=VMEM_LIMIT),
        name="setup",
    )(where, *(pltpu.with_memory_space_constraint(v, pltpu.HBM) for v in (obs, flux, nbr, prior, jac)))


def grouped_products(plan, sizes, lists, x, blocks, total):
    group, per_round = plan
    slots, groups = sizes

    def one(c, _):
        products = []
        for u in range(per_round):
            first = (c * per_round + u) * group
            rows = [x[lists[0, first + g]] for g in range(group)]
            tiles = [blocks[lists[0, slots + first + g]] for g in range(group)]
            products.append(matmul(jnp.concatenate(rows, axis=1), jnp.concatenate(tiles, axis=0)))
        for u in range(per_round):
            total[lists[0, 2 * slots + c * per_round + u]] += products[u]
        return 0

    lax.fori_loop(0, lists[0, 2 * slots + groups - 1], one, 0)


def jac_kernel(plan, sizes, n_parts, started, n_outs, lists, *refs):
    parts, refs = refs[:n_parts], refs[n_parts:]
    if started:
        begun, refs = refs[0], refs[1:]
    jac, outs, (x, total) = refs[0], refs[1 : 1 + n_outs], refs[1 + n_outs :]
    rows = parts[0].shape[0]
    for k, part in enumerate(parts):
        x[k * rows : (k + 1) * rows] = part[...]
    x[x.shape[0] - 1] = jnp.zeros(x.shape[1:], HALF)
    if started:
        total[: begun.shape[0]] = begun[...]
    else:
        total[...] = jnp.zeros_like(total)
    grouped_products(plan, sizes, lists, x, jac, total)
    rows = outs[0].shape[0]
    for k, out in enumerate(outs):
        out[...] = total[k * rows : (k + 1) * rows].astype(out.dtype)


def jac_pass(plan, lists, parts, begun, jac, rows, out_rows, out_types, name):
    probes, width = parts[0].shape[1:]
    n_outs = len(out_types)
    smem = pl.BlockSpec(memory_space=pltpu.SMEM)
    vmem = pl.BlockSpec(memory_space=pltpu.VMEM)
    operands = (lists, *parts) + (() if begun is None else (begun,)) + (jac,)
    sizes = plan_sizes(plan, jac.shape[0], rows)
    return pl.pallas_call(
        functools.partial(jac_kernel, plan, sizes, len(parts), begun is not None, n_outs),
        in_specs=[smem] + [vmem] * (len(operands) - 1),
        out_specs=[vmem] * n_outs,
        out_shape=[jax.ShapeDtypeStruct((out_rows // n_outs, probes, width), t) for t in out_types],
        scratch_shapes=[
            pltpu.VMEM((rows + 1, probes, width), HALF),
            pltpu.VMEM((rows + 1, probes, width), F32),
        ],
        compiler_params=pltpu.CompilerParams(vmem_limit_bytes=VMEM_LIMIT),
        cost_estimate=pl.CostEstimate(flops=0, bytes_accessed=jac.size, transcendentals=0),
        name=name,
    )(*operands)


def gather_kernel(rows, sizes, nbr, lists, mine, other, prior, ext, to_core, to_far, x, total):
    half = mine.shape[0]
    side = nbr[0, nbr.shape[1] - 1]
    x[:half] = (mine[...].astype(F32) + other[...].astype(F32)).astype(HALF)
    x[rows] = jnp.zeros(x.shape[1:], HALF)
    total[...] = jnp.zeros_like(total)
    grouped_products(PRIOR_PLAN, sizes, lists, x, prior, total)
    ext[...] = total[: 2 * half]
    to_core[...] = total[pl.ds(half * (1 - side), half)].astype(HALF)
    to_far[...] = total[pl.ds(half * side, half)].astype(HALF)


def gather_tiles(nbr, lists, mine, other, prior, rows):
    tiles, probes, width = mine.shape
    smem = pl.BlockSpec(memory_space=pltpu.SMEM)
    vmem = pl.BlockSpec(memory_space=pltpu.VMEM)
    return pl.pallas_call(
        functools.partial(gather_kernel, rows, plan_sizes(PRIOR_PLAN, nbr.shape[1] - LANES, rows)),
        in_specs=[smem, smem, vmem, vmem, vmem],
        out_specs=[vmem] * 3,
        out_shape=[
            jax.ShapeDtypeStruct((2 * tiles, probes, width), F32),
            jax.ShapeDtypeStruct((tiles, probes, width), HALF),
            jax.ShapeDtypeStruct((tiles, probes, width), HALF),
        ],
        scratch_shapes=[
            pltpu.VMEM((rows + 1, probes, width), HALF),
            pltpu.VMEM((rows + 1, probes, width), F32),
        ],
        compiler_params=pltpu.CompilerParams(vmem_limit_bytes=VMEM_LIMIT),
        name="prior_adjoint",
    )(nbr, lists, mine, other, prior)


def spread_kernel(first, fan, nbr, *refs):
    prior, out, field = refs[-3:]
    tiles = out.shape[0]
    chunk = chunk_of(tiles, 24)
    side = nbr[0, nbr.shape[1] - 1]
    if first:
        probes, beyond = refs[:2]
        reach = beyond.shape[0]
        inner = 2 * tiles - reach
        field[pl.ds(reach * (1 - side), inner)] = probes[pl.ds(reach * side, inner)]
        field[pl.ds(inner * side, reach)] = beyond[...]
    else:
        ext, from_core, from_far = refs[:3]
        for begin, update in ((tiles * (1 - side), from_core), (tiles * side, from_far)):
            at = pl.ds(begin, tiles)
            field[at] = (ext[at] + update[...].astype(F32)).astype(HALF)

    def one(c, _):
        for u in range(chunk):
            t = c * chunk + u
            row = [field[nbr[0, (side * tiles + t) * fan + k]] for k in range(fan)]
            tile = prior[pl.ds(t * fan, fan)]
            tile = tile.reshape(fan * tile.shape[1], tile.shape[2])
            out[t] = matmul(jnp.concatenate(row, axis=1), tile).astype(HALF)
        return 0

    lax.fori_loop(0, tiles // chunk, one, 0)


def spread_tiles(nbr, fields, prior):
    ext_tiles, probes, width = fields[0].shape
    tiles = ext_tiles // 2
    smem = pl.BlockSpec(memory_space=pltpu.SMEM)
    vmem = pl.BlockSpec(memory_space=pltpu.VMEM)
    return pl.pallas_call(
        functools.partial(spread_kernel, len(fields) == 2, prior.shape[0] // tiles),
        in_specs=[smem] + [vmem] * len(fields) + [vmem],
        out_specs=vmem,
        out_shape=jax.ShapeDtypeStruct((tiles, probes, width), HALF),
        scratch_shapes=[pltpu.VMEM(fields[0].shape, HALF)],
        compiler_params=pltpu.CompilerParams(vmem_limit_bytes=VMEM_LIMIT),
        name="prior_spread",
    )(nbr, *fields, prior)


def shards(probes, prior_tiles, neighbours, jac, jac_obs, jac_flux, counts, rinv):
    n_obs, n_flux = lax.axis_size("obs"), lax.axis_size("flux")
    tile_count = probes.shape[0]
    half = tile_count // 2
    reach = tile_count // 4
    obs_rows = rinv.shape[0]
    quarter = obs_rows // 4
    blocks = jac[0, 0]
    flux_at = lax.axis_index("flux")
    side = lax.rem(lax.axis_index("obs"), 2)
    corner = lax.rem(flux_at, 4)
    fan = neighbours.shape[1]
    prior = prior_tiles.reshape((tile_count * fan,) + prior_tiles.shape[2:])
    own_rinv = lax.dynamic_slice_in_dim(rinv, corner * quarter, quarter, 0)[:, None, :]
    rows = max(obs_rows, tile_count)
    sizes = (obs_rows, tile_count, fan)

    def swap_core(value):
        return exchange(value, lambda i, j: (i ^ 1, j))

    def swap_far(value):
        def partner(i, j):
            to = j - 1 if i % 2 == 0 else j + 1
            return (i ^ 1, to) if 0 <= to < n_flux else None

        return exchange(value, partner)

    def swap_flux(value, bits):
        return exchange(value, lambda i, j: (i, j ^ bits))

    edge = jnp.where(side == 0, probes[:reach], probes[tile_count - reach :])
    beyond = swap_far(edge)
    where = jnp.stack([side, corner, counts[0, 0], flux_at * tile_count + side * half])
    nbr = neighbours.reshape(1, tile_count * fan)

    where, own_rinv, nbr, prior, blocks = lax.optimization_barrier((where, own_rinv, nbr, prior, blocks))
    prior_plain, jac_plain, *jac_lists, prior_lists, nbr = setup(
        where, jac_obs[0], jac_flux[0], nbr, prior, blocks, sizes
    )
    fields = (probes, beyond)
    for step in range(STEPS):
        spread = spread_tiles(nbr, fields, prior_plain)
        other = swap_core(spread)
        (begun,) = jac_pass(
            FORWARD_PLAN, jac_lists[0], (spread,), None, jac_plain, rows, obs_rows, [F32], "forward_own"
        )
        types = [F32, HALF, HALF, HALF]
        pieces = jac_pass(
            FORWARD_PLAN, jac_lists[1], (other,), begun, jac_plain, rows, obs_rows, types, "forward_other"
        )
        if step == 0:
            pieces, jac_plain = lax.optimization_barrier((pieces, jac_plain))
            jac_turned = turn_blocks(jac_plain, "jac_turn")
        total = pieces[0]
        for bits in range(1, 4):
            total = total + swap_flux(pieces[bits], bits).astype(F32)
        bits = 4
        while bits < n_flux:
            sent = total.astype(HALF)
            total = sent.astype(F32) + swap_flux(sent, bits).astype(F32)
            bits *= 2
        weighted = (total * own_rinv).astype(HALF)
        rest = tuple(swap_flux(weighted, bits) for bits in range(1, 4))
        mine, theirs = jac_pass(
            NEAR_PLAN, jac_lists[2], (weighted,), None, jac_turned, rows, tile_count, [F32, F32], "adjoint_near"
        )
        (theirs,) = jac_pass(
            REST_PLAN, jac_lists[3], rest, theirs, jac_turned, rows, half, [HALF], "adjoint_other"
        )
        (mine,) = jac_pass(REST_PLAN, jac_lists[4], rest, mine, jac_turned, rows, half, [F32], "adjoint_own")
        mine = (mine + swap_core(theirs).astype(F32)).astype(HALF)
        if step == 0:
            mine, prior_plain = lax.optimization_barrier((mine, prior_plain))
            prior_turned = turn_blocks(prior_plain, "prior_turn")
        bits = 2
        while bits < n_obs:
            other = exchange(mine, lambda i, j, bits=bits: (i ^ bits, j))
            bits *= 2
            if bits < n_obs:
                mine = (mine.astype(F32) + other.astype(F32)).astype(HALF)
        ext, to_core, to_far = gather_tiles(nbr, prior_lists, mine, other, prior_turned, rows)
        if step < STEPS - 1:
            fields = (ext, swap_core(to_core), swap_far(to_far))
    lower = side == 0
    from_core = swap_core(jnp.where(lower, to_core[half - reach :], to_core[:reach])).astype(F32)
    from_far = swap_far(jnp.where(lower, to_far[:reach], to_far[half - reach :])).astype(F32)
    low = jnp.where(lower, from_far, from_core)
    high = jnp.where(lower, from_core, from_far)
    own = (ext[reach : reach + half] + jnp.concatenate([low, high], axis=0)).astype(HALF)
    other = swap_core(own)
    first = jnp.where(side == 0, own, other)
    second = jnp.where(side == 0, other, own)
    return jnp.concatenate([first, second], axis=0)


def solution(mesh):
    placed = (
        P("flux", None, None),
        P("flux", None, None, None),
        P("flux", None),
        P("obs", "flux", None, None, None),
        P("obs", "flux", None),
        P("obs", "flux", None),
        P("obs", "flux"),
        P("obs", None),
    )
    return jax.shard_map(
        shards, mesh=mesh, in_specs=placed, out_specs=P("flux", None, None), check_vma=False
    )
```

```python
import functools
import math

import jax
import jax.numpy as jnp
from jax import lax
from jax.experimental import pallas as pl
from jax.experimental.pallas import tpu as pltpu
from jax.sharding import PartitionSpec as P

STEPS = 4
F32 = jnp.float32
HALF = jnp.bfloat16
VMEM_LIMIT = 8 * 2**20
LANES = 128
FORWARD_PLAN = (2, 56)
NEAR_PLAN = (2, 32)
REST_PLAN = (2, 42)
PRIOR_PLAN = (2, 56)


def matmul(a, b):
    return lax.dot_general(a, b, (((1,), (0,)), ((), ())), preferred_element_type=F32)


def chunk_of(count, most):
    return max(c for c in range(1, most + 1) if count % c == 0)


def exchange(value, partner):
    n_obs, n_flux = lax.axis_size("obs"), lax.axis_size("flux")
    route = []
    for i in range(n_obs):
        for j in range(n_flux):
            to = partner(i, j)
            if to is not None:
                route.append((i * n_flux + j, to[0] * n_flux + to[1]))
    return lax.ppermute(value, ("obs", "flux"), route)


def plan_sizes(plan, blocks, dst_rows):
    group, per_round = plan
    groups = blocks // group + dst_rows
    groups += -groups % per_round
    slots = groups * group
    return slots + -slots % LANES, groups + 1 + -(groups + 1) % LANES


def columns(row):
    parts = [
        jnp.broadcast_to(row[:, k : k + LANES], (LANES, LANES)).T for k in range(0, row.shape[1], LANES)
    ]
    return jnp.concatenate(parts, axis=0)


def plan_groups(plan, src, dst, first, rows, out):
    group, per_round = plan
    blocks = dst.shape[1]
    slots, groups = plan_sizes(plan, blocks, rows)
    i32 = jnp.int32
    lane = lax.broadcasted_iota(i32, (blocks, LANES), 1)
    at = lax.broadcasted_iota(i32, (blocks, LANES), 0)
    src_at, dst_at = columns(src), columns(dst)
    rank = jnp.zeros((blocks, LANES), F32)
    for k in range(0, blocks, LANES):
        same = (dst_at == dst[:, k : k + LANES]) & (lane + k < at)
        rank += same.astype(F32)
    rank = jnp.sum(rank, axis=1, keepdims=True)
    fills = jnp.sum((dst_at == lane).astype(F32), axis=0, keepdims=True)
    sizes = jnp.where(lane[:1] < rows, jnp.floor((fills + (group - 1)) * (1.0 / group)), 0.0)
    begin = jnp.sum(jnp.where(lane < dst_at, sizes, 0.0), axis=1, keepdims=True)
    place = (begin * group + rank).astype(i32)
    place = jnp.where(dst_at < rows, place, slots)
    for k in range(0, slots, LANES):
        hit = place == lane + k
        of = jnp.sum(jnp.where(hit, (src_at - rows).astype(F32), 0.0), axis=0, keepdims=True)
        out[:, k : k + LANES] = of.astype(i32) + rows
        of = jnp.sum(jnp.where(hit, (at - first).astype(F32), 0.0), axis=0, keepdims=True)
        out[:, slots + k : slots + k + LANES] = of.astype(i32)
    full = jnp.sum(sizes, axis=1, keepdims=True)
    rounds = jnp.sum((lane[:1].astype(F32) * per_round < full).astype(F32), axis=1, keepdims=True)
    for k in range(0, groups, LANES):
        lead = place == (lane + k) * group
        of = jnp.sum(jnp.where(lead, (dst_at - rows).astype(F32), 0.0), axis=0, keepdims=True)
        of = jnp.where(lane[:1] + k == groups - 1, rounds, of + rows)
        out[:, 2 * slots + k : 2 * slots + k + LANES] = of.astype(i32)


def setup_kernel(
    rows, chunk, where, obs, flux, nbr, prior,
    prior_plain, *refs
):
    plans, (obs_in, flux_in, nbr_in) = refs[:7], refs[7:10]
    built, (small_sems, sems) = refs[10:17], refs[17:]
    side, corner, count, first_tile = where[0], where[1], where[2], where[3]
    owned = prior_plain.shape[0]
    begin = side * owned
    rounds = (owned // chunk,)

    def copy(c, first, source, plain, offset):
        to = pl.ds(c * chunk, chunk)
        return pltpu.make_async_copy(source.at[pl.ds(first + c * chunk, chunk)], plain.at[to], sems.at[offset + c])

    def start(first, source, plain, offset):
        def one(c, _):
            copy(c, first, source, plain, offset).start()
            return 0

        return one

    def wait(first, source, plain, offset):
        def one(c, _):
            copy(c, first, source, plain, offset).wait()
            return 0

        return one

    small = ((obs, obs_in), (flux, flux_in), (nbr, nbr_in))
    small = [pltpu.make_async_copy(src, dst, small_sems.at[k]) for k, (src, dst) in enumerate(small)]
    for one in small:
        one.start()
    lax.fori_loop(0, rounds[0], start(begin, prior, prior_plain, 0), 0)
    for one in small:
        one.wait()

    obs_rows, tile_rows, fan = rows
    half = tile_rows // 2
    reach = tile_rows // 4
    quarter = obs_rows // 4
    most = max(obs_rows, tile_rows)
    i32 = jnp.int32
    at = lax.broadcasted_iota(i32, obs_in.shape, 1)
    live = at < count
    block = sum((obs_in[...] >= k * quarter).astype(i32) for k in range(1, 4))
    obs_at = (block ^ corner) * quarter + obs_in[...] - block * quarter
    block = (flux_in[...] >= half).astype(i32)
    tile_at = (block ^ side) * half + flux_in[...] - block * half
    own, near = tile_at < half, obs_at < quarter
    for plan, src, dst, use, out in (
        (FORWARD_PLAN, tile_at, obs_at, own, built[0]),
        (FORWARD_PLAN, tile_at - half, obs_at, ~own, built[1]),
        (NEAR_PLAN, obs_at, tile_at, near, built[2]),
        (REST_PLAN, obs_at - quarter, tile_at - half, ~near & ~own, built[3]),
        (REST_PLAN, obs_at - quarter, tile_at, ~near & own, built[4]),
    ):
        use = live & use
        plan_groups(plan, jnp.where(use, src, 0), jnp.where(use, dst, most), 0, most, out)
    at = lax.broadcasted_iota(i32, nbr_in.shape, 1)
    tile = sum((at >= k * fan).astype(i32) for k in range(1, tile_rows)) - side * half
    owns = (tile >= 0) & (tile < half)
    ext = nbr_in[...] - first_tile + reach
    plan_groups(PRIOR_PLAN, jnp.where(owns, tile, 0), jnp.where(owns, ext, most), begin, most, built[5])
    built[6][:, : ext.shape[1]] = ext
    built[6][:, ext.shape[1] :] = jnp.zeros((1, LANES), i32) + side
    lists = [
        pltpu.make_async_copy(src, dst, small_sems.at[3 + k])
        for k, (src, dst) in enumerate(zip(built, plans))
    ]
    for one in lists:
        one.start()

    lax.fori_loop(0, rounds[0], wait(begin, prior, prior_plain, 0), 0)
    for one in lists:
        one.wait()


def turn_kernel(chunk, plain, turned):
    def one(c, _):
        for u in range(chunk):
            turned[c * chunk + u] = plain[c * chunk + u].T
        return 0

    lax.fori_loop(0, plain.shape[0] // chunk, one, 0)


def turn_blocks(plain, name):
    vmem = pl.BlockSpec(memory_space=pltpu.VMEM)
    return pl.pallas_call(
        functools.partial(turn_kernel, chunk_of(plain.shape[0], 48)),
        in_specs=[vmem],
        out_specs=vmem,
        out_shape=pltpu.VMEM(plain.shape, HALF),
        compiler_params=pltpu.CompilerParams(vmem_limit_bytes=VMEM_LIMIT),
        cost_estimate=pl.CostEstimate(flops=0, bytes_accessed=2 * plain.size, transcendentals=0),
        name=name,
    )(plain)


def setup(where, obs, flux, nbr, prior, rows):
    most = max(rows[:2])
    owned = rows[1] // 2 * rows[2]
    chunk = chunk_of(owned, 24)
    smem = pl.BlockSpec(memory_space=pltpu.SMEM)
    vmem = pl.BlockSpec(memory_space=pltpu.VMEM)
    hbm = pl.BlockSpec(memory_space=pl.ANY)
    own = pltpu.VMEM((owned,) + prior.shape[1:], HALF)
    i32 = jnp.int32
    lengths = []
    used = (FORWARD_PLAN, FORWARD_PLAN, NEAR_PLAN, REST_PLAN, REST_PLAN, PRIOR_PLAN)
    for plan in used:
        slots, groups = plan_sizes(plan, (nbr if plan is used[-1] else obs).shape[1], most)
        lengths.append(2 * slots + groups)
    lengths.append(nbr.shape[1] + LANES)
    return pl.pallas_call(
        functools.partial(setup_kernel, rows, chunk),
        in_specs=[smem] + [hbm] * 4,
        out_specs=[vmem] + [smem] * 7,
        out_shape=[own] + [pltpu.SMEM((1, n), i32) for n in lengths],
        scratch_shapes=[pltpu.VMEM(v.shape, i32) for v in (obs, flux, nbr)]
        + [pltpu.VMEM((1, n), i32) for n in lengths]
        + [
            pltpu.SemaphoreType.DMA((10,)),
            pltpu.SemaphoreType.DMA((owned // chunk,)),
        ],
        compiler_params=pltpu.CompilerParams(vmem_limit_bytes=VMEM_LIMIT),
        name="setup",
    )(where, *(pltpu.with_memory_space_constraint(v, pltpu.HBM) for v in (obs, flux, nbr, prior)))


def grouped_products(plan, sizes, lists, x, blocks, total):
    group, per_round = plan
    slots, groups = sizes

    def one(c, _):
        products = []
        for u in range(per_round):
            first = (c * per_round + u) * group
            rows = [x[lists[0, first + g]] for g in range(group)]
            tiles = [blocks[lists[0, slots + first + g]] for g in range(group)]
            products.append(matmul(jnp.concatenate(rows, axis=1), jnp.concatenate(tiles, axis=0)))
        for u in range(per_round):
            total[lists[0, 2 * slots + c * per_round + u]] += products[u]
        return 0

    lax.fori_loop(0, lists[0, 2 * slots + groups - 1], one, 0)


def jac_kernel(plan, sizes, n_parts, started, n_outs, lists, *refs):
    parts, refs = refs[:n_parts], refs[n_parts:]
    if started:
        begun, refs = refs[0], refs[1:]
    jac, outs, (x, total) = refs[0], refs[1 : 1 + n_outs], refs[1 + n_outs :]
    rows = parts[0].shape[0]
    for k, part in enumerate(parts):
        x[k * rows : (k + 1) * rows] = part[...]
    x[x.shape[0] - 1] = jnp.zeros(x.shape[1:], HALF)
    if started:
        total[: begun.shape[0]] = begun[...]
    else:
        total[...] = jnp.zeros_like(total)
    grouped_products(plan, sizes, lists, x, jac, total)
    rows = outs[0].shape[0]
    for k, out in enumerate(outs):
        out[...] = total[k * rows : (k + 1) * rows].astype(out.dtype)


def jac_pass(plan, lists, parts, begun, jac, rows, out_rows, out_types, name):
    probes, width = parts[0].shape[1:]
    n_outs = len(out_types)
    smem = pl.BlockSpec(memory_space=pltpu.SMEM)
    vmem = pl.BlockSpec(memory_space=pltpu.VMEM)
    operands = (lists, *parts) + (() if begun is None else (begun,)) + (jac,)
    sizes = plan_sizes(plan, jac.shape[0], rows)
    return pl.pallas_call(
        functools.partial(jac_kernel, plan, sizes, len(parts), begun is not None, n_outs),
        in_specs=[smem] + [vmem] * (len(operands) - 1),
        out_specs=[vmem] * n_outs,
        out_shape=[jax.ShapeDtypeStruct((out_rows // n_outs, probes, width), t) for t in out_types],
        scratch_shapes=[
            pltpu.VMEM((rows + 1, probes, width), HALF),
            pltpu.VMEM((rows + 1, probes, width), F32),
        ],
        compiler_params=pltpu.CompilerParams(vmem_limit_bytes=VMEM_LIMIT),
        cost_estimate=pl.CostEstimate(flops=0, bytes_accessed=jac.size, transcendentals=0),
        name=name,
    )(*operands)


def gather_kernel(rows, sizes, nbr, lists, mine, other, prior, ext, to_core, to_far, x, total):
    half = mine.shape[0]
    side = nbr[0, nbr.shape[1] - 1]
    x[:half] = (mine[...].astype(F32) + other[...].astype(F32)).astype(HALF)
    x[rows] = jnp.zeros(x.shape[1:], HALF)
    total[...] = jnp.zeros_like(total)
    grouped_products(PRIOR_PLAN, sizes, lists, x, prior, total)
    ext[...] = total[: 2 * half]
    to_core[...] = total[pl.ds(half * (1 - side), half)].astype(HALF)
    to_far[...] = total[pl.ds(half * side, half)].astype(HALF)


def gather_tiles(nbr, lists, mine, other, prior, rows):
    tiles, probes, width = mine.shape
    smem = pl.BlockSpec(memory_space=pltpu.SMEM)
    vmem = pl.BlockSpec(memory_space=pltpu.VMEM)
    return pl.pallas_call(
        functools.partial(gather_kernel, rows, plan_sizes(PRIOR_PLAN, nbr.shape[1] - LANES, rows)),
        in_specs=[smem, smem, vmem, vmem, vmem],
        out_specs=[vmem] * 3,
        out_shape=[
            jax.ShapeDtypeStruct((2 * tiles, probes, width), F32),
            jax.ShapeDtypeStruct((tiles, probes, width), HALF),
            jax.ShapeDtypeStruct((tiles, probes, width), HALF),
        ],
        scratch_shapes=[
            pltpu.VMEM((rows + 1, probes, width), HALF),
            pltpu.VMEM((rows + 1, probes, width), F32),
        ],
        compiler_params=pltpu.CompilerParams(vmem_limit_bytes=VMEM_LIMIT),
        name="prior_adjoint",
    )(nbr, lists, mine, other, prior)


def spread_kernel(first, fan, nbr, *refs):
    prior, out, field = refs[-3:]
    tiles = out.shape[0]
    chunk = chunk_of(tiles, 24)
    side = nbr[0, nbr.shape[1] - 1]
    if first:
        probes, beyond = refs[:2]
        reach = beyond.shape[0]
        inner = 2 * tiles - reach
        field[pl.ds(reach * (1 - side), inner)] = probes[pl.ds(reach * side, inner)]
        field[pl.ds(inner * side, reach)] = beyond[...]
    else:
        ext, from_core, from_far = refs[:3]
        for begin, update in ((tiles * (1 - side), from_core), (tiles * side, from_far)):
            at = pl.ds(begin, tiles)
            field[at] = (ext[at] + update[...].astype(F32)).astype(HALF)

    def one(c, _):
        for u in range(chunk):
            t = c * chunk + u
            row = [field[nbr[0, (side * tiles + t) * fan + k]] for k in range(fan)]
            tile = prior[pl.ds(t * fan, fan)]
            tile = tile.reshape(fan * tile.shape[1], tile.shape[2])
            out[t] = matmul(jnp.concatenate(row, axis=1), tile).astype(HALF)
        return 0

    lax.fori_loop(0, tiles // chunk, one, 0)


def spread_tiles(nbr, fields, prior):
    ext_tiles, probes, width = fields[0].shape
    tiles = ext_tiles // 2
    smem = pl.BlockSpec(memory_space=pltpu.SMEM)
    vmem = pl.BlockSpec(memory_space=pltpu.VMEM)
    return pl.pallas_call(
        functools.partial(spread_kernel, len(fields) == 2, prior.shape[0] // tiles),
        in_specs=[smem] + [vmem] * len(fields) + [vmem],
        out_specs=vmem,
        out_shape=jax.ShapeDtypeStruct((tiles, probes, width), HALF),
        scratch_shapes=[pltpu.VMEM(fields[0].shape, HALF)],
        compiler_params=pltpu.CompilerParams(vmem_limit_bytes=VMEM_LIMIT),
        name="prior_spread",
    )(nbr, *fields, prior)


def shards(probes, prior_tiles, neighbours, jac, jac_obs, jac_flux, counts, rinv):
    n_obs, n_flux = lax.axis_size("obs"), lax.axis_size("flux")
    tile_count = probes.shape[0]
    half = tile_count // 2
    reach = tile_count // 4
    obs_rows = rinv.shape[0]
    quarter = obs_rows // 4
    blocks = jac[0, 0]
    flux_at = lax.axis_index("flux")
    side = lax.rem(lax.axis_index("obs"), 2)
    corner = lax.rem(flux_at, 4)
    fan = neighbours.shape[1]
    prior = prior_tiles.reshape((tile_count * fan,) + prior_tiles.shape[2:])
    own_rinv = lax.dynamic_slice_in_dim(rinv, corner * quarter, quarter, 0)[:, None, :]
    rows = max(obs_rows, tile_count)
    sizes = (obs_rows, tile_count, fan)

    def swap_core(value):
        return exchange(value, lambda i, j: (i ^ 1, j))

    def swap_far(value):
        def partner(i, j):
            to = j - 1 if i % 2 == 0 else j + 1
            return (i ^ 1, to) if 0 <= to < n_flux else None

        return exchange(value, partner)

    def swap_flux(value, bits):
        return exchange(value, lambda i, j: (i, j ^ bits))

    edge = jnp.where(side == 0, probes[:reach], probes[tile_count - reach :])
    beyond = swap_far(edge)
    where = jnp.stack([side, corner, counts[0, 0], flux_at * tile_count + side * half])
    nbr = neighbours.reshape(1, tile_count * fan)

    where, own_rinv, nbr, prior, blocks = lax.optimization_barrier((where, own_rinv, nbr, prior, blocks))
    jac_plain = blocks
    prior_plain, *jac_lists, prior_lists, nbr = setup(
        where, jac_obs[0], jac_flux[0], nbr, prior, sizes
    )
    fields = (probes, beyond)
    for step in range(STEPS):
        spread = spread_tiles(nbr, fields, prior_plain)
        other = swap_core(spread)
        (begun,) = jac_pass(
            FORWARD_PLAN, jac_lists[0], (spread,), None, jac_plain, rows, obs_rows, [F32], "forward_own"
        )
        types = [F32, HALF, HALF, HALF]
        pieces = jac_pass(
            FORWARD_PLAN, jac_lists[1], (other,), begun, jac_plain, rows, obs_rows, types, "forward_other"
        )
        if step == 0:
            pieces, jac_plain = lax.optimization_barrier((pieces, jac_plain))
            jac_turned = turn_blocks(jac_plain, "jac_turn")
        total = pieces[0]
        for bits in range(1, 4):
            total = total + swap_flux(pieces[bits], bits).astype(F32)
        if step == 0:
            total, jac_turned = lax.optimization_barrier((total, jac_turned))
        bits = 4
        while bits < n_flux:
            sent = total.astype(HALF)
            total = sent.astype(F32) + swap_flux(sent, bits).astype(F32)
            bits *= 2
        weighted = (total * own_rinv).astype(HALF)
        rest = tuple(swap_flux(weighted, bits) for bits in range(1, 4))
        mine, theirs = jac_pass(
            NEAR_PLAN, jac_lists[2], (weighted,), None, jac_turned, rows, tile_count, [F32, F32], "adjoint_near"
        )
        (theirs,) = jac_pass(
            REST_PLAN, jac_lists[3], rest, theirs, jac_turned, rows, half, [HALF], "adjoint_other"
        )
        (mine,) = jac_pass(REST_PLAN, jac_lists[4], rest, mine, jac_turned, rows, half, [F32], "adjoint_own")
        mine = (mine + swap_core(theirs).astype(F32)).astype(HALF)
        if step == 0:
            mine, prior_plain = lax.optimization_barrier((mine, prior_plain))
            prior_turned = turn_blocks(prior_plain, "prior_turn")
        bits = 2
        while bits < n_obs:
            other = exchange(mine, lambda i, j, bits=bits: (i ^ bits, j))
            bits *= 2
            if bits < n_obs:
                mine = (mine.astype(F32) + other.astype(F32)).astype(HALF)
        ext, to_core, to_far = gather_tiles(nbr, prior_lists, mine, other, prior_turned, rows)
        if step < STEPS - 1:
            fields = (ext, swap_core(to_core), swap_far(to_far))
    lower = side == 0
    from_core = swap_core(jnp.where(lower, to_core[half - reach :], to_core[:reach])).astype(F32)
    from_far = swap_far(jnp.where(lower, to_far[:reach], to_far[half - reach :])).astype(F32)
    low = jnp.where(lower, from_far, from_core)
    high = jnp.where(lower, from_core, from_far)
    own = (ext[reach : reach + half] + jnp.concatenate([low, high], axis=0)).astype(HALF)
    other = swap_core(own)
    first = jnp.where(side == 0, own, other)
    second = jnp.where(side == 0, other, own)
    return jnp.concatenate([first, second], axis=0)


def solution(mesh):
    placed = (
        P("flux", None, None),
        P("flux", None, None, None),
        P("flux", None),
        P("obs", "flux", None, None, None),
        P("obs", "flux", None),
        P("obs", "flux", None),
        P("obs", "flux"),
        P("obs", None),
    )
    return jax.shard_map(
        shards, mesh=mesh, in_specs=placed, out_specs=P("flux", None, None), check_vma=False
    )
```

```python
import functools
import math

import jax
import jax.numpy as jnp
from jax import lax
from jax.experimental import pallas as pl
from jax.experimental.pallas import tpu as pltpu
from jax.sharding import PartitionSpec as P

STEPS = 4
F32 = jnp.float32
HALF = jnp.bfloat16
VMEM_LIMIT = 8 * 2**20
LANES = 128
FORWARD_PLANS = ((2, 42), (2, 42), (2, 28))
ADJOINT_PLANS = ((2, 32), (2, 32), (2, 32), (2, 18), (2, 18))
PRIOR_PLAN = (2, 56)


def matmul(a, b):
    return lax.dot_general(a, b, (((1,), (0,)), ((), ())), preferred_element_type=F32)


def chunk_of(count, most):
    return max(c for c in range(1, most + 1) if count % c == 0)


def exchange(value, partner):
    n_obs, n_flux = lax.axis_size("obs"), lax.axis_size("flux")
    route = []
    for i in range(n_obs):
        for j in range(n_flux):
            to = partner(i, j)
            if to is not None:
                route.append((i * n_flux + j, to[0] * n_flux + to[1]))
    return lax.ppermute(value, ("obs", "flux"), route)


def plan_sizes(plan, blocks, dst_rows):
    group, per_round = plan
    groups = blocks // group + dst_rows
    groups += -groups % per_round
    slots = groups * group
    return slots + -slots % LANES, groups + 1 + -(groups + 1) % LANES


def columns(row):
    parts = [
        jnp.broadcast_to(row[:, k : k + LANES], (LANES, LANES)).T for k in range(0, row.shape[1], LANES)
    ]
    return jnp.concatenate(parts, axis=0)


def plan_groups(plan, src, dst, first, rows, out):
    group, per_round = plan
    blocks = dst.shape[1]
    slots, groups = plan_sizes(plan, blocks, rows)
    i32 = jnp.int32
    lane = lax.broadcasted_iota(i32, (blocks, LANES), 1)
    at = lax.broadcasted_iota(i32, (blocks, LANES), 0)
    src_at, dst_at = columns(src), columns(dst)
    rank = jnp.zeros((blocks, LANES), F32)
    for k in range(0, blocks, LANES):
        same = (dst_at == dst[:, k : k + LANES]) & (lane + k < at)
        rank += same.astype(F32)
    rank = jnp.sum(rank, axis=1, keepdims=True)
    fills = jnp.sum((dst_at == lane).astype(F32), axis=0, keepdims=True)
    sizes = jnp.where(lane[:1] < rows, jnp.floor((fills + (group - 1)) * (1.0 / group)), 0.0)
    begin = jnp.sum(jnp.where(lane < dst_at, sizes, 0.0), axis=1, keepdims=True)
    place = (begin * group + rank).astype(i32)
    place = jnp.where(dst_at < rows, place, slots)
    for k in range(0, slots, LANES):
        hit = place == lane + k
        of = jnp.sum(jnp.where(hit, (src_at - rows).astype(F32), 0.0), axis=0, keepdims=True)
        out[:, k : k + LANES] = of.astype(i32) + rows
        of = jnp.sum(jnp.where(hit, (at - first).astype(F32), 0.0), axis=0, keepdims=True)
        out[:, slots + k : slots + k + LANES] = of.astype(i32)
    full = jnp.sum(sizes, axis=1, keepdims=True)
    rounds = jnp.sum((lane[:1].astype(F32) * per_round < full).astype(F32), axis=1, keepdims=True)
    for k in range(0, groups, LANES):
        lead = place == (lane + k) * group
        of = jnp.sum(jnp.where(lead, (dst_at - rows).astype(F32), 0.0), axis=0, keepdims=True)
        of = jnp.where(lane[:1] + k == groups - 1, rounds, of + rows)
        out[:, 2 * slots + k : 2 * slots + k + LANES] = of.astype(i32)


def setup_kernel(
    rows, chunk, where, obs, flux, nbr, prior,
    prior_plain, *refs
):
    (obs_row, tile_row, ext_row), plans, refs = refs[:3], refs[3:7], refs[7:]
    (obs_in, flux_in, nbr_in), built, (small_sems, sems) = refs[:3], refs[3:7], refs[7:]
    side, corner, count, first_tile = where[0], where[1], where[2], where[3]
    owned = prior_plain.shape[0]
    begin = side * owned
    rounds = (owned // chunk,)

    def copy(c, first, source, plain, offset):
        to = pl.ds(c * chunk, chunk)
        return pltpu.make_async_copy(source.at[pl.ds(first + c * chunk, chunk)], plain.at[to], sems.at[offset + c])

    def start(first, source, plain, offset):
        def one(c, _):
            copy(c, first, source, plain, offset).start()
            return 0

        return one

    def wait(first, source, plain, offset):
        def one(c, _):
            copy(c, first, source, plain, offset).wait()
            return 0

        return one

    small = ((obs, obs_in), (flux, flux_in), (nbr, nbr_in))
    small = [pltpu.make_async_copy(src, dst, small_sems.at[k]) for k, (src, dst) in enumerate(small)]
    for one in small:
        one.start()
    lax.fori_loop(0, rounds[0], start(begin, prior, prior_plain, 0), 0)
    for one in small:
        one.wait()

    obs_rows, tile_rows, fan = rows
    half = tile_rows // 2
    reach = tile_rows // 4
    quarter = obs_rows // 4
    most = max(obs_rows, tile_rows)
    i32 = jnp.int32
    at = lax.broadcasted_iota(i32, obs_in.shape, 1)
    live = at < count
    block = sum((obs_in[...] >= k * quarter).astype(i32) for k in range(1, 4))
    obs_at = (block ^ corner) * quarter + obs_in[...] - block * quarter
    block = (flux_in[...] >= half).astype(i32)
    tile_at = (block ^ side) * half + flux_in[...] - block * half
    obs_at, tile_at = jnp.where(live, obs_at, 2 * most), jnp.where(live, tile_at, 2 * most)
    obs_row[...], tile_row[...] = obs_at, tile_at
    own, near = tile_at < half, obs_at < quarter
    uses = (
        (tile_at, obs_at - quarter, live & own & ~near),
        (tile_at - half, obs_at - quarter, live & ~own & ~near),
        (tile_at, obs_at, near),
    )
    for plan, (src, dst, use), out in zip(FORWARD_PLANS, uses, built):
        plan_groups(plan, jnp.where(use, src, 0), jnp.where(use, dst, most), 0, most, out)
    ext = nbr_in[...] - first_tile + reach
    ext_row[...] = ext
    built[3][:, : ext.shape[1]] = ext
    built[3][:, ext.shape[1] :] = jnp.zeros((1, LANES), i32) + side
    lists = [
        pltpu.make_async_copy(src, dst, small_sems.at[3 + k])
        for k, (src, dst) in enumerate(zip(built, plans))
    ]
    for one in lists:
        one.start()

    lax.fori_loop(0, rounds[0], wait(begin, prior, prior_plain, 0), 0)
    for one in lists:
        one.wait()


def turn_kernel(chunk, plain, turned):
    def one(c, _):
        for u in range(chunk):
            turned[c * chunk + u] = plain[c * chunk + u].T
        return 0

    lax.fori_loop(0, plain.shape[0] // chunk, one, 0)


def turn_blocks(plain, name):
    vmem = pl.BlockSpec(memory_space=pltpu.VMEM)
    return pl.pallas_call(
        functools.partial(turn_kernel, chunk_of(plain.shape[0], 48)),
        in_specs=[vmem],
        out_specs=vmem,
        out_shape=pltpu.VMEM(plain.shape, HALF),
        compiler_params=pltpu.CompilerParams(vmem_limit_bytes=VMEM_LIMIT),
        cost_estimate=pl.CostEstimate(flops=0, bytes_accessed=2 * plain.size, transcendentals=0),
        name=name,
    )(plain)


def plan_lengths(plans, width, most):
    sizes = (plan_sizes(plan, width, most) for plan in plans)
    return [2 * slots + groups for slots, groups in sizes]


def setup(where, obs, flux, nbr, prior, rows):
    owned = rows[1] // 2 * rows[2]
    chunk = chunk_of(owned, 24)
    smem = pl.BlockSpec(memory_space=pltpu.SMEM)
    vmem = pl.BlockSpec(memory_space=pltpu.VMEM)
    hbm = pl.BlockSpec(memory_space=pl.ANY)
    i32 = jnp.int32
    lengths = plan_lengths(FORWARD_PLANS, obs.shape[1], max(rows[:2])) + [nbr.shape[1] + LANES]
    return pl.pallas_call(
        functools.partial(setup_kernel, rows, chunk),
        in_specs=[smem] + [hbm] * 4,
        out_specs=[vmem] * 4 + [smem] * 4,
        out_shape=[pltpu.VMEM((owned,) + prior.shape[1:], HALF)]
        + [pltpu.VMEM(v.shape, i32) for v in (obs, flux, nbr)]
        + [pltpu.SMEM((1, n), i32) for n in lengths],
        scratch_shapes=[pltpu.VMEM(v.shape, i32) for v in (obs, flux, nbr)]
        + [pltpu.VMEM((1, n), i32) for n in lengths]
        + [
            pltpu.SemaphoreType.DMA((7,)),
            pltpu.SemaphoreType.DMA((owned // chunk,)),
        ],
        compiler_params=pltpu.CompilerParams(vmem_limit_bytes=VMEM_LIMIT),
        name="setup",
    )(where, *(pltpu.with_memory_space_constraint(v, pltpu.HBM) for v in (obs, flux, nbr, prior)))


def late_kernel(rows, nbr, obs_row, tile_row, ext_row, *refs):
    plans, built, sems = refs[:6], refs[6:12], refs[12]
    obs_rows, tile_rows, fan = rows
    half, quarter, most = tile_rows // 2, obs_rows // 4, max(obs_rows, tile_rows)
    side = nbr[0, nbr.shape[1] - 1]
    obs_at, tile_at, ext = obs_row[...], tile_row[...], ext_row[...]
    part = [(obs_at >= k * quarter) & (obs_at < (k + 1) * quarter) for k in range(4)]
    uses = (
        (obs_at, tile_at, part[0]),
        (obs_at - 3 * quarter, tile_at, part[3]),
        (obs_at - 2 * quarter, tile_at, part[2]),
        (obs_at - quarter, tile_at - half, part[1] & (tile_at >= half)),
        (obs_at - quarter, tile_at, part[1] & (tile_at < half)),
    )
    for plan, (src, dst, use), out in zip(ADJOINT_PLANS, uses, built):
        plan_groups(plan, jnp.where(use, src, 0), jnp.where(use, dst, most), 0, most, out)
    at = lax.broadcasted_iota(jnp.int32, ext.shape, 1)
    tile = sum((at >= k * fan).astype(jnp.int32) for k in range(1, tile_rows)) - side * half
    owns = (tile >= 0) & (tile < half)
    src, dst = jnp.where(owns, tile, 0), jnp.where(owns, ext, most)
    plan_groups(PRIOR_PLAN, src, dst, side * (half * fan), most, built[5])
    lists = [pltpu.make_async_copy(a, b, sems.at[k]) for k, (a, b) in enumerate(zip(built, plans))]
    for one in lists:
        one.start()
    for one in lists:
        one.wait()


def late_plans(nbr, obs_row, tile_row, ext_row, rows):
    smem = pl.BlockSpec(memory_space=pltpu.SMEM)
    vmem = pl.BlockSpec(memory_space=pltpu.VMEM)
    most = max(rows[:2])
    lengths = plan_lengths(ADJOINT_PLANS, obs_row.shape[1], most)
    lengths += plan_lengths((PRIOR_PLAN,), ext_row.shape[1], most)
    return pl.pallas_call(
        functools.partial(late_kernel, rows),
        in_specs=[smem] + [vmem] * 3,
        out_specs=[smem] * 6,
        out_shape=[pltpu.SMEM((1, n), jnp.int32) for n in lengths],
        scratch_shapes=[pltpu.VMEM((1, n), jnp.int32) for n in lengths]
        + [pltpu.SemaphoreType.DMA((6,))],
        compiler_params=pltpu.CompilerParams(vmem_limit_bytes=VMEM_LIMIT),
        cost_estimate=pl.CostEstimate(flops=0, bytes_accessed=2**23, transcendentals=0),
        name="late_plans",
    )(nbr, obs_row, tile_row, ext_row)


def grouped_products(plan, sizes, lists, x, blocks, total):
    group, per_round = plan
    slots, groups = sizes

    def one(c, _):
        products = []
        for u in range(per_round):
            first = (c * per_round + u) * group
            rows = [x[lists[0, first + g]] for g in range(group)]
            tiles = [blocks[lists[0, slots + first + g]] for g in range(group)]
            products.append(matmul(jnp.concatenate(rows, axis=1), jnp.concatenate(tiles, axis=0)))
        for u in range(per_round):
            total[lists[0, 2 * slots + c * per_round + u]] += products[u]
        return 0

    lax.fori_loop(0, lists[0, 2 * slots + groups - 1], one, 0)


def jac_kernel(plan, sizes, n_parts, started, n_outs, lists, *refs):
    parts, refs = refs[:n_parts], refs[n_parts:]
    if started:
        begun, refs = refs[0], refs[1:]
    jac, outs, (x, total) = refs[0], refs[1 : 1 + n_outs], refs[1 + n_outs :]
    rows = parts[0].shape[0]
    for k, part in enumerate(parts):
        x[k * rows : (k + 1) * rows] = part[...]
    x[x.shape[0] - 1] = jnp.zeros(x.shape[1:], HALF)
    if started:
        total[: begun.shape[0]] = begun[...]
    else:
        total[...] = jnp.zeros_like(total)
    grouped_products(plan, sizes, lists, x, jac, total)
    rows = outs[0].shape[0]
    for k, out in enumerate(outs):
        out[...] = total[k * rows : (k + 1) * rows].astype(out.dtype)


def jac_pass(plan, lists, parts, begun, jac, rows, out_rows, out_types, name):
    probes, width = parts[0].shape[1:]
    n_outs = len(out_types)
    smem = pl.BlockSpec(memory_space=pltpu.SMEM)
    vmem = pl.BlockSpec(memory_space=pltpu.VMEM)
    operands = (lists, *parts) + (() if begun is None else (begun,)) + (jac,)
    sizes = plan_sizes(plan, jac.shape[0], rows)
    return pl.pallas_call(
        functools.partial(jac_kernel, plan, sizes, len(parts), begun is not None, n_outs),
        in_specs=[smem] + [vmem] * (len(operands) - 1),
        out_specs=[vmem] * n_outs,
        out_shape=[jax.ShapeDtypeStruct((out_rows // n_outs, probes, width), t) for t in out_types],
        scratch_shapes=[
            pltpu.VMEM((rows + 1, probes, width), HALF),
            pltpu.VMEM((rows + 1, probes, width), F32),
        ],
        compiler_params=pltpu.CompilerParams(vmem_limit_bytes=VMEM_LIMIT),
        cost_estimate=pl.CostEstimate(flops=0, bytes_accessed=jac.size, transcendentals=0),
        name=name,
    )(*operands)


def gather_kernel(rows, sizes, nbr, lists, mine, other, prior, ext, to_core, to_far, x, total):
    half = mine.shape[0]
    side = nbr[0, nbr.shape[1] - 1]
    x[:half] = (mine[...].astype(F32) + other[...].astype(F32)).astype(HALF)
    x[rows] = jnp.zeros(x.shape[1:], HALF)
    total[...] = jnp.zeros_like(total)
    grouped_products(PRIOR_PLAN, sizes, lists, x, prior, total)
    ext[...] = total[: 2 * half]
    to_core[...] = total[pl.ds(half * (1 - side), half)].astype(HALF)
    to_far[...] = total[pl.ds(half * side, half)].astype(HALF)


def gather_tiles(nbr, lists, mine, other, prior, rows):
    tiles, probes, width = mine.shape
    smem = pl.BlockSpec(memory_space=pltpu.SMEM)
    vmem = pl.BlockSpec(memory_space=pltpu.VMEM)
    return pl.pallas_call(
        functools.partial(gather_kernel, rows, plan_sizes(PRIOR_PLAN, nbr.shape[1] - LANES, rows)),
        in_specs=[smem, smem, vmem, vmem, vmem],
        out_specs=[vmem] * 3,
        out_shape=[
            jax.ShapeDtypeStruct((2 * tiles, probes, width), F32),
            jax.ShapeDtypeStruct((tiles, probes, width), HALF),
            jax.ShapeDtypeStruct((tiles, probes, width), HALF),
        ],
        scratch_shapes=[
            pltpu.VMEM((rows + 1, probes, width), HALF),
            pltpu.VMEM((rows + 1, probes, width), F32),
        ],
        compiler_params=pltpu.CompilerParams(vmem_limit_bytes=VMEM_LIMIT),
        name="prior_adjoint",
    )(nbr, lists, mine, other, prior)


def spread_kernel(first, fan, nbr, *refs):
    prior, out, field = refs[-3:]
    tiles = out.shape[0]
    chunk = chunk_of(tiles, 24)
    side = nbr[0, nbr.shape[1] - 1]
    if first:
        probes, beyond = refs[:2]
        reach = beyond.shape[0]
        inner = 2 * tiles - reach
        field[pl.ds(reach * (1 - side), inner)] = probes[pl.ds(reach * side, inner)]
        field[pl.ds(inner * side, reach)] = beyond[...]
    else:
        ext, from_core, from_far = refs[:3]
        for begin, update in ((tiles * (1 - side), from_core), (tiles * side, from_far)):
            at = pl.ds(begin, tiles)
            field[at] = (ext[at] + update[...].astype(F32)).astype(HALF)

    def one(c, _):
        for u in range(chunk):
            t = c * chunk + u
            row = [field[nbr[0, (side * tiles + t) * fan + k]] for k in range(fan)]
            tile = prior[pl.ds(t * fan, fan)]
            tile = tile.reshape(fan * tile.shape[1], tile.shape[2])
            out[t] = matmul(jnp.concatenate(row, axis=1), tile).astype(HALF)
        return 0

    lax.fori_loop(0, tiles // chunk, one, 0)


def spread_tiles(nbr, fields, prior):
    ext_tiles, probes, width = fields[0].shape
    tiles = ext_tiles // 2
    smem = pl.BlockSpec(memory_space=pltpu.SMEM)
    vmem = pl.BlockSpec(memory_space=pltpu.VMEM)
    return pl.pallas_call(
        functools.partial(spread_kernel, len(fields) == 2, prior.shape[0] // tiles),
        in_specs=[smem] + [vmem] * len(fields) + [vmem],
        out_specs=vmem,
        out_shape=jax.ShapeDtypeStruct((tiles, probes, width), HALF),
        scratch_shapes=[pltpu.VMEM(fields[0].shape, HALF)],
        compiler_params=pltpu.CompilerParams(vmem_limit_bytes=VMEM_LIMIT),
        name="prior_spread",
    )(nbr, *fields, prior)


def shards(probes, prior_tiles, neighbours, jac, jac_obs, jac_flux, counts, rinv):
    n_obs, n_flux = lax.axis_size("obs"), lax.axis_size("flux")
    tile_count = probes.shape[0]
    half = tile_count // 2
    reach = tile_count // 4
    obs_rows = rinv.shape[0]
    quarter = obs_rows // 4
    blocks = jac[0, 0]
    flux_at = lax.axis_index("flux")
    side = lax.rem(lax.axis_index("obs"), 2)
    corner = lax.rem(flux_at, 4)
    fan = neighbours.shape[1]
    prior = prior_tiles.reshape((tile_count * fan,) + prior_tiles.shape[2:])
    own_rinv = lax.dynamic_slice_in_dim(rinv, corner * quarter, quarter, 0)[:, None, :]
    rows = max(obs_rows, tile_count)
    sizes = (obs_rows, tile_count, fan)

    def swap_core(value):
        return exchange(value, lambda i, j: (i ^ 1, j))

    def swap_far(value):
        def partner(i, j):
            to = j - 1 if i % 2 == 0 else j + 1
            return (i ^ 1, to) if 0 <= to < n_flux else None

        return exchange(value, partner)

    def swap_flux(value, bits):
        return exchange(value, lambda i, j: (i, j ^ bits))

    edge = jnp.where(side == 0, probes[:reach], probes[tile_count - reach :])
    beyond = swap_far(edge)
    where = jnp.stack([side, corner, counts[0, 0], flux_at * tile_count + side * half])
    nbr = neighbours.reshape(1, tile_count * fan)

    where, own_rinv, nbr, prior, blocks = lax.optimization_barrier((where, own_rinv, nbr, prior, blocks))
    jac_plain = blocks
    prior_plain, *index_rows, own_lists, other_lists, near_lists, nbr = setup(
        where, jac_obs[0], jac_flux[0], nbr, prior, sizes
    )
    fields = (probes, beyond)
    for step in range(STEPS):
        spread = spread_tiles(nbr, fields, prior_plain)
        other = swap_core(spread)
        far_rows = obs_rows - quarter
        (begun,) = jac_pass(
            FORWARD_PLANS[0], own_lists, (spread,), None, jac_plain, rows, far_rows, [F32], "forward_own"
        )
        pieces = jac_pass(
            FORWARD_PLANS[1], other_lists, (other,), begun, jac_plain, rows, far_rows, [HALF] * 3, "forward_other"
        )
        (total,) = jac_pass(
            FORWARD_PLANS[2], near_lists, (spread, other), None, jac_plain, rows, quarter, [F32], "forward_near"
        )
        if step == 0:
            pieces, jac_plain = lax.optimization_barrier((pieces, jac_plain))
            jac_turned = turn_blocks(jac_plain, "jac_turn")
        for bits in range(1, 4):
            total = total + swap_flux(pieces[bits - 1], bits).astype(F32)
        if step == 0:
            total, jac_turned, index_rows = lax.optimization_barrier((total, jac_turned, index_rows))
            adjoint_lists = late_plans(nbr, *index_rows, sizes)
        bits = 4
        while bits < n_flux:
            sent = total.astype(HALF)
            total = sent.astype(F32) + swap_flux(sent, bits).astype(F32)
            bits *= 2
        if step == 0:
            total, adjoint_lists = lax.optimization_barrier((total, adjoint_lists))
            prior_lists = adjoint_lists[5]
        weighted = (total * own_rinv).astype(HALF)
        quarters = [weighted] + [swap_flux(weighted, bits) for bits in range(1, 4)]
        begun = None
        for part, at in enumerate((0, 3, 2)):
            types = [F32] * (2 if part == 2 else 1)
            begun = jac_pass(
                ADJOINT_PLANS[part],
                adjoint_lists[part],
                (quarters[at],),
                None if part == 0 else begun[0],
                jac_turned,
                rows,
                tile_count,
                types,
                f"adjoint_quarter{at}",
            )
        mine, theirs = begun
        (theirs,) = jac_pass(
            ADJOINT_PLANS[3], adjoint_lists[3], (quarters[1],), theirs, jac_turned, rows, half, [HALF], "adjoint_other"
        )
        (mine,) = jac_pass(
            ADJOINT_PLANS[4], adjoint_lists[4], (quarters[1],), mine, jac_turned, rows, half, [F32], "adjoint_own"
        )
        mine = (mine + swap_core(theirs).astype(F32)).astype(HALF)
        if step == 0:
            mine, prior_plain = lax.optimization_barrier((mine, prior_plain))
            prior_turned = turn_blocks(prior_plain, "prior_turn")
        bits = 2
        while bits < n_obs:
            other = exchange(mine, lambda i, j, bits=bits: (i ^ bits, j))
            bits *= 2
            if bits < n_obs:
                mine = (mine.astype(F32) + other.astype(F32)).astype(HALF)
        ext, to_core, to_far = gather_tiles(nbr, prior_lists, mine, other, prior_turned, rows)
        if step < STEPS - 1:
            fields = (ext, swap_core(to_core), swap_far(to_far))
    lower = side == 0
    from_core = swap_core(jnp.where(lower, to_core[half - reach :], to_core[:reach])).astype(F32)
    from_far = swap_far(jnp.where(lower, to_far[:reach], to_far[half - reach :])).astype(F32)
    low = jnp.where(lower, from_far, from_core)
    high = jnp.where(lower, from_core, from_far)
    own = (ext[reach : reach + half] + jnp.concatenate([low, high], axis=0)).astype(HALF)
    other = swap_core(own)
    first = jnp.where(side == 0, own, other)
    second = jnp.where(side == 0, other, own)
    return jnp.concatenate([first, second], axis=0)


def solution(mesh):
    placed = (
        P("flux", None, None),
        P("flux", None, None, None),
        P("flux", None),
        P("obs", "flux", None, None, None),
        P("obs", "flux", None),
        P("obs", "flux", None),
        P("obs", "flux"),
        P("obs", None),
    )
    return jax.shard_map(
        shards, mesh=mesh, in_specs=placed, out_specs=P("flux", None, None), check_vma=False
    )
```

```python
import functools
import math

import jax
import jax.numpy as jnp
from jax import lax
from jax.experimental import pallas as pl
from jax.experimental.pallas import tpu as pltpu
from jax.sharding import PartitionSpec as P

STEPS = 4
F32 = jnp.float32
HALF = jnp.bfloat16
VMEM_LIMIT = 8 * 2**20
LANES = 128
FORWARD_PLANS = ((2, 42), (2, 42), (2, 28))
ADJOINT_PLANS = ((2, 32), (2, 32), (2, 32), (2, 18), (2, 18))
PRIOR_PLAN = (2, 56)


def matmul(a, b):
    return lax.dot_general(a, b, (((1,), (0,)), ((), ())), preferred_element_type=F32)


def chunk_of(count, most):
    return max(c for c in range(1, most + 1) if count % c == 0)


def exchange(value, partner):
    n_obs, n_flux = lax.axis_size("obs"), lax.axis_size("flux")
    route = []
    for i in range(n_obs):
        for j in range(n_flux):
            to = partner(i, j)
            if to is not None:
                route.append((i * n_flux + j, to[0] * n_flux + to[1]))
    return lax.ppermute(value, ("obs", "flux"), route)


def plan_sizes(plan, blocks, dst_rows):
    group, per_round = plan
    groups = blocks // group + dst_rows
    groups += -groups % per_round
    slots = groups * group
    return slots + -slots % LANES, groups + 1 + -(groups + 1) % LANES


def columns(row):
    parts = [
        jnp.broadcast_to(row[:, k : k + LANES], (LANES, LANES)).T for k in range(0, row.shape[1], LANES)
    ]
    return jnp.concatenate(parts, axis=0)


def plan_groups(plan, src, dst, first, rows, out):
    group, per_round = plan
    blocks = dst.shape[1]
    slots, groups = plan_sizes(plan, blocks, rows)
    i32 = jnp.int32
    lane = lax.broadcasted_iota(i32, (blocks, LANES), 1)
    at = lax.broadcasted_iota(i32, (blocks, LANES), 0)
    src_at, dst_at = columns(src), columns(dst)
    rank = jnp.zeros((blocks, LANES), F32)
    for k in range(0, blocks, LANES):
        same = (dst_at == dst[:, k : k + LANES]) & (lane + k < at)
        rank += same.astype(F32)
    rank = jnp.sum(rank, axis=1, keepdims=True)
    fills = jnp.sum((dst_at == lane).astype(F32), axis=0, keepdims=True)
    sizes = jnp.where(lane[:1] < rows, jnp.floor((fills + (group - 1)) * (1.0 / group)), 0.0)
    begin = jnp.sum(jnp.where(lane < dst_at, sizes, 0.0), axis=1, keepdims=True)
    place = (begin * group + rank).astype(i32)
    place = jnp.where(dst_at < rows, place, slots)
    for k in range(0, slots, LANES):
        hit = place == lane + k
        of = jnp.sum(jnp.where(hit, (src_at - rows).astype(F32), 0.0), axis=0, keepdims=True)
        out[:, k : k + LANES] = of.astype(i32) + rows
        of = jnp.sum(jnp.where(hit, (at - first).astype(F32), 0.0), axis=0, keepdims=True)
        out[:, slots + k : slots + k + LANES] = of.astype(i32)
    full = jnp.sum(sizes, axis=1, keepdims=True)
    rounds = jnp.sum((lane[:1].astype(F32) * per_round < full).astype(F32), axis=1, keepdims=True)
    for k in range(0, groups, LANES):
        lead = place == (lane + k) * group
        of = jnp.sum(jnp.where(lead, (dst_at - rows).astype(F32), 0.0), axis=0, keepdims=True)
        of = jnp.where(lane[:1] + k == groups - 1, rounds, of + rows)
        out[:, 2 * slots + k : 2 * slots + k + LANES] = of.astype(i32)


def setup_kernel(
    rows, chunk, where, obs, flux, nbr, prior,
    prior_plain, *refs
):
    (obs_row, tile_row, ext_row), plans, refs = refs[:3], refs[3:7], refs[7:]
    (obs_in, flux_in, nbr_in), built, (small_sems, sems) = refs[:3], refs[3:7], refs[7:]
    side, corner, count, first_tile = where[0], where[1], where[2], where[3]
    owned = prior_plain.shape[0]
    begin = side * owned
    rounds = (owned // chunk,)

    def copy(c, first, source, plain, offset):
        to = pl.ds(c * chunk, chunk)
        return pltpu.make_async_copy(source.at[pl.ds(first + c * chunk, chunk)], plain.at[to], sems.at[offset + c])

    def start(first, source, plain, offset):
        def one(c, _):
            copy(c, first, source, plain, offset).start()
            return 0

        return one

    def wait(first, source, plain, offset):
        def one(c, _):
            copy(c, first, source, plain, offset).wait()
            return 0

        return one

    small = ((obs, obs_in), (flux, flux_in), (nbr, nbr_in))
    small = [pltpu.make_async_copy(src, dst, small_sems.at[k]) for k, (src, dst) in enumerate(small)]
    for one in small:
        one.start()
    lax.fori_loop(0, rounds[0], start(begin, prior, prior_plain, 0), 0)
    for one in small:
        one.wait()

    obs_rows, tile_rows, fan = rows
    half = tile_rows // 2
    reach = tile_rows // 4
    quarter = obs_rows // 4
    most = max(obs_rows, tile_rows)
    i32 = jnp.int32
    at = lax.broadcasted_iota(i32, obs_in.shape, 1)
    live = at < count
    block = sum((obs_in[...] >= k * quarter).astype(i32) for k in range(1, 4))
    obs_at = (block ^ corner) * quarter + obs_in[...] - block * quarter
    block = (flux_in[...] >= half).astype(i32)
    tile_at = (block ^ side) * half + flux_in[...] - block * half
    obs_at, tile_at = jnp.where(live, obs_at, 2 * most), jnp.where(live, tile_at, 2 * most)
    obs_row[...], tile_row[...] = obs_at, tile_at
    own, near = tile_at < half, obs_at < quarter
    uses = (
        (tile_at, obs_at - quarter, live & own & ~near),
        (tile_at - half, obs_at - quarter, live & ~own & ~near),
        (tile_at, obs_at, near),
    )
    for plan, (src, dst, use), out in zip(FORWARD_PLANS, uses, built):
        plan_groups(plan, jnp.where(use, src, 0), jnp.where(use, dst, most), 0, most, out)
    count = tile_rows * fan
    entry = lax.broadcasted_iota(i32, (fan, count), 1) - lax.broadcasted_iota(i32, (fan, count), 0)
    local = nbr_in[...] - first_tile + reach
    spread = sum(
        jnp.where(entry == t * fan, local[:, t : t + 1], 0).astype(F32) for t in range(tile_rows)
    )
    ext = jnp.sum(spread, axis=0, keepdims=True).astype(i32)
    ext_row[...] = ext
    built[3][:, : ext.shape[1]] = ext
    built[3][:, ext.shape[1] :] = jnp.zeros((1, LANES), i32) + side
    lists = [
        pltpu.make_async_copy(src, dst, small_sems.at[3 + k])
        for k, (src, dst) in enumerate(zip(built, plans))
    ]
    for one in lists:
        one.start()

    lax.fori_loop(0, rounds[0], wait(begin, prior, prior_plain, 0), 0)
    for one in lists:
        one.wait()


def turn_kernel(chunk, plain, turned):
    def one(c, _):
        for u in range(chunk):
            turned[c * chunk + u] = plain[c * chunk + u].T
        return 0

    lax.fori_loop(0, plain.shape[0] // chunk, one, 0)


def turn_blocks(plain, name):
    vmem = pl.BlockSpec(memory_space=pltpu.VMEM)
    return pl.pallas_call(
        functools.partial(turn_kernel, chunk_of(plain.shape[0], 48)),
        in_specs=[vmem],
        out_specs=vmem,
        out_shape=pltpu.VMEM(plain.shape, HALF),
        compiler_params=pltpu.CompilerParams(vmem_limit_bytes=VMEM_LIMIT),
        cost_estimate=pl.CostEstimate(flops=0, bytes_accessed=2 * plain.size, transcendentals=0),
        name=name,
    )(plain)


def plan_lengths(plans, width, most):
    sizes = (plan_sizes(plan, width, most) for plan in plans)
    return [2 * slots + groups for slots, groups in sizes]


def setup(where, obs, flux, nbr, prior, rows):
    owned = rows[1] // 2 * rows[2]
    chunk = chunk_of(owned, 24)
    smem = pl.BlockSpec(memory_space=pltpu.SMEM)
    vmem = pl.BlockSpec(memory_space=pltpu.VMEM)
    hbm = pl.BlockSpec(memory_space=pl.ANY)
    i32 = jnp.int32
    lengths = plan_lengths(FORWARD_PLANS, obs.shape[1], max(rows[:2])) + [nbr.size + LANES]
    return pl.pallas_call(
        functools.partial(setup_kernel, rows, chunk),
        in_specs=[smem] + [hbm] * 4,
        out_specs=[vmem] * 4 + [smem] * 4,
        out_shape=[pltpu.VMEM((owned,) + prior.shape[1:], HALF)]
        + [pltpu.VMEM(s, i32) for s in (obs.shape, flux.shape, (1, nbr.size))]
        + [pltpu.SMEM((1, n), i32) for n in lengths],
        scratch_shapes=[pltpu.VMEM(v.shape, i32) for v in (obs, flux, nbr)]
        + [pltpu.VMEM((1, n), i32) for n in lengths]
        + [
            pltpu.SemaphoreType.DMA((7,)),
            pltpu.SemaphoreType.DMA((owned // chunk,)),
        ],
        compiler_params=pltpu.CompilerParams(vmem_limit_bytes=VMEM_LIMIT),
        name="setup",
    )(where, *(pltpu.with_memory_space_constraint(v, pltpu.HBM) for v in (obs, flux, nbr, prior)))


def late_kernel(rows, nbr, obs_row, tile_row, ext_row, *refs):
    plans, built, sems = refs[:6], refs[6:12], refs[12]
    obs_rows, tile_rows, fan = rows
    half, quarter, most = tile_rows // 2, obs_rows // 4, max(obs_rows, tile_rows)
    side = nbr[0, nbr.shape[1] - 1]
    obs_at, tile_at, ext = obs_row[...], tile_row[...], ext_row[...]
    part = [(obs_at >= k * quarter) & (obs_at < (k + 1) * quarter) for k in range(4)]
    uses = (
        (obs_at, tile_at, part[0]),
        (obs_at - 3 * quarter, tile_at, part[3]),
        (obs_at - 2 * quarter, tile_at, part[2]),
        (obs_at - quarter, tile_at - half, part[1] & (tile_at >= half)),
        (obs_at - quarter, tile_at, part[1] & (tile_at < half)),
    )
    for plan, (src, dst, use), out in zip(ADJOINT_PLANS, uses, built):
        plan_groups(plan, jnp.where(use, src, 0), jnp.where(use, dst, most), 0, most, out)
    at = lax.broadcasted_iota(jnp.int32, ext.shape, 1)
    tile = sum((at >= k * fan).astype(jnp.int32) for k in range(1, tile_rows)) - side * half
    owns = (tile >= 0) & (tile < half)
    src, dst = jnp.where(owns, tile, 0), jnp.where(owns, ext, most)
    plan_groups(PRIOR_PLAN, src, dst, side * (half * fan), most, built[5])
    lists = [pltpu.make_async_copy(a, b, sems.at[k]) for k, (a, b) in enumerate(zip(built, plans))]
    for one in lists:
        one.start()
    for one in lists:
        one.wait()


def late_plans(nbr, obs_row, tile_row, ext_row, rows):
    smem = pl.BlockSpec(memory_space=pltpu.SMEM)
    vmem = pl.BlockSpec(memory_space=pltpu.VMEM)
    most = max(rows[:2])
    lengths = plan_lengths(ADJOINT_PLANS, obs_row.shape[1], most)
    lengths += plan_lengths((PRIOR_PLAN,), ext_row.shape[1], most)
    return pl.pallas_call(
        functools.partial(late_kernel, rows),
        in_specs=[smem] + [vmem] * 3,
        out_specs=[smem] * 6,
        out_shape=[pltpu.SMEM((1, n), jnp.int32) for n in lengths],
        scratch_shapes=[pltpu.VMEM((1, n), jnp.int32) for n in lengths]
        + [pltpu.SemaphoreType.DMA((6,))],
        compiler_params=pltpu.CompilerParams(vmem_limit_bytes=VMEM_LIMIT),
        cost_estimate=pl.CostEstimate(flops=0, bytes_accessed=2**23, transcendentals=0),
        name="late_plans",
    )(nbr, obs_row, tile_row, ext_row)


def grouped_products(plan, sizes, lists, x, blocks, total):
    group, per_round = plan
    slots, groups = sizes

    def one(c, _):
        products = []
        for u in range(per_round):
            first = (c * per_round + u) * group
            rows = [x[lists[0, first + g]] for g in range(group)]
            tiles = [blocks[lists[0, slots + first + g]] for g in range(group)]
            products.append(matmul(jnp.concatenate(rows, axis=1), jnp.concatenate(tiles, axis=0)))
        for u in range(per_round):
            total[lists[0, 2 * slots + c * per_round + u]] += products[u]
        return 0

    lax.fori_loop(0, lists[0, 2 * slots + groups - 1], one, 0)


def jac_kernel(plan, sizes, n_parts, started, n_outs, lists, *refs):
    parts, refs = refs[:n_parts], refs[n_parts:]
    if started:
        begun, refs = refs[0], refs[1:]
    jac, outs, (x, total) = refs[0], refs[1 : 1 + n_outs], refs[1 + n_outs :]
    rows = parts[0].shape[0]
    for k, part in enumerate(parts):
        x[k * rows : (k + 1) * rows] = part[...]
    x[x.shape[0] - 1] = jnp.zeros(x.shape[1:], HALF)
    if started:
        total[: begun.shape[0]] = begun[...]
    else:
        total[...] = jnp.zeros_like(total)
    grouped_products(plan, sizes, lists, x, jac, total)
    rows = outs[0].shape[0]
    for k, out in enumerate(outs):
        out[...] = total[k * rows : (k + 1) * rows].astype(out.dtype)


def jac_pass(plan, lists, parts, begun, jac, rows, out_rows, out_types, name):
    probes, width = parts[0].shape[1:]
    n_outs = len(out_types)
    smem = pl.BlockSpec(memory_space=pltpu.SMEM)
    vmem = pl.BlockSpec(memory_space=pltpu.VMEM)
    operands = (lists, *parts) + (() if begun is None else (begun,)) + (jac,)
    sizes = plan_sizes(plan, jac.shape[0], rows)
    return pl.pallas_call(
        functools.partial(jac_kernel, plan, sizes, len(parts), begun is not None, n_outs),
        in_specs=[smem] + [vmem] * (len(operands) - 1),
        out_specs=[vmem] * n_outs,
        out_shape=[jax.ShapeDtypeStruct((out_rows // n_outs, probes, width), t) for t in out_types],
        scratch_shapes=[
            pltpu.VMEM((rows + 1, probes, width), HALF),
            pltpu.VMEM((rows + 1, probes, width), F32),
        ],
        compiler_params=pltpu.CompilerParams(vmem_limit_bytes=VMEM_LIMIT),
        cost_estimate=pl.CostEstimate(flops=0, bytes_accessed=jac.size, transcendentals=0),
        name=name,
    )(*operands)


def gather_kernel(rows, sizes, nbr, lists, mine, other, prior, ext, to_core, to_far, x, total):
    half = mine.shape[0]
    side = nbr[0, nbr.shape[1] - 1]
    x[:half] = (mine[...].astype(F32) + other[...].astype(F32)).astype(HALF)
    x[rows] = jnp.zeros(x.shape[1:], HALF)
    total[...] = jnp.zeros_like(total)
    grouped_products(PRIOR_PLAN, sizes, lists, x, prior, total)
    ext[...] = total[: 2 * half]
    to_core[...] = total[pl.ds(half * (1 - side), half)].astype(HALF)
    to_far[...] = total[pl.ds(half * side, half)].astype(HALF)


def gather_tiles(nbr, lists, mine, other, prior, rows):
    tiles, probes, width = mine.shape
    smem = pl.BlockSpec(memory_space=pltpu.SMEM)
    vmem = pl.BlockSpec(memory_space=pltpu.VMEM)
    return pl.pallas_call(
        functools.partial(gather_kernel, rows, plan_sizes(PRIOR_PLAN, nbr.shape[1] - LANES, rows)),
        in_specs=[smem, smem, vmem, vmem, vmem],
        out_specs=[vmem] * 3,
        out_shape=[
            jax.ShapeDtypeStruct((2 * tiles, probes, width), F32),
            jax.ShapeDtypeStruct((tiles, probes, width), HALF),
            jax.ShapeDtypeStruct((tiles, probes, width), HALF),
        ],
        scratch_shapes=[
            pltpu.VMEM((rows + 1, probes, width), HALF),
            pltpu.VMEM((rows + 1, probes, width), F32),
        ],
        compiler_params=pltpu.CompilerParams(vmem_limit_bytes=VMEM_LIMIT),
        name="prior_adjoint",
    )(nbr, lists, mine, other, prior)


def spread_kernel(first, fan, nbr, *refs):
    prior, out, field = refs[-3:]
    tiles = out.shape[0]
    chunk = chunk_of(tiles, 24)
    side = nbr[0, nbr.shape[1] - 1]
    if first:
        probes, beyond = refs[:2]
        reach = beyond.shape[0]
        inner = 2 * tiles - reach
        field[pl.ds(reach * (1 - side), inner)] = probes[pl.ds(reach * side, inner)]
        field[pl.ds(inner * side, reach)] = beyond[...]
    else:
        ext, from_core, from_far = refs[:3]
        for begin, update in ((tiles * (1 - side), from_core), (tiles * side, from_far)):
            at = pl.ds(begin, tiles)
            field[at] = (ext[at] + update[...].astype(F32)).astype(HALF)

    def one(c, _):
        for u in range(chunk):
            t = c * chunk + u
            row = [field[nbr[0, (side * tiles + t) * fan + k]] for k in range(fan)]
            tile = prior[pl.ds(t * fan, fan)]
            tile = tile.reshape(fan * tile.shape[1], tile.shape[2])
            out[t] = matmul(jnp.concatenate(row, axis=1), tile).astype(HALF)
        return 0

    lax.fori_loop(0, tiles // chunk, one, 0)


def spread_tiles(nbr, fields, prior):
    ext_tiles, probes, width = fields[0].shape
    tiles = ext_tiles // 2
    smem = pl.BlockSpec(memory_space=pltpu.SMEM)
    vmem = pl.BlockSpec(memory_space=pltpu.VMEM)
    return pl.pallas_call(
        functools.partial(spread_kernel, len(fields) == 2, prior.shape[0] // tiles),
        in_specs=[smem] + [vmem] * len(fields) + [vmem],
        out_specs=vmem,
        out_shape=jax.ShapeDtypeStruct((tiles, probes, width), HALF),
        scratch_shapes=[pltpu.VMEM(fields[0].shape, HALF)],
        compiler_params=pltpu.CompilerParams(vmem_limit_bytes=VMEM_LIMIT),
        name="prior_spread",
    )(nbr, *fields, prior)


def shards(probes, prior_tiles, neighbours, jac, jac_obs, jac_flux, counts, rinv):
    n_obs, n_flux = lax.axis_size("obs"), lax.axis_size("flux")
    tile_count = probes.shape[0]
    half = tile_count // 2
    reach = tile_count // 4
    obs_rows = rinv.shape[0]
    quarter = obs_rows // 4
    blocks = jac[0, 0]
    flux_at = lax.axis_index("flux")
    side = lax.rem(lax.axis_index("obs"), 2)
    corner = lax.rem(flux_at, 4)
    fan = neighbours.shape[1]
    prior = prior_tiles.reshape((tile_count * fan,) + prior_tiles.shape[2:])
    own_rinv = lax.dynamic_slice_in_dim(rinv, corner * quarter, quarter, 0)[:, None, :]
    rows = max(obs_rows, tile_count)
    sizes = (obs_rows, tile_count, fan)

    def swap_core(value):
        return exchange(value, lambda i, j: (i ^ 1, j))

    def swap_far(value):
        def partner(i, j):
            to = j - 1 if i % 2 == 0 else j + 1
            return (i ^ 1, to) if 0 <= to < n_flux else None

        return exchange(value, partner)

    def swap_flux(value, bits):
        return exchange(value, lambda i, j: (i, j ^ bits))

    edge = jnp.where(side == 0, probes[:reach], probes[tile_count - reach :])
    beyond = swap_far(edge)
    where = jnp.stack([side, corner, counts[0, 0], flux_at * tile_count + side * half])

    where, own_rinv, prior, blocks = lax.optimization_barrier((where, own_rinv, prior, blocks))
    jac_plain = blocks
    prior_plain, *index_rows, own_lists, other_lists, near_lists, nbr = setup(
        where, jac_obs[0], jac_flux[0], neighbours.T, prior, sizes
    )
    fields = (probes, beyond)
    for step in range(STEPS):
        spread = spread_tiles(nbr, fields, prior_plain)
        other = swap_core(spread)
        far_rows = obs_rows - quarter
        (begun,) = jac_pass(
            FORWARD_PLANS[0], own_lists, (spread,), None, jac_plain, rows, far_rows, [F32], "forward_own"
        )
        pieces = jac_pass(
            FORWARD_PLANS[1], other_lists, (other,), begun, jac_plain, rows, far_rows, [HALF] * 3, "forward_other"
        )
        (total,) = jac_pass(
            FORWARD_PLANS[2], near_lists, (spread, other), None, jac_plain, rows, quarter, [F32], "forward_near"
        )
        if step == 0:
            pieces, jac_plain = lax.optimization_barrier((pieces, jac_plain))
            jac_turned = turn_blocks(jac_plain, "jac_turn")
        for bits in (3, 2, 1):
            total = total + swap_flux(pieces[bits - 1], bits).astype(F32)
        if step == 0:
            total, jac_turned, index_rows = lax.optimization_barrier((total, jac_turned, index_rows))
            adjoint_lists = late_plans(nbr, *index_rows, sizes)
        bits = 4
        while bits < n_flux:
            sent = total.astype(HALF)
            total = sent.astype(F32) + swap_flux(sent, bits).astype(F32)
            bits *= 2
        if step == 0:
            total, adjoint_lists = lax.optimization_barrier((total, adjoint_lists))
            prior_lists = adjoint_lists[5]
        weighted = (total * own_rinv).astype(HALF)
        quarters = [weighted] + [swap_flux(weighted, bits) for bits in range(1, 4)]
        begun = None
        for part, at in enumerate((0, 3, 2)):
            types = [F32] * (2 if part == 2 else 1)
            begun = jac_pass(
                ADJOINT_PLANS[part],
                adjoint_lists[part],
                (quarters[at],),
                None if part == 0 else begun[0],
                jac_turned,
                rows,
                tile_count,
                types,
                f"adjoint_quarter{at}",
            )
        mine, theirs = begun
        (theirs,) = jac_pass(
            ADJOINT_PLANS[3], adjoint_lists[3], (quarters[1],), theirs, jac_turned, rows, half, [HALF], "adjoint_other"
        )
        (mine,) = jac_pass(
            ADJOINT_PLANS[4], adjoint_lists[4], (quarters[1],), mine, jac_turned, rows, half, [F32], "adjoint_own"
        )
        mine = (mine + swap_core(theirs).astype(F32)).astype(HALF)
        if step == 0:
            mine, prior_plain = lax.optimization_barrier((mine, prior_plain))
            prior_turned = turn_blocks(prior_plain, "prior_turn")
        bits = 2
        while bits < n_obs:
            other = exchange(mine, lambda i, j, bits=bits: (i ^ bits, j))
            bits *= 2
            if bits < n_obs:
                mine = (mine.astype(F32) + other.astype(F32)).astype(HALF)
        ext, to_core, to_far = gather_tiles(nbr, prior_lists, mine, other, prior_turned, rows)
        if step < STEPS - 1:
            from_far = swap_far(to_far)
            fields = (ext, swap_core(to_core), from_far)
    lower = side == 0
    from_core = swap_core(jnp.where(lower, to_core[half - reach :], to_core[:reach])).astype(F32)
    from_far = swap_far(jnp.where(lower, to_far[:reach], to_far[half - reach :])).astype(F32)
    low = jnp.where(lower, from_far, from_core)
    high = jnp.where(lower, from_core, from_far)
    own = (ext[reach : reach + half] + jnp.concatenate([low, high], axis=0)).astype(HALF)
    other = swap_core(own)
    first = jnp.where(side == 0, own, other)
    second = jnp.where(side == 0, other, own)
    return jnp.concatenate([first, second], axis=0)


def solution(mesh):
    placed = (
        P("flux", None, None),
        P("flux", None, None, None),
        P("flux", None),
        P("obs", "flux", None, None, None),
        P("obs", "flux", None),
        P("obs", "flux", None),
        P("obs", "flux"),
        P("obs", None),
    )
    return jax.shard_map(
        shards, mesh=mesh, in_specs=placed, out_specs=P("flux", None, None), check_vma=False
    )
```

```python
import functools
import math

import jax
import jax.numpy as jnp
from jax import lax
from jax.experimental import pallas as pl
from jax.experimental.pallas import tpu as pltpu
from jax.sharding import PartitionSpec as P

STEPS = 4
F32 = jnp.float32
HALF = jnp.bfloat16
VMEM_LIMIT = 8 * 2**20
LANES = 128
FORWARD_PLANS = ((2, 45), (2, 45), (2, 29))
ADJOINT_PLANS = ((2, 35), (2, 35), (2, 35), (2, 19), (2, 19))
PRIOR_PLAN = (2, 56)


def matmul(a, b):
    return lax.dot_general(a, b, (((1,), (0,)), ((), ())), preferred_element_type=F32)


def chunk_of(count, most):
    return max(c for c in range(1, most + 1) if count % c == 0)


def exchange(value, partner):
    n_obs, n_flux = lax.axis_size("obs"), lax.axis_size("flux")
    route = []
    for i in range(n_obs):
        for j in range(n_flux):
            to = partner(i, j)
            if to is not None:
                route.append((i * n_flux + j, to[0] * n_flux + to[1]))
    return lax.ppermute(value, ("obs", "flux"), route)


def plan_sizes(plan, blocks, dst_rows):
    group, per_round = plan
    groups = blocks // group + dst_rows
    groups += -groups % per_round
    slots = groups * group
    return slots + -slots % LANES, groups + 1 + -(groups + 1) % LANES


def columns(row):
    parts = [
        jnp.broadcast_to(row[:, k : k + LANES], (LANES, LANES)).T for k in range(0, row.shape[1], LANES)
    ]
    return jnp.concatenate(parts, axis=0)


def plan_groups(plan, src, dst, first, rows, out):
    group, per_round = plan
    blocks = dst.shape[1]
    slots, groups = plan_sizes(plan, blocks, rows)
    i32 = jnp.int32
    lane = lax.broadcasted_iota(i32, (blocks, LANES), 1)
    at = lax.broadcasted_iota(i32, (blocks, LANES), 0)
    src_at, dst_at = columns(src), columns(dst)
    rank = jnp.zeros((blocks, LANES), F32)
    for k in range(0, blocks, LANES):
        same = (dst_at == dst[:, k : k + LANES]) & (lane + k < at)
        rank += same.astype(F32)
    rank = jnp.sum(rank, axis=1, keepdims=True)
    fills = jnp.sum((dst_at == lane).astype(F32), axis=0, keepdims=True)
    sizes = jnp.where(lane[:1] < rows, jnp.floor((fills + (group - 1)) * (1.0 / group)), 0.0)
    begin = jnp.sum(jnp.where(lane < dst_at, sizes, 0.0), axis=1, keepdims=True)
    place = (begin * group + rank).astype(i32)
    place = jnp.where(dst_at < rows, place, slots)
    for k in range(0, slots, LANES):
        hit = place == lane + k
        of = jnp.sum(jnp.where(hit, (src_at - rows).astype(F32), 0.0), axis=0, keepdims=True)
        out[:, k : k + LANES] = of.astype(i32) + rows
        of = jnp.sum(jnp.where(hit, (at - first).astype(F32), 0.0), axis=0, keepdims=True)
        out[:, slots + k : slots + k + LANES] = of.astype(i32)
    full = jnp.sum(sizes, axis=1, keepdims=True)
    rounds = jnp.sum((lane[:1].astype(F32) * per_round < full).astype(F32), axis=1, keepdims=True)
    for k in range(0, groups, LANES):
        lead = place == (lane + k) * group
        of = jnp.sum(jnp.where(lead, (dst_at - rows).astype(F32), 0.0), axis=0, keepdims=True)
        of = jnp.where(lane[:1] + k == groups - 1, rounds, of + rows)
        out[:, 2 * slots + k : 2 * slots + k + LANES] = of.astype(i32)


def setup_kernel(
    rows, chunk, where, obs, flux, nbr, prior,
    prior_plain, *refs
):
    (obs_row, tile_row, ext_row), plans, refs = refs[:3], refs[3:7], refs[7:]
    (obs_in, flux_in, nbr_in), built, (small_sems, sems) = refs[:3], refs[3:7], refs[7:]
    side, corner, count, first_tile = where[0], where[1], where[2], where[3]
    owned = prior_plain.shape[0]
    begin = side * owned
    rounds = (owned // chunk,)

    def copy(c, first, source, plain, offset):
        to = pl.ds(c * chunk, chunk)
        return pltpu.make_async_copy(source.at[pl.ds(first + c * chunk, chunk)], plain.at[to], sems.at[offset + c])

    def start(first, source, plain, offset):
        def one(c, _):
            copy(c, first, source, plain, offset).start()
            return 0

        return one

    def wait(first, source, plain, offset):
        def one(c, _):
            copy(c, first, source, plain, offset).wait()
            return 0

        return one

    small = ((obs, obs_in), (flux, flux_in), (nbr, nbr_in))
    small = [pltpu.make_async_copy(src, dst, small_sems.at[k]) for k, (src, dst) in enumerate(small)]
    for one in small:
        one.start()
    lax.fori_loop(0, rounds[0], start(begin, prior, prior_plain, 0), 0)
    for one in small:
        one.wait()

    obs_rows, tile_rows, fan = rows
    half = tile_rows // 2
    reach = tile_rows // 4
    quarter = obs_rows // 4
    most = max(obs_rows, tile_rows)
    i32 = jnp.int32
    at = lax.broadcasted_iota(i32, obs_in.shape, 1)
    live = at < count
    block = sum((obs_in[...] >= k * quarter).astype(i32) for k in range(1, 4))
    obs_at = (block ^ corner) * quarter + obs_in[...] - block * quarter
    block = (flux_in[...] >= half).astype(i32)
    tile_at = (block ^ side) * half + flux_in[...] - block * half
    obs_at, tile_at = jnp.where(live, obs_at, 2 * most), jnp.where(live, tile_at, 2 * most)
    obs_row[...], tile_row[...] = obs_at, tile_at
    own, near = tile_at < half, obs_at < quarter
    uses = (
        (tile_at, obs_at - quarter, live & own & ~near),
        (tile_at - half, obs_at - quarter, live & ~own & ~near),
        (tile_at, obs_at, near),
    )
    for plan, (src, dst, use), out in zip(FORWARD_PLANS, uses, built):
        plan_groups(plan, jnp.where(use, src, 0), jnp.where(use, dst, most), 0, most, out)
    count = tile_rows * fan
    entry = lax.broadcasted_iota(i32, (fan, count), 1) - lax.broadcasted_iota(i32, (fan, count), 0)
    local = nbr_in[...] - first_tile + reach
    spread = sum(
        jnp.where(entry == t * fan, local[:, t : t + 1], 0).astype(F32) for t in range(tile_rows)
    )
    ext = jnp.sum(spread, axis=0, keepdims=True).astype(i32)
    ext_row[...] = ext
    built[3][:, : ext.shape[1]] = ext
    built[3][:, ext.shape[1] :] = jnp.zeros((1, LANES), i32) + side
    lists = [
        pltpu.make_async_copy(src, dst, small_sems.at[3 + k])
        for k, (src, dst) in enumerate(zip(built, plans))
    ]
    for one in lists:
        one.start()

    lax.fori_loop(0, rounds[0], wait(begin, prior, prior_plain, 0), 0)
    for one in lists:
        one.wait()


def turn_kernel(chunk, plain, turned):
    def one(c, _):
        for u in range(chunk):
            turned[c * chunk + u] = plain[c * chunk + u].T
        return 0

    lax.fori_loop(0, plain.shape[0] // chunk, one, 0)


def turn_blocks(plain, name):
    vmem = pl.BlockSpec(memory_space=pltpu.VMEM)
    return pl.pallas_call(
        functools.partial(turn_kernel, chunk_of(plain.shape[0], 48)),
        in_specs=[vmem],
        out_specs=vmem,
        out_shape=pltpu.VMEM(plain.shape, HALF),
        compiler_params=pltpu.CompilerParams(vmem_limit_bytes=VMEM_LIMIT),
        cost_estimate=pl.CostEstimate(flops=0, bytes_accessed=2 * plain.size, transcendentals=0),
        name=name,
    )(plain)


def plan_lengths(plans, width, most):
    sizes = (plan_sizes(plan, width, most) for plan in plans)
    return [2 * slots + groups for slots, groups in sizes]


def setup(where, obs, flux, nbr, prior, rows):
    owned = rows[1] // 2 * rows[2]
    chunk = chunk_of(owned, 24)
    smem = pl.BlockSpec(memory_space=pltpu.SMEM)
    vmem = pl.BlockSpec(memory_space=pltpu.VMEM)
    hbm = pl.BlockSpec(memory_space=pl.ANY)
    i32 = jnp.int32
    lengths = plan_lengths(FORWARD_PLANS, obs.shape[1], max(rows[:2])) + [nbr.size + LANES]
    return pl.pallas_call(
        functools.partial(setup_kernel, rows, chunk),
        in_specs=[smem] + [hbm] * 4,
        out_specs=[vmem] * 4 + [smem] * 4,
        out_shape=[pltpu.VMEM((owned,) + prior.shape[1:], HALF)]
        + [pltpu.VMEM(s, i32) for s in (obs.shape, flux.shape, (1, nbr.size))]
        + [pltpu.SMEM((1, n), i32) for n in lengths],
        scratch_shapes=[pltpu.VMEM(v.shape, i32) for v in (obs, flux, nbr)]
        + [pltpu.VMEM((1, n), i32) for n in lengths]
        + [
            pltpu.SemaphoreType.DMA((7,)),
            pltpu.SemaphoreType.DMA((owned // chunk,)),
        ],
        compiler_params=pltpu.CompilerParams(vmem_limit_bytes=VMEM_LIMIT),
        name="setup",
    )(where, *(pltpu.with_memory_space_constraint(v, pltpu.HBM) for v in (obs, flux, nbr, prior)))


def late_kernel(rows, nbr, obs_row, tile_row, ext_row, *refs):
    plans, built, sems = refs[:6], refs[6:12], refs[12]
    obs_rows, tile_rows, fan = rows
    half, quarter, most = tile_rows // 2, obs_rows // 4, max(obs_rows, tile_rows)
    side = nbr[0, nbr.shape[1] - 1]
    obs_at, tile_at, ext = obs_row[...], tile_row[...], ext_row[...]
    part = [(obs_at >= k * quarter) & (obs_at < (k + 1) * quarter) for k in range(4)]
    uses = (
        (obs_at, tile_at, part[0]),
        (obs_at - 3 * quarter, tile_at, part[3]),
        (obs_at - 2 * quarter, tile_at, part[2]),
        (obs_at - quarter, tile_at - half, part[1] & (tile_at >= half)),
        (obs_at - quarter, tile_at, part[1] & (tile_at < half)),
    )
    for plan, (src, dst, use), out in zip(ADJOINT_PLANS, uses, built):
        plan_groups(plan, jnp.where(use, src, 0), jnp.where(use, dst, most), 0, most, out)
    at = lax.broadcasted_iota(jnp.int32, ext.shape, 1)
    tile = sum((at >= k * fan).astype(jnp.int32) for k in range(1, tile_rows)) - side * half
    owns = (tile >= 0) & (tile < half)
    src, dst = jnp.where(owns, tile, 0), jnp.where(owns, ext, most)
    plan_groups(PRIOR_PLAN, src, dst, side * (half * fan), most, built[5])
    lists = [pltpu.make_async_copy(a, b, sems.at[k]) for k, (a, b) in enumerate(zip(built, plans))]
    for one in lists:
        one.start()
    for one in lists:
        one.wait()


def late_plans(nbr, obs_row, tile_row, ext_row, rows):
    smem = pl.BlockSpec(memory_space=pltpu.SMEM)
    vmem = pl.BlockSpec(memory_space=pltpu.VMEM)
    most = max(rows[:2])
    lengths = plan_lengths(ADJOINT_PLANS, obs_row.shape[1], most)
    lengths += plan_lengths((PRIOR_PLAN,), ext_row.shape[1], most)
    return pl.pallas_call(
        functools.partial(late_kernel, rows),
        in_specs=[smem] + [vmem] * 3,
        out_specs=[smem] * 6,
        out_shape=[pltpu.SMEM((1, n), jnp.int32) for n in lengths],
        scratch_shapes=[pltpu.VMEM((1, n), jnp.int32) for n in lengths]
        + [pltpu.SemaphoreType.DMA((6,))],
        compiler_params=pltpu.CompilerParams(vmem_limit_bytes=VMEM_LIMIT),
        cost_estimate=pl.CostEstimate(flops=0, bytes_accessed=2**23, transcendentals=0),
        name="late_plans",
    )(nbr, obs_row, tile_row, ext_row)


def grouped_products(plan, sizes, lists, x, blocks, total):
    group, per_round = plan
    slots, groups = sizes

    def one(c, _):
        products = []
        for u in range(per_round):
            first = (c * per_round + u) * group
            rows = [x[lists[0, first + g]] for g in range(group)]
            tiles = [blocks[lists[0, slots + first + g]] for g in range(group)]
            products.append(matmul(jnp.concatenate(rows, axis=1), jnp.concatenate(tiles, axis=0)))
        for u in range(per_round):
            total[lists[0, 2 * slots + c * per_round + u]] += products[u]
        return 0

    lax.fori_loop(0, lists[0, 2 * slots + groups - 1], one, 0)


def jac_kernel(plan, sizes, n_parts, started, n_outs, lists, *refs):
    parts, refs = refs[:n_parts], refs[n_parts:]
    if started:
        begun, refs = refs[0], refs[1:]
    jac, outs, (x, total) = refs[0], refs[1 : 1 + n_outs], refs[1 + n_outs :]
    rows = parts[0].shape[0]
    for k, part in enumerate(parts):
        x[k * rows : (k + 1) * rows] = part[...]
    x[x.shape[0] - 1] = jnp.zeros(x.shape[1:], HALF)
    if started:
        total[: begun.shape[0]] = begun[...]
    else:
        total[...] = jnp.zeros_like(total)
    grouped_products(plan, sizes, lists, x, jac, total)
    rows = outs[0].shape[0]
    for k, out in enumerate(outs):
        out[...] = total[k * rows : (k + 1) * rows].astype(out.dtype)


def jac_pass(plan, lists, parts, begun, jac, rows, out_rows, out_types, name):
    probes, width = parts[0].shape[1:]
    n_outs = len(out_types)
    smem = pl.BlockSpec(memory_space=pltpu.SMEM)
    vmem = pl.BlockSpec(memory_space=pltpu.VMEM)
    operands = (lists, *parts) + (() if begun is None else (begun,)) + (jac,)
    sizes = plan_sizes(plan, jac.shape[0], rows)
    return pl.pallas_call(
        functools.partial(jac_kernel, plan, sizes, len(parts), begun is not None, n_outs),
        in_specs=[smem] + [vmem] * (len(operands) - 1),
        out_specs=[vmem] * n_outs,
        out_shape=[jax.ShapeDtypeStruct((out_rows // n_outs, probes, width), t) for t in out_types],
        scratch_shapes=[
            pltpu.VMEM((rows + 1, probes, width), HALF),
            pltpu.VMEM((rows + 1, probes, width), F32),
        ],
        compiler_params=pltpu.CompilerParams(vmem_limit_bytes=VMEM_LIMIT),
        cost_estimate=pl.CostEstimate(flops=0, bytes_accessed=jac.size, transcendentals=0),
        name=name,
    )(*operands)


def gather_kernel(rows, sizes, nbr, lists, mine, other, prior, ext, to_core, to_far, x, total):
    half = mine.shape[0]
    side = nbr[0, nbr.shape[1] - 1]
    x[:half] = (mine[...].astype(F32) + other[...].astype(F32)).astype(HALF)
    x[rows] = jnp.zeros(x.shape[1:], HALF)
    total[...] = jnp.zeros_like(total)
    grouped_products(PRIOR_PLAN, sizes, lists, x, prior, total)
    ext[...] = total[: 2 * half]
    to_core[...] = total[pl.ds(half * (1 - side), half)].astype(HALF)
    to_far[...] = total[pl.ds(half * side, half)].astype(HALF)


def gather_tiles(nbr, lists, mine, other, prior, rows):
    tiles, probes, width = mine.shape
    smem = pl.BlockSpec(memory_space=pltpu.SMEM)
    vmem = pl.BlockSpec(memory_space=pltpu.VMEM)
    return pl.pallas_call(
        functools.partial(gather_kernel, rows, plan_sizes(PRIOR_PLAN, nbr.shape[1] - LANES, rows)),
        in_specs=[smem, smem, vmem, vmem, vmem],
        out_specs=[vmem] * 3,
        out_shape=[
            jax.ShapeDtypeStruct((2 * tiles, probes, width), F32),
            jax.ShapeDtypeStruct((tiles, probes, width), HALF),
            jax.ShapeDtypeStruct((tiles, probes, width), HALF),
        ],
        scratch_shapes=[
            pltpu.VMEM((rows + 1, probes, width), HALF),
            pltpu.VMEM((rows + 1, probes, width), F32),
        ],
        compiler_params=pltpu.CompilerParams(vmem_limit_bytes=VMEM_LIMIT),
        name="prior_adjoint",
    )(nbr, lists, mine, other, prior)


def spread_kernel(first, fan, nbr, *refs):
    prior, out, field = refs[-3:]
    tiles = out.shape[0]
    chunk = chunk_of(tiles, 24)
    side = nbr[0, nbr.shape[1] - 1]
    if first:
        probes, beyond = refs[:2]
        reach = beyond.shape[0]
        inner = 2 * tiles - reach
        field[pl.ds(reach * (1 - side), inner)] = probes[pl.ds(reach * side, inner)]
        field[pl.ds(inner * side, reach)] = beyond[...]
    else:
        ext, from_far, from_core = refs[:3]
        for begin, update in ((tiles * (1 - side), from_core), (tiles * side, from_far)):
            at = pl.ds(begin, tiles)
            field[at] = (ext[at] + update[...].astype(F32)).astype(HALF)

    def one(c, _):
        for u in range(chunk):
            t = c * chunk + u
            row = [field[nbr[0, (side * tiles + t) * fan + k]] for k in range(fan)]
            tile = prior[pl.ds(t * fan, fan)]
            tile = tile.reshape(fan * tile.shape[1], tile.shape[2])
            out[t] = matmul(jnp.concatenate(row, axis=1), tile).astype(HALF)
        return 0

    lax.fori_loop(0, tiles // chunk, one, 0)


def spread_tiles(nbr, fields, prior):
    ext_tiles, probes, width = fields[0].shape
    tiles = ext_tiles // 2
    smem = pl.BlockSpec(memory_space=pltpu.SMEM)
    vmem = pl.BlockSpec(memory_space=pltpu.VMEM)
    return pl.pallas_call(
        functools.partial(spread_kernel, len(fields) == 2, prior.shape[0] // tiles),
        in_specs=[smem] + [vmem] * len(fields) + [vmem],
        out_specs=vmem,
        out_shape=jax.ShapeDtypeStruct((tiles, probes, width), HALF),
        scratch_shapes=[pltpu.VMEM(fields[0].shape, HALF)],
        compiler_params=pltpu.CompilerParams(vmem_limit_bytes=VMEM_LIMIT),
        name="prior_spread",
    )(nbr, *fields, prior)


def shards(probes, prior_tiles, neighbours, jac, jac_obs, jac_flux, counts, rinv):
    n_obs, n_flux = lax.axis_size("obs"), lax.axis_size("flux")
    tile_count = probes.shape[0]
    half = tile_count // 2
    reach = tile_count // 4
    obs_rows = rinv.shape[0]
    quarter = obs_rows // 4
    blocks = jac[0, 0]
    flux_at = lax.axis_index("flux")
    side = lax.rem(lax.axis_index("obs"), 2)
    corner = lax.rem(flux_at, 4)
    fan = neighbours.shape[1]
    prior = prior_tiles.reshape((tile_count * fan,) + prior_tiles.shape[2:])
    own_rinv = lax.dynamic_slice_in_dim(rinv, corner * quarter, quarter, 0)[:, None, :]
    rows = max(obs_rows, tile_count)
    sizes = (obs_rows, tile_count, fan)

    def swap_core(value):
        return exchange(value, lambda i, j: (i ^ 1, j))

    def swap_far(value):
        def partner(i, j):
            to = j - 1 if i % 2 == 0 else j + 1
            return (i ^ 1, to) if 0 <= to < n_flux else None

        return exchange(value, partner)

    def swap_flux(value, bits):
        return exchange(value, lambda i, j: (i, j ^ bits))

    edge = jnp.where(side == 0, probes[:reach], probes[tile_count - reach :])
    beyond = swap_far(edge)
    where = jnp.stack([side, corner, counts[0, 0], flux_at * tile_count + side * half])

    where, own_rinv, prior, blocks = lax.optimization_barrier((where, own_rinv, prior, blocks))
    jac_plain = blocks
    prior_plain, *index_rows, own_lists, other_lists, near_lists, nbr = setup(
        where, jac_obs[0], jac_flux[0], neighbours.T, prior, sizes
    )
    fields = (probes, beyond)
    for step in range(STEPS):
        spread = spread_tiles(nbr, fields, prior_plain)
        other = swap_core(spread)
        far_rows = obs_rows - quarter
        (begun,) = jac_pass(
            FORWARD_PLANS[0], own_lists, (spread,), None, jac_plain, rows, far_rows, [F32], "forward_own"
        )
        pieces = jac_pass(
            FORWARD_PLANS[1], other_lists, (other,), begun, jac_plain, rows, far_rows, [HALF] * 3, "forward_other"
        )
        (total,) = jac_pass(
            FORWARD_PLANS[2], near_lists, (spread, other), None, jac_plain, rows, quarter, [F32], "forward_near"
        )
        if step == 0:
            pieces, jac_plain = lax.optimization_barrier((pieces, jac_plain))
            jac_turned = turn_blocks(jac_plain, "jac_turn")
        for bits in (3, 2, 1):
            total = total + swap_flux(pieces[bits - 1], bits).astype(F32)
        if step == 0:
            total, jac_turned, index_rows = lax.optimization_barrier((total, jac_turned, index_rows))
            adjoint_lists = late_plans(nbr, *index_rows, sizes)
        bits = 4
        while bits < n_flux:
            sent = total.astype(HALF)
            total = sent.astype(F32) + swap_flux(sent, bits).astype(F32)
            bits *= 2
        if step == 0:
            total, adjoint_lists = lax.optimization_barrier((total, adjoint_lists))
            prior_lists = adjoint_lists[5]
        weighted = (total * own_rinv).astype(HALF)
        quarters = [weighted] + [swap_flux(weighted, bits) for bits in range(1, 4)]
        begun = None
        for part, at in enumerate((0, 3, 2)):
            types = [F32] * (2 if part == 2 else 1)
            begun = jac_pass(
                ADJOINT_PLANS[part],
                adjoint_lists[part],
                (quarters[at],),
                None if part == 0 else begun[0],
                jac_turned,
                rows,
                tile_count,
                types,
                f"adjoint_quarter{at}",
            )
        mine, theirs = begun
        (theirs,) = jac_pass(
            ADJOINT_PLANS[3], adjoint_lists[3], (quarters[1],), theirs, jac_turned, rows, half, [HALF], "adjoint_other"
        )
        (mine,) = jac_pass(
            ADJOINT_PLANS[4], adjoint_lists[4], (quarters[1],), mine, jac_turned, rows, half, [F32], "adjoint_own"
        )
        mine = (mine + swap_core(theirs).astype(F32)).astype(HALF)
        if step == 0:
            mine, prior_plain = lax.optimization_barrier((mine, prior_plain))
            prior_turned = turn_blocks(prior_plain, "prior_turn")
        bits = 2
        while bits < n_obs:
            other = exchange(mine, lambda i, j, bits=bits: (i ^ bits, j))
            bits *= 2
            if bits < n_obs:
                mine = (mine.astype(F32) + other.astype(F32)).astype(HALF)
        ext, to_core, to_far = gather_tiles(nbr, prior_lists, mine, other, prior_turned, rows)
        if step < STEPS - 1:
            fields = (ext, swap_far(to_far), swap_core(to_core))
    lower = side == 0
    from_core = swap_core(jnp.where(lower, to_core[half - reach :], to_core[:reach])).astype(F32)
    from_far = swap_far(jnp.where(lower, to_far[:reach], to_far[half - reach :])).astype(F32)
    low = jnp.where(lower, from_far, from_core)
    high = jnp.where(lower, from_core, from_far)
    own = (ext[reach : reach + half] + jnp.concatenate([low, high], axis=0)).astype(HALF)
    other = swap_core(own)
    first = jnp.where(side == 0, own, other)
    second = jnp.where(side == 0, other, own)
    return jnp.concatenate([first, second], axis=0)


def solution(mesh):
    placed = (
        P("flux", None, None),
        P("flux", None, None, None),
        P("flux", None),
        P("obs", "flux", None, None, None),
        P("obs", "flux", None),
        P("obs", "flux", None),
        P("obs", "flux"),
        P("obs", None),
    )
    return jax.shard_map(
        shards, mesh=mesh, in_specs=placed, out_specs=P("flux", None, None), check_vma=False
    )
```

```python
import functools
import math

import jax
import jax.numpy as jnp
from jax import lax
from jax.experimental import pallas as pl
from jax.experimental.pallas import tpu as pltpu
from jax.sharding import PartitionSpec as P

STEPS = 4
F32 = jnp.float32
HALF = jnp.bfloat16
VMEM_LIMIT = 8 * 2**20
LANES = 128
FORWARD_PLANS = ((2, 45), (2, 45), (2, 29))
ADJOINT_PLANS = ((2, 35), (2, 35), (2, 35), (2, 19), (2, 19))
PRIOR_PLAN = (2, 56)


def matmul(a, b):
    return lax.dot_general(a, b, (((1,), (0,)), ((), ())), preferred_element_type=F32)


def chunk_of(count, most):
    return max(c for c in range(1, most + 1) if count % c == 0)


def exchange(value, partner):
    n_obs, n_flux = lax.axis_size("obs"), lax.axis_size("flux")
    route = []
    for i in range(n_obs):
        for j in range(n_flux):
            to = partner(i, j)
            if to is not None:
                route.append((i * n_flux + j, to[0] * n_flux + to[1]))
    return lax.ppermute(value, ("obs", "flux"), route)


def plan_sizes(plan, blocks, dst_rows):
    group, per_round = plan
    groups = blocks // group + dst_rows
    groups += -groups % per_round
    slots = groups * group
    return slots + -slots % LANES, groups + 1 + -(groups + 1) % LANES


def columns(row):
    parts = [
        jnp.broadcast_to(row[:, k : k + LANES], (LANES, LANES)).T for k in range(0, row.shape[1], LANES)
    ]
    return jnp.concatenate(parts, axis=0)


def plan_groups(plan, src, dst, first, rows, out):
    group, per_round = plan
    blocks = dst.shape[1]
    slots, groups = plan_sizes(plan, blocks, rows)
    i32 = jnp.int32
    lane = lax.broadcasted_iota(i32, (blocks, LANES), 1)
    at = lax.broadcasted_iota(i32, (blocks, LANES), 0)
    src_at, dst_at = columns(src), columns(dst)
    rank = jnp.zeros((blocks, LANES), F32)
    for k in range(0, blocks, LANES):
        same = (dst_at == dst[:, k : k + LANES]) & (lane + k < at)
        rank += same.astype(F32)
    rank = jnp.sum(rank, axis=1, keepdims=True)
    fills = jnp.sum((dst_at == lane).astype(F32), axis=0, keepdims=True)
    sizes = jnp.where(lane[:1] < rows, jnp.floor((fills + (group - 1)) * (1.0 / group)), 0.0)
    begin = jnp.sum(jnp.where(lane < dst_at, sizes, 0.0), axis=1, keepdims=True)
    place = (begin * group + rank).astype(i32)
    place = jnp.where(dst_at < rows, place, slots)
    for k in range(0, slots, LANES):
        hit = place == lane + k
        of = jnp.sum(jnp.where(hit, (src_at - rows).astype(F32), 0.0), axis=0, keepdims=True)
        out[:, k : k + LANES] = of.astype(i32) + rows
        of = jnp.sum(jnp.where(hit, (at - first).astype(F32), 0.0), axis=0, keepdims=True)
        out[:, slots + k : slots + k + LANES] = of.astype(i32)
    full = jnp.sum(sizes, axis=1, keepdims=True)
    rounds = jnp.sum((lane[:1].astype(F32) * per_round < full).astype(F32), axis=1, keepdims=True)
    for k in range(0, groups, LANES):
        lead = place == (lane + k) * group
        of = jnp.sum(jnp.where(lead, (dst_at - rows).astype(F32), 0.0), axis=0, keepdims=True)
        of = jnp.where(lane[:1] + k == groups - 1, rounds, of + rows)
        out[:, 2 * slots + k : 2 * slots + k + LANES] = of.astype(i32)


def setup_kernel(
    rows, chunk, where, obs, flux, nbr, prior,
    prior_plain, *refs
):
    (obs_row, tile_row, ext_row), plans, refs = refs[:3], refs[3:7], refs[7:]
    (obs_in, flux_in, nbr_in), built, (small_sems, sems) = refs[:3], refs[3:7], refs[7:]
    side, corner, count, first_tile = where[0], where[1], where[2], where[3]
    owned = prior_plain.shape[0]
    begin = side * owned
    rounds = (owned // chunk,)

    def copy(c, first, source, plain, offset):
        to = pl.ds(c * chunk, chunk)
        return pltpu.make_async_copy(source.at[pl.ds(first + c * chunk, chunk)], plain.at[to], sems.at[offset + c])

    def start(first, source, plain, offset):
        def one(c, _):
            copy(c, first, source, plain, offset).start()
            return 0

        return one

    def wait(first, source, plain, offset):
        def one(c, _):
            copy(c, first, source, plain, offset).wait()
            return 0

        return one

    small = ((obs, obs_in), (flux, flux_in), (nbr, nbr_in))
    small = [pltpu.make_async_copy(src, dst, small_sems.at[k]) for k, (src, dst) in enumerate(small)]
    for one in small:
        one.start()
    lax.fori_loop(0, rounds[0], start(begin, prior, prior_plain, 0), 0)
    for one in small:
        one.wait()

    obs_rows, tile_rows, fan = rows
    half = tile_rows // 2
    reach = tile_rows // 4
    quarter = obs_rows // 4
    most = max(obs_rows, tile_rows)
    i32 = jnp.int32
    at = lax.broadcasted_iota(i32, obs_in.shape, 1)
    live = at < count
    block = sum((obs_in[...] >= k * quarter).astype(i32) for k in range(1, 4))
    obs_at = (block ^ corner) * quarter + obs_in[...] - block * quarter
    block = (flux_in[...] >= half).astype(i32)
    tile_at = (block ^ side) * half + flux_in[...] - block * half
    obs_at, tile_at = jnp.where(live, obs_at, 2 * most), jnp.where(live, tile_at, 2 * most)
    obs_row[...], tile_row[...] = obs_at, tile_at
    own, near = tile_at < half, obs_at < quarter
    uses = (
        (tile_at, obs_at - quarter, live & own & ~near),
        (tile_at - half, obs_at - quarter, live & ~own & ~near),
        (tile_at, obs_at, near),
    )
    for plan, (src, dst, use), out in zip(FORWARD_PLANS, uses, built):
        plan_groups(plan, jnp.where(use, src, 0), jnp.where(use, dst, most), 0, most, out)
    count = tile_rows * fan
    entry = lax.broadcasted_iota(i32, (fan, count), 1) - lax.broadcasted_iota(i32, (fan, count), 0)
    local = nbr_in[...] - first_tile + reach
    spread = sum(
        jnp.where(entry == t * fan, local[:, t : t + 1], 0).astype(F32) for t in range(tile_rows)
    )
    ext = jnp.sum(spread, axis=0, keepdims=True).astype(i32)
    ext_row[...] = ext
    built[3][:, : ext.shape[1]] = ext
    built[3][:, ext.shape[1] :] = jnp.zeros((1, LANES), i32) + side
    lists = [
        pltpu.make_async_copy(src, dst, small_sems.at[3 + k])
        for k, (src, dst) in enumerate(zip(built, plans))
    ]
    for one in lists:
        one.start()

    lax.fori_loop(0, rounds[0], wait(begin, prior, prior_plain, 0), 0)
    for one in lists:
        one.wait()


def turn_kernel(chunk, plain, turned):
    def one(c, _):
        for u in range(chunk):
            turned[c * chunk + u] = plain[c * chunk + u].T
        return 0

    lax.fori_loop(0, plain.shape[0] // chunk, one, 0)


def turn_blocks(plain, name):
    vmem = pl.BlockSpec(memory_space=pltpu.VMEM)
    return pl.pallas_call(
        functools.partial(turn_kernel, chunk_of(plain.shape[0], 48)),
        in_specs=[vmem],
        out_specs=vmem,
        out_shape=pltpu.VMEM(plain.shape, HALF),
        compiler_params=pltpu.CompilerParams(vmem_limit_bytes=VMEM_LIMIT),
        cost_estimate=pl.CostEstimate(flops=0, bytes_accessed=2 * plain.size, transcendentals=0),
        name=name,
    )(plain)


def plan_lengths(plans, width, most):
    sizes = (plan_sizes(plan, width, most) for plan in plans)
    return [2 * slots + groups for slots, groups in sizes]


def setup(where, obs, flux, nbr, prior, rows):
    owned = rows[1] // 2 * rows[2]
    chunk = chunk_of(owned, 24)
    smem = pl.BlockSpec(memory_space=pltpu.SMEM)
    vmem = pl.BlockSpec(memory_space=pltpu.VMEM)
    hbm = pl.BlockSpec(memory_space=pl.ANY)
    i32 = jnp.int32
    lengths = plan_lengths(FORWARD_PLANS, obs.shape[1], max(rows[:2])) + [nbr.size + LANES]
    return pl.pallas_call(
        functools.partial(setup_kernel, rows, chunk),
        in_specs=[smem] + [hbm] * 4,
        out_specs=[vmem] * 4 + [smem] * 4,
        out_shape=[pltpu.VMEM((owned,) + prior.shape[1:], HALF)]
        + [pltpu.VMEM(s, i32) for s in (obs.shape, flux.shape, (1, nbr.size))]
        + [pltpu.SMEM((1, n), i32) for n in lengths],
        scratch_shapes=[pltpu.VMEM(v.shape, i32) for v in (obs, flux, nbr)]
        + [pltpu.VMEM((1, n), i32) for n in lengths]
        + [
            pltpu.SemaphoreType.DMA((7,)),
            pltpu.SemaphoreType.DMA((owned // chunk,)),
        ],
        compiler_params=pltpu.CompilerParams(vmem_limit_bytes=VMEM_LIMIT),
        name="setup",
    )(where, *(pltpu.with_memory_space_constraint(v, pltpu.HBM) for v in (obs, flux, nbr, prior)))


def late_kernel(rows, nbr, obs_row, tile_row, ext_row, *refs):
    plans, built, sems = refs[:6], refs[6:12], refs[12]
    obs_rows, tile_rows, fan = rows
    half, quarter, most = tile_rows // 2, obs_rows // 4, max(obs_rows, tile_rows)
    side = nbr[0, nbr.shape[1] - 1]
    obs_at, tile_at, ext = obs_row[...], tile_row[...], ext_row[...]
    part = [(obs_at >= k * quarter) & (obs_at < (k + 1) * quarter) for k in range(4)]
    uses = (
        (obs_at, tile_at, part[0]),
        (obs_at - 3 * quarter, tile_at, part[3]),
        (obs_at - 2 * quarter, tile_at, part[2]),
        (obs_at - quarter, tile_at - half, part[1] & (tile_at >= half)),
        (obs_at - quarter, tile_at, part[1] & (tile_at < half)),
    )
    for plan, (src, dst, use), out in zip(ADJOINT_PLANS, uses, built):
        plan_groups(plan, jnp.where(use, src, 0), jnp.where(use, dst, most), 0, most, out)
    at = lax.broadcasted_iota(jnp.int32, ext.shape, 1)
    tile = sum((at >= k * fan).astype(jnp.int32) for k in range(1, tile_rows)) - side * half
    owns = (tile >= 0) & (tile < half)
    src, dst = jnp.where(owns, tile, 0), jnp.where(owns, ext, most)
    plan_groups(PRIOR_PLAN, src, dst, side * (half * fan), most, built[5])
    lists = [pltpu.make_async_copy(a, b, sems.at[k]) for k, (a, b) in enumerate(zip(built, plans))]
    for one in lists:
        one.start()
    for one in lists:
        one.wait()


def late_plans(nbr, obs_row, tile_row, ext_row, rows):
    smem = pl.BlockSpec(memory_space=pltpu.SMEM)
    vmem = pl.BlockSpec(memory_space=pltpu.VMEM)
    most = max(rows[:2])
    lengths = plan_lengths(ADJOINT_PLANS, obs_row.shape[1], most)
    lengths += plan_lengths((PRIOR_PLAN,), ext_row.shape[1], most)
    return pl.pallas_call(
        functools.partial(late_kernel, rows),
        in_specs=[smem] + [vmem] * 3,
        out_specs=[smem] * 6,
        out_shape=[pltpu.SMEM((1, n), jnp.int32) for n in lengths],
        scratch_shapes=[pltpu.VMEM((1, n), jnp.int32) for n in lengths]
        + [pltpu.SemaphoreType.DMA((6,))],
        compiler_params=pltpu.CompilerParams(vmem_limit_bytes=VMEM_LIMIT),
        cost_estimate=pl.CostEstimate(flops=0, bytes_accessed=2**23, transcendentals=0),
        name="late_plans",
    )(nbr, obs_row, tile_row, ext_row)


def grouped_products(plan, sizes, lists, x, blocks, total):
    group, per_round = plan
    slots, groups = sizes

    def one(c, _):
        products = []
        for u in range(per_round):
            first = (c * per_round + u) * group
            rows = [x[lists[0, first + g]] for g in range(group)]
            tiles = [blocks[lists[0, slots + first + g]] for g in range(group)]
            products.append(matmul(jnp.concatenate(rows, axis=1), jnp.concatenate(tiles, axis=0)))
        for u in range(per_round):
            total[lists[0, 2 * slots + c * per_round + u]] += products[u]
        return 0

    lax.fori_loop(0, lists[0, 2 * slots + groups - 1], one, 0)


def jac_kernel(plan, sizes, n_parts, started, n_outs, lists, *refs):
    parts, refs = refs[:n_parts], refs[n_parts:]
    if started:
        begun, refs = refs[0], refs[1:]
    jac, outs, (x, total) = refs[0], refs[1 : 1 + n_outs], refs[1 + n_outs :]
    rows = parts[0].shape[0]
    for k, part in enumerate(parts):
        x[k * rows : (k + 1) * rows] = part[...]
    x[x.shape[0] - 1] = jnp.zeros(x.shape[1:], HALF)
    if started:
        total[: begun.shape[0]] = begun[...]
    else:
        total[...] = jnp.zeros_like(total)
    grouped_products(plan, sizes, lists, x, jac, total)
    rows = outs[0].shape[0]
    for k, out in enumerate(outs):
        out[...] = total[k * rows : (k + 1) * rows].astype(out.dtype)


def jac_pass(plan, lists, parts, begun, jac, rows, out_rows, out_types, name):
    probes, width = parts[0].shape[1:]
    n_outs = len(out_types)
    smem = pl.BlockSpec(memory_space=pltpu.SMEM)
    vmem = pl.BlockSpec(memory_space=pltpu.VMEM)
    operands = (lists, *parts) + (() if begun is None else (begun,)) + (jac,)
    sizes = plan_sizes(plan, jac.shape[0], rows)
    return pl.pallas_call(
        functools.partial(jac_kernel, plan, sizes, len(parts), begun is not None, n_outs),
        in_specs=[smem] + [vmem] * (len(operands) - 1),
        out_specs=[vmem] * n_outs,
        out_shape=[jax.ShapeDtypeStruct((out_rows // n_outs, probes, width), t) for t in out_types],
        scratch_shapes=[
            pltpu.VMEM((rows + 1, probes, width), HALF),
            pltpu.VMEM((rows + 1, probes, width), F32),
        ],
        compiler_params=pltpu.CompilerParams(vmem_limit_bytes=VMEM_LIMIT),
        cost_estimate=pl.CostEstimate(flops=0, bytes_accessed=jac.size, transcendentals=0),
        name=name,
    )(*operands)


def gather_kernel(rows, sizes, nbr, lists, mine, other, prior, ext, to_core, to_far, x, total):
    half = mine.shape[0]
    side = nbr[0, nbr.shape[1] - 1]
    x[:half] = (mine[...].astype(F32) + other[...].astype(F32)).astype(HALF)
    x[rows] = jnp.zeros(x.shape[1:], HALF)
    total[...] = jnp.zeros_like(total)
    grouped_products(PRIOR_PLAN, sizes, lists, x, prior, total)
    ext[...] = total[: 2 * half]
    to_core[...] = total[pl.ds(half * (1 - side), half)].astype(HALF)
    to_far[...] = total[pl.ds(half * side, half)].astype(HALF)


def gather_tiles(nbr, lists, mine, other, prior, rows):
    tiles, probes, width = mine.shape
    smem = pl.BlockSpec(memory_space=pltpu.SMEM)
    vmem = pl.BlockSpec(memory_space=pltpu.VMEM)
    return pl.pallas_call(
        functools.partial(gather_kernel, rows, plan_sizes(PRIOR_PLAN, nbr.shape[1] - LANES, rows)),
        in_specs=[smem, smem, vmem, vmem, vmem],
        out_specs=[vmem] * 3,
        out_shape=[
            jax.ShapeDtypeStruct((2 * tiles, probes, width), F32),
            jax.ShapeDtypeStruct((tiles, probes, width), HALF),
            jax.ShapeDtypeStruct((tiles, probes, width), HALF),
        ],
        scratch_shapes=[
            pltpu.VMEM((rows + 1, probes, width), HALF),
            pltpu.VMEM((rows + 1, probes, width), F32),
        ],
        compiler_params=pltpu.CompilerParams(vmem_limit_bytes=VMEM_LIMIT),
        name="prior_adjoint",
    )(nbr, lists, mine, other, prior)


def spread_kernel(first, fan, nbr, *refs):
    prior, out, field = refs[-3:]
    tiles = out.shape[0]
    chunk = chunk_of(tiles, 24)
    side = nbr[0, nbr.shape[1] - 1]
    if first:
        probes, beyond = refs[:2]
        reach = beyond.shape[0]
        inner = 2 * tiles - reach
        field[pl.ds(reach * (1 - side), inner)] = probes[pl.ds(reach * side, inner)]
        field[pl.ds(inner * side, reach)] = beyond[...]
    else:
        for part in range(2):
            ext, from_far, from_core = refs[3 * part : 3 * part + 3]
            span = ext.shape[1]
            across = slice(part * span, (part + 1) * span)
            for begin, update in ((tiles * (1 - side), from_core), (tiles * side, from_far)):
                at = pl.ds(begin, tiles)
                field[at, across] = (ext[at] + update[...].astype(F32)).astype(HALF)

    def one(c, _):
        for u in range(chunk):
            t = c * chunk + u
            row = [field[nbr[0, (side * tiles + t) * fan + k]] for k in range(fan)]
            tile = prior[pl.ds(t * fan, fan)]
            tile = tile.reshape(fan * tile.shape[1], tile.shape[2])
            out[t] = matmul(jnp.concatenate(row, axis=1), tile).astype(HALF)
        return 0

    lax.fori_loop(0, tiles // chunk, one, 0)


def spread_tiles(nbr, fields, prior):
    first = len(fields) == 2
    ext_tiles, probes, width = fields[0].shape
    if not first:
        probes *= 2
    tiles = ext_tiles // 2
    smem = pl.BlockSpec(memory_space=pltpu.SMEM)
    vmem = pl.BlockSpec(memory_space=pltpu.VMEM)
    return pl.pallas_call(
        functools.partial(spread_kernel, first, prior.shape[0] // tiles),
        in_specs=[smem] + [vmem] * len(fields) + [vmem],
        out_specs=vmem,
        out_shape=jax.ShapeDtypeStruct((tiles, probes, width), HALF),
        scratch_shapes=[pltpu.VMEM((ext_tiles, probes, width), HALF)],
        compiler_params=pltpu.CompilerParams(vmem_limit_bytes=VMEM_LIMIT),
        name="prior_spread",
    )(nbr, *fields, prior)


def shards(probes, prior_tiles, neighbours, jac, jac_obs, jac_flux, counts, rinv):
    n_obs, n_flux = lax.axis_size("obs"), lax.axis_size("flux")
    tile_count = probes.shape[0]
    half = tile_count // 2
    reach = tile_count // 4
    obs_rows = rinv.shape[0]
    quarter = obs_rows // 4
    blocks = jac[0, 0]
    flux_at = lax.axis_index("flux")
    side = lax.rem(lax.axis_index("obs"), 2)
    corner = lax.rem(flux_at, 4)
    fan = neighbours.shape[1]
    prior = prior_tiles.reshape((tile_count * fan,) + prior_tiles.shape[2:])
    own_rinv = lax.dynamic_slice_in_dim(rinv, corner * quarter, quarter, 0)[:, None, :]
    rows = max(obs_rows, tile_count)
    sizes = (obs_rows, tile_count, fan)

    def swap_core(value):
        return exchange(value, lambda i, j: (i ^ 1, j))

    def swap_far(value):
        def partner(i, j):
            to = j - 1 if i % 2 == 0 else j + 1
            return (i ^ 1, to) if 0 <= to < n_flux else None

        return exchange(value, partner)

    def swap_flux(value, bits):
        return exchange(value, lambda i, j: (i, j ^ bits))

    edge = jnp.where(side == 0, probes[:reach], probes[tile_count - reach :])
    beyond = swap_far(edge)
    where = jnp.stack([side, corner, counts[0, 0], flux_at * tile_count + side * half])

    where, own_rinv, prior, blocks = lax.optimization_barrier((where, own_rinv, prior, blocks))
    jac_plain = blocks
    prior_plain, *index_rows, own_lists, other_lists, near_lists, nbr = setup(
        where, jac_obs[0], jac_flux[0], neighbours.T, prior, sizes
    )
    fields = (probes, beyond)
    for step in range(STEPS):
        spread = spread_tiles(nbr, fields, prior_plain)
        other = swap_core(spread)
        far_rows = obs_rows - quarter
        (begun,) = jac_pass(
            FORWARD_PLANS[0], own_lists, (spread,), None, jac_plain, rows, far_rows, [F32], "forward_own"
        )
        pieces = jac_pass(
            FORWARD_PLANS[1], other_lists, (other,), begun, jac_plain, rows, far_rows, [HALF] * 3, "forward_other"
        )
        (total,) = jac_pass(
            FORWARD_PLANS[2], near_lists, (spread, other), None, jac_plain, rows, quarter, [F32], "forward_near"
        )
        if step == 0:
            pieces, jac_plain = lax.optimization_barrier((pieces, jac_plain))
            jac_turned = turn_blocks(jac_plain, "jac_turn")
        for bits in (3, 2, 1):
            total = total + swap_flux(pieces[bits - 1], bits).astype(F32)
        if step == 0:
            total, jac_turned, index_rows = lax.optimization_barrier((total, jac_turned, index_rows))
            adjoint_lists = late_plans(nbr, *index_rows, sizes)
        bits = 4
        while bits < n_flux:
            sent = total.astype(HALF)
            total = sent.astype(F32) + swap_flux(sent, bits).astype(F32)
            bits *= 2
        if step == 0:
            total, adjoint_lists = lax.optimization_barrier((total, adjoint_lists))
            prior_lists = adjoint_lists[5]
        weighted = (total * own_rinv).astype(HALF)
        quarters = [weighted] + [swap_flux(weighted, bits) for bits in range(1, 4)]
        begun = None
        for part, at in enumerate((0, 3, 2)):
            types = [F32] * (2 if part == 2 else 1)
            begun = jac_pass(
                ADJOINT_PLANS[part],
                adjoint_lists[part],
                (quarters[at],),
                None if part == 0 else begun[0],
                jac_turned,
                rows,
                tile_count,
                types,
                f"adjoint_quarter{at}",
            )
        mine, theirs = begun
        (theirs,) = jac_pass(
            ADJOINT_PLANS[3], adjoint_lists[3], (quarters[1],), theirs, jac_turned, rows, half, [HALF], "adjoint_other"
        )
        (mine,) = jac_pass(
            ADJOINT_PLANS[4], adjoint_lists[4], (quarters[1],), mine, jac_turned, rows, half, [F32], "adjoint_own"
        )
        mine = (mine + swap_core(theirs).astype(F32)).astype(HALF)
        if step == 0:
            mine, prior_plain = lax.optimization_barrier((mine, prior_plain))
            prior_turned = turn_blocks(prior_plain, "prior_turn")
        span = mine.shape[1] // 2
        sums = [mine[:, :span], mine[:, span:]]
        bits = 2
        while bits < n_obs:
            others = [exchange(v, lambda i, j, bits=bits: (i ^ bits, j)) for v in sums]
            bits *= 2
            if bits < n_obs:
                sums = [(v.astype(F32) + o.astype(F32)).astype(HALF) for v, o in zip(sums, others)]
        gathered = [
            gather_tiles(nbr, prior_lists, v, o, prior_turned, rows) for v, o in zip(sums, others)
        ]
        if step < STEPS - 1:
            fields = ()
            for ext, to_core, to_far in gathered:
                fields += (ext, swap_far(to_far), swap_core(to_core))
    ext, to_core, to_far = (jnp.concatenate(v, axis=1) for v in zip(*gathered))
    lower = side == 0
    from_core = swap_core(jnp.where(lower, to_core[half - reach :], to_core[:reach])).astype(F32)
    from_far = swap_far(jnp.where(lower, to_far[:reach], to_far[half - reach :])).astype(F32)
    low = jnp.where(lower, from_far, from_core)
    high = jnp.where(lower, from_core, from_far)
    own = (ext[reach : reach + half] + jnp.concatenate([low, high], axis=0)).astype(HALF)
    other = swap_core(own)
    first = jnp.where(side == 0, own, other)
    second = jnp.where(side == 0, other, own)
    return jnp.concatenate([first, second], axis=0)


def solution(mesh):
    placed = (
        P("flux", None, None),
        P("flux", None, None, None),
        P("flux", None),
        P("obs", "flux", None, None, None),
        P("obs", "flux", None),
        P("obs", "flux", None),
        P("obs", "flux"),
        P("obs", None),
    )
    return jax.shard_map(
        shards, mesh=mesh, in_specs=placed, out_specs=P("flux", None, None), check_vma=False
    )
```

```python
import functools
import math

import jax
import jax.numpy as jnp
from jax import lax
from jax.experimental import pallas as pl
from jax.experimental.pallas import tpu as pltpu
from jax.sharding import PartitionSpec as P

STEPS = 4
F32 = jnp.float32
HALF = jnp.bfloat16
VMEM_LIMIT = 8 * 2**20
LANES = 128
FORWARD_PLANS = ((2, 45), (2, 45), (2, 29))
ADJOINT_PLANS = ((2, 35), (2, 35), (2, 35), (2, 19), (2, 19))
PRIOR_PLAN = (2, 56)


def matmul(a, b):
    return lax.dot_general(a, b, (((1,), (0,)), ((), ())), preferred_element_type=F32)


def chunk_of(count, most):
    return max(c for c in range(1, most + 1) if count % c == 0)


def exchange(value, partner):
    n_obs, n_flux = lax.axis_size("obs"), lax.axis_size("flux")
    route = []
    for i in range(n_obs):
        for j in range(n_flux):
            to = partner(i, j)
            if to is not None:
                route.append((i * n_flux + j, to[0] * n_flux + to[1]))
    return lax.ppermute(value, ("obs", "flux"), route)


def plan_sizes(plan, blocks, dst_rows):
    group, per_round = plan
    groups = blocks // group + dst_rows
    groups += -groups % per_round
    slots = groups * group
    return slots + -slots % LANES, groups + 1 + -(groups + 1) % LANES


def columns(row):
    parts = [
        jnp.broadcast_to(row[:, k : k + LANES], (LANES, LANES)).T for k in range(0, row.shape[1], LANES)
    ]
    return jnp.concatenate(parts, axis=0)


def plan_groups(plan, src, dst, first, rows, out):
    group, per_round = plan
    blocks = dst.shape[1]
    slots, groups = plan_sizes(plan, blocks, rows)
    i32 = jnp.int32
    lane = lax.broadcasted_iota(i32, (blocks, LANES), 1)
    at = lax.broadcasted_iota(i32, (blocks, LANES), 0)
    src_at, dst_at = columns(src), columns(dst)
    rank = jnp.zeros((blocks, LANES), F32)
    for k in range(0, blocks, LANES):
        same = (dst_at == dst[:, k : k + LANES]) & (lane + k < at)
        rank += same.astype(F32)
    rank = jnp.sum(rank, axis=1, keepdims=True)
    fills = jnp.sum((dst_at == lane).astype(F32), axis=0, keepdims=True)
    sizes = jnp.where(lane[:1] < rows, jnp.floor((fills + (group - 1)) * (1.0 / group)), 0.0)
    begin = jnp.sum(jnp.where(lane < dst_at, sizes, 0.0), axis=1, keepdims=True)
    place = (begin * group + rank).astype(i32)
    place = jnp.where(dst_at < rows, place, slots)
    for k in range(0, slots, LANES):
        hit = place == lane + k
        of = jnp.sum(jnp.where(hit, (src_at - rows).astype(F32), 0.0), axis=0, keepdims=True)
        out[:, k : k + LANES] = of.astype(i32) + rows
        of = jnp.sum(jnp.where(hit, (at - first).astype(F32), 0.0), axis=0, keepdims=True)
        out[:, slots + k : slots + k + LANES] = of.astype(i32)
    full = jnp.sum(sizes, axis=1, keepdims=True)
    rounds = jnp.sum((lane[:1].astype(F32) * per_round < full).astype(F32), axis=1, keepdims=True)
    for k in range(0, groups, LANES):
        lead = place == (lane + k) * group
        of = jnp.sum(jnp.where(lead, (dst_at - rows).astype(F32), 0.0), axis=0, keepdims=True)
        of = jnp.where(lane[:1] + k == groups - 1, rounds, of + rows)
        out[:, 2 * slots + k : 2 * slots + k + LANES] = of.astype(i32)


def setup_kernel(
    rows, chunk, where, obs, flux, nbr, prior,
    prior_plain, *refs
):
    (obs_row, tile_row, ext_row), plans, refs = refs[:3], refs[3:7], refs[7:]
    (obs_in, flux_in, nbr_in), built, (small_sems, sems) = refs[:3], refs[3:7], refs[7:]
    side, corner, count, first_tile = where[0], where[1], where[2], where[3]
    owned = prior_plain.shape[0]
    begin = side * owned
    rounds = (owned // chunk,)

    def copy(c, first, source, plain, offset):
        to = pl.ds(c * chunk, chunk)
        return pltpu.make_async_copy(source.at[pl.ds(first + c * chunk, chunk)], plain.at[to], sems.at[offset + c])

    def start(first, source, plain, offset):
        def one(c, _):
            copy(c, first, source, plain, offset).start()
            return 0

        return one

    def wait(first, source, plain, offset):
        def one(c, _):
            copy(c, first, source, plain, offset).wait()
            return 0

        return one

    small = ((obs, obs_in), (flux, flux_in), (nbr, nbr_in))
    small = [pltpu.make_async_copy(src, dst, small_sems.at[k]) for k, (src, dst) in enumerate(small)]
    for one in small:
        one.start()
    lax.fori_loop(0, rounds[0], start(begin, prior, prior_plain, 0), 0)
    for one in small:
        one.wait()

    obs_rows, tile_rows, fan = rows
    half = tile_rows // 2
    reach = tile_rows // 4
    quarter = obs_rows // 4
    most = max(obs_rows, tile_rows)
    i32 = jnp.int32
    at = lax.broadcasted_iota(i32, obs_in.shape, 1)
    live = at < count
    block = sum((obs_in[...] >= k * quarter).astype(i32) for k in range(1, 4))
    obs_at = (block ^ corner) * quarter + obs_in[...] - block * quarter
    block = (flux_in[...] >= half).astype(i32)
    tile_at = (block ^ side) * half + flux_in[...] - block * half
    obs_at, tile_at = jnp.where(live, obs_at, 2 * most), jnp.where(live, tile_at, 2 * most)
    obs_row[...], tile_row[...] = obs_at, tile_at
    own, near = tile_at < half, obs_at < quarter
    uses = (
        (tile_at, obs_at - quarter, live & own & ~near),
        (tile_at - half, obs_at - quarter, live & ~own & ~near),
        (tile_at, obs_at, near),
    )
    for plan, (src, dst, use), out in zip(FORWARD_PLANS, uses, built):
        plan_groups(plan, jnp.where(use, src, 0), jnp.where(use, dst, most), 0, most, out)
    count = tile_rows * fan
    entry = lax.broadcasted_iota(i32, (fan, count), 1) - lax.broadcasted_iota(i32, (fan, count), 0)
    local = nbr_in[...] - first_tile + reach
    spread = sum(
        jnp.where(entry == t * fan, local[:, t : t + 1], 0).astype(F32) for t in range(tile_rows)
    )
    ext = jnp.sum(spread, axis=0, keepdims=True).astype(i32)
    ext_row[...] = ext
    built[3][:, : ext.shape[1]] = ext
    built[3][:, ext.shape[1] :] = jnp.zeros((1, LANES), i32) + side
    lists = [
        pltpu.make_async_copy(src, dst, small_sems.at[3 + k])
        for k, (src, dst) in enumerate(zip(built, plans))
    ]
    for one in lists:
        one.start()

    lax.fori_loop(0, rounds[0], wait(begin, prior, prior_plain, 0), 0)
    for one in lists:
        one.wait()


def turn_kernel(chunk, plain, turned):
    def one(c, _):
        for u in range(chunk):
            turned[c * chunk + u] = plain[c * chunk + u].T
        return 0

    lax.fori_loop(0, plain.shape[0] // chunk, one, 0)


def turn_blocks(plain, name):
    vmem = pl.BlockSpec(memory_space=pltpu.VMEM)
    return pl.pallas_call(
        functools.partial(turn_kernel, chunk_of(plain.shape[0], 48)),
        in_specs=[vmem],
        out_specs=vmem,
        out_shape=pltpu.VMEM(plain.shape, HALF),
        compiler_params=pltpu.CompilerParams(vmem_limit_bytes=VMEM_LIMIT),
        cost_estimate=pl.CostEstimate(flops=0, bytes_accessed=2 * plain.size, transcendentals=0),
        name=name,
    )(plain)


def plan_lengths(plans, width, most):
    sizes = (plan_sizes(plan, width, most) for plan in plans)
    return [2 * slots + groups for slots, groups in sizes]


def setup(where, obs, flux, nbr, prior, rows):
    owned = rows[1] // 2 * rows[2]
    chunk = chunk_of(owned, 24)
    smem = pl.BlockSpec(memory_space=pltpu.SMEM)
    vmem = pl.BlockSpec(memory_space=pltpu.VMEM)
    hbm = pl.BlockSpec(memory_space=pl.ANY)
    i32 = jnp.int32
    lengths = plan_lengths(FORWARD_PLANS, obs.shape[1], max(rows[:2])) + [nbr.size + LANES]
    return pl.pallas_call(
        functools.partial(setup_kernel, rows, chunk),
        in_specs=[smem] + [hbm] * 4,
        out_specs=[vmem] * 4 + [smem] * 4,
        out_shape=[pltpu.VMEM((owned,) + prior.shape[1:], HALF)]
        + [pltpu.VMEM(s, i32) for s in (obs.shape, flux.shape, (1, nbr.size))]
        + [pltpu.SMEM((1, n), i32) for n in lengths],
        scratch_shapes=[pltpu.VMEM(v.shape, i32) for v in (obs, flux, nbr)]
        + [pltpu.VMEM((1, n), i32) for n in lengths]
        + [
            pltpu.SemaphoreType.DMA((7,)),
            pltpu.SemaphoreType.DMA((owned // chunk,)),
        ],
        compiler_params=pltpu.CompilerParams(vmem_limit_bytes=VMEM_LIMIT),
        name="setup",
    )(where, *(pltpu.with_memory_space_constraint(v, pltpu.HBM) for v in (obs, flux, nbr, prior)))


def late_kernel(rows, nbr, obs_row, tile_row, ext_row, *refs):
    plans, built, sems = refs[:6], refs[6:12], refs[12]
    obs_rows, tile_rows, fan = rows
    half, quarter, most = tile_rows // 2, obs_rows // 4, max(obs_rows, tile_rows)
    side = nbr[0, nbr.shape[1] - 1]
    obs_at, tile_at, ext = obs_row[...], tile_row[...], ext_row[...]
    part = [(obs_at >= k * quarter) & (obs_at < (k + 1) * quarter) for k in range(4)]
    uses = (
        (obs_at, tile_at, part[0]),
        (obs_at - 3 * quarter, tile_at, part[3]),
        (obs_at - 2 * quarter, tile_at, part[2]),
        (obs_at - quarter, tile_at - half, part[1] & (tile_at >= half)),
        (obs_at - quarter, tile_at, part[1] & (tile_at < half)),
    )
    for plan, (src, dst, use), out in zip(ADJOINT_PLANS, uses, built):
        plan_groups(plan, jnp.where(use, src, 0), jnp.where(use, dst, most), 0, most, out)
    at = lax.broadcasted_iota(jnp.int32, ext.shape, 1)
    tile = sum((at >= k * fan).astype(jnp.int32) for k in range(1, tile_rows)) - side * half
    owns = (tile >= 0) & (tile < half)
    src, dst = jnp.where(owns, tile, 0), jnp.where(owns, ext, most)
    plan_groups(PRIOR_PLAN, src, dst, side * (half * fan), most, built[5])
    lists = [pltpu.make_async_copy(a, b, sems.at[k]) for k, (a, b) in enumerate(zip(built, plans))]
    for one in lists:
        one.start()
    for one in lists:
        one.wait()


def late_plans(nbr, obs_row, tile_row, ext_row, rows):
    smem = pl.BlockSpec(memory_space=pltpu.SMEM)
    vmem = pl.BlockSpec(memory_space=pltpu.VMEM)
    most = max(rows[:2])
    lengths = plan_lengths(ADJOINT_PLANS, obs_row.shape[1], most)
    lengths += plan_lengths((PRIOR_PLAN,), ext_row.shape[1], most)
    return pl.pallas_call(
        functools.partial(late_kernel, rows),
        in_specs=[smem] + [vmem] * 3,
        out_specs=[smem] * 6,
        out_shape=[pltpu.SMEM((1, n), jnp.int32) for n in lengths],
        scratch_shapes=[pltpu.VMEM((1, n), jnp.int32) for n in lengths]
        + [pltpu.SemaphoreType.DMA((6,))],
        compiler_params=pltpu.CompilerParams(vmem_limit_bytes=VMEM_LIMIT),
        cost_estimate=pl.CostEstimate(flops=0, bytes_accessed=2**23, transcendentals=0),
        name="late_plans",
    )(nbr, obs_row, tile_row, ext_row)


def grouped_products(plan, sizes, lists, x, blocks, total):
    group, per_round = plan
    slots, groups = sizes

    def one(c, _):
        products = []
        for u in range(per_round):
            first = (c * per_round + u) * group
            rows = [x[lists[0, first + g]] for g in range(group)]
            tiles = [blocks[lists[0, slots + first + g]] for g in range(group)]
            products.append(matmul(jnp.concatenate(rows, axis=1), jnp.concatenate(tiles, axis=0)))
        for u in range(per_round):
            total[lists[0, 2 * slots + c * per_round + u]] += products[u]
        return 0

    lax.fori_loop(0, lists[0, 2 * slots + groups - 1], one, 0)


def jac_kernel(plan, sizes, n_parts, started, n_outs, lists, *refs):
    parts, refs = refs[:n_parts], refs[n_parts:]
    if started:
        begun, refs = refs[0], refs[1:]
    jac, outs, (x, total) = refs[0], refs[1 : 1 + n_outs], refs[1 + n_outs :]
    rows = parts[0].shape[0]
    for k, part in enumerate(parts):
        x[k * rows : (k + 1) * rows] = part[...]
    x[x.shape[0] - 1] = jnp.zeros(x.shape[1:], HALF)
    if started:
        total[: begun.shape[0]] = begun[...]
    else:
        total[...] = jnp.zeros_like(total)
    grouped_products(plan, sizes, lists, x, jac, total)
    rows = outs[0].shape[0]
    for k, out in enumerate(outs):
        out[...] = total[k * rows : (k + 1) * rows].astype(out.dtype)


def jac_pass(plan, lists, parts, begun, jac, rows, out_rows, out_types, name):
    probes, width = parts[0].shape[1:]
    n_outs = len(out_types)
    smem = pl.BlockSpec(memory_space=pltpu.SMEM)
    vmem = pl.BlockSpec(memory_space=pltpu.VMEM)
    operands = (lists, *parts) + (() if begun is None else (begun,)) + (jac,)
    sizes = plan_sizes(plan, jac.shape[0], rows)
    return pl.pallas_call(
        functools.partial(jac_kernel, plan, sizes, len(parts), begun is not None, n_outs),
        in_specs=[smem] + [vmem] * (len(operands) - 1),
        out_specs=[vmem] * n_outs,
        out_shape=[jax.ShapeDtypeStruct((out_rows // n_outs, probes, width), t) for t in out_types],
        scratch_shapes=[
            pltpu.VMEM((rows + 1, probes, width), HALF),
            pltpu.VMEM((rows + 1, probes, width), F32),
        ],
        compiler_params=pltpu.CompilerParams(vmem_limit_bytes=VMEM_LIMIT),
        cost_estimate=pl.CostEstimate(flops=0, bytes_accessed=jac.size, transcendentals=0),
        name=name,
    )(*operands)


def gather_kernel(rows, sizes, nbr, lists, mine, other, prior, ext, to_core, to_far, x, total):
    half = mine.shape[0]
    side = nbr[0, nbr.shape[1] - 1]
    x[:half] = (mine[...].astype(F32) + other[...].astype(F32)).astype(HALF)
    x[rows] = jnp.zeros(x.shape[1:], HALF)
    total[...] = jnp.zeros_like(total)
    grouped_products(PRIOR_PLAN, sizes, lists, x, prior, total)
    ext[...] = total[: 2 * half]
    to_core[...] = total[pl.ds(half * (1 - side), half)].astype(HALF)
    to_far[...] = total[pl.ds(half * side, half)].astype(HALF)


def gather_tiles(nbr, lists, mine, other, prior, rows):
    tiles, probes, width = mine.shape
    smem = pl.BlockSpec(memory_space=pltpu.SMEM)
    vmem = pl.BlockSpec(memory_space=pltpu.VMEM)
    return pl.pallas_call(
        functools.partial(gather_kernel, rows, plan_sizes(PRIOR_PLAN, nbr.shape[1] - LANES, rows)),
        in_specs=[smem, smem, vmem, vmem, vmem],
        out_specs=[vmem] * 3,
        out_shape=[
            jax.ShapeDtypeStruct((2 * tiles, probes, width), F32),
            jax.ShapeDtypeStruct((tiles, probes, width), HALF),
            jax.ShapeDtypeStruct((tiles, probes, width), HALF),
        ],
        scratch_shapes=[
            pltpu.VMEM((rows + 1, probes, width), HALF),
            pltpu.VMEM((rows + 1, probes, width), F32),
        ],
        compiler_params=pltpu.CompilerParams(vmem_limit_bytes=VMEM_LIMIT),
        name="prior_adjoint",
    )(nbr, lists, mine, other, prior)


def spread_kernel(first, fan, nbr, *refs):
    prior, out, field = refs[-3:]
    tiles = out.shape[0]
    chunk = chunk_of(tiles, 24)
    side = nbr[0, nbr.shape[1] - 1]
    if first:
        probes, beyond = refs[:2]
        reach = beyond.shape[0]
        inner = 2 * tiles - reach
        field[pl.ds(reach * (1 - side), inner)] = probes[pl.ds(reach * side, inner)]
        field[pl.ds(inner * side, reach)] = beyond[...]
    else:
        for part in range(2):
            ext, from_far, from_core = refs[part], refs[2], refs[3]
            span = ext.shape[1]
            across = slice(part * span, (part + 1) * span)
            for begin, update in ((tiles * (1 - side), from_core), (tiles * side, from_far)):
                at = pl.ds(begin, tiles)
                field[at, across] = (ext[at] + update[:, across].astype(F32)).astype(HALF)

    def one(c, _):
        for u in range(chunk):
            t = c * chunk + u
            row = [field[nbr[0, (side * tiles + t) * fan + k]] for k in range(fan)]
            tile = prior[pl.ds(t * fan, fan)]
            tile = tile.reshape(fan * tile.shape[1], tile.shape[2])
            out[t] = matmul(jnp.concatenate(row, axis=1), tile).astype(HALF)
        return 0

    lax.fori_loop(0, tiles // chunk, one, 0)


def spread_tiles(nbr, fields, prior):
    first = len(fields) == 2
    ext_tiles, probes, width = fields[0].shape
    if not first:
        probes *= 2
    tiles = ext_tiles // 2
    smem = pl.BlockSpec(memory_space=pltpu.SMEM)
    vmem = pl.BlockSpec(memory_space=pltpu.VMEM)
    return pl.pallas_call(
        functools.partial(spread_kernel, first, prior.shape[0] // tiles),
        in_specs=[smem] + [vmem] * len(fields) + [vmem],
        out_specs=vmem,
        out_shape=jax.ShapeDtypeStruct((tiles, probes, width), HALF),
        scratch_shapes=[pltpu.VMEM((ext_tiles, probes, width), HALF)],
        compiler_params=pltpu.CompilerParams(vmem_limit_bytes=VMEM_LIMIT),
        name="prior_spread",
    )(nbr, *fields, prior)


def shards(probes, prior_tiles, neighbours, jac, jac_obs, jac_flux, counts, rinv):
    n_obs, n_flux = lax.axis_size("obs"), lax.axis_size("flux")
    tile_count = probes.shape[0]
    half = tile_count // 2
    reach = tile_count // 4
    obs_rows = rinv.shape[0]
    quarter = obs_rows // 4
    blocks = jac[0, 0]
    flux_at = lax.axis_index("flux")
    side = lax.rem(lax.axis_index("obs"), 2)
    corner = lax.rem(flux_at, 4)
    fan = neighbours.shape[1]
    prior = prior_tiles.reshape((tile_count * fan,) + prior_tiles.shape[2:])
    own_rinv = lax.dynamic_slice_in_dim(rinv, corner * quarter, quarter, 0)[:, None, :]
    rows = max(obs_rows, tile_count)
    sizes = (obs_rows, tile_count, fan)

    def swap_core(value):
        return exchange(value, lambda i, j: (i ^ 1, j))

    def swap_far(value):
        def partner(i, j):
            to = j - 1 if i % 2 == 0 else j + 1
            return (i ^ 1, to) if 0 <= to < n_flux else None

        return exchange(value, partner)

    def swap_flux(value, bits):
        return exchange(value, lambda i, j: (i, j ^ bits))

    edge = jnp.where(side == 0, probes[:reach], probes[tile_count - reach :])
    beyond = swap_far(edge)
    where = jnp.stack([side, corner, counts[0, 0], flux_at * tile_count + side * half])

    where, own_rinv, prior, blocks = lax.optimization_barrier((where, own_rinv, prior, blocks))
    jac_plain = blocks
    prior_plain, *index_rows, own_lists, other_lists, near_lists, nbr = setup(
        where, jac_obs[0], jac_flux[0], neighbours.T, prior, sizes
    )
    fields = (probes, beyond)
    for step in range(STEPS):
        spread = spread_tiles(nbr, fields, prior_plain)
        other = swap_core(spread)
        far_rows = obs_rows - quarter
        (begun,) = jac_pass(
            FORWARD_PLANS[0], own_lists, (spread,), None, jac_plain, rows, far_rows, [F32], "forward_own"
        )
        pieces = jac_pass(
            FORWARD_PLANS[1], other_lists, (other,), begun, jac_plain, rows, far_rows, [HALF] * 3, "forward_other"
        )
        (total,) = jac_pass(
            FORWARD_PLANS[2], near_lists, (spread, other), None, jac_plain, rows, quarter, [F32], "forward_near"
        )
        if step == 0:
            pieces, jac_plain = lax.optimization_barrier((pieces, jac_plain))
            jac_turned = turn_blocks(jac_plain, "jac_turn")
        for bits in (3, 2, 1):
            total = total + swap_flux(pieces[bits - 1], bits).astype(F32)
        if step == 0:
            total, jac_turned, index_rows = lax.optimization_barrier((total, jac_turned, index_rows))
            adjoint_lists = late_plans(nbr, *index_rows, sizes)
        bits = 4
        while bits < n_flux:
            sent = total.astype(HALF)
            total = sent.astype(F32) + swap_flux(sent, bits).astype(F32)
            bits *= 2
        if step == 0:
            total, adjoint_lists = lax.optimization_barrier((total, adjoint_lists))
            prior_lists = adjoint_lists[5]
        weighted = (total * own_rinv).astype(HALF)
        quarters = [weighted] + [swap_flux(weighted, bits) for bits in range(1, 4)]
        begun = None
        for part, at in enumerate((0, 3, 2)):
            types = [F32] * (2 if part == 2 else 1)
            begun = jac_pass(
                ADJOINT_PLANS[part],
                adjoint_lists[part],
                (quarters[at],),
                None if part == 0 else begun[0],
                jac_turned,
                rows,
                tile_count,
                types,
                f"adjoint_quarter{at}",
            )
        mine, theirs = begun
        (theirs,) = jac_pass(
            ADJOINT_PLANS[3], adjoint_lists[3], (quarters[1],), theirs, jac_turned, rows, half, [HALF], "adjoint_other"
        )
        (mine,) = jac_pass(
            ADJOINT_PLANS[4], adjoint_lists[4], (quarters[1],), mine, jac_turned, rows, half, [F32], "adjoint_own"
        )
        mine = (mine + swap_core(theirs).astype(F32)).astype(HALF)
        if step == 0:
            mine, prior_plain = lax.optimization_barrier((mine, prior_plain))
            prior_turned = turn_blocks(prior_plain, "prior_turn")
        span = mine.shape[1] // 2
        sums = [mine[:, :span], mine[:, span:]]
        bits = 2
        while bits < n_obs:
            others = [exchange(v, lambda i, j, bits=bits: (i ^ bits, j)) for v in sums]
            bits *= 2
            if bits < n_obs:
                sums = [(v.astype(F32) + o.astype(F32)).astype(HALF) for v, o in zip(sums, others)]
        gathered = [
            gather_tiles(nbr, prior_lists, v, o, prior_turned, rows) for v, o in zip(sums, others)
        ]
        if step < STEPS - 1:
            to_core, to_far = (jnp.concatenate([v[k] for v in gathered], axis=1) for k in (1, 2))
            fields = (gathered[0][0], gathered[1][0], swap_far(to_far), swap_core(to_core))
    ext, to_core, to_far = (jnp.concatenate(v, axis=1) for v in zip(*gathered))
    lower = side == 0
    from_core = swap_core(jnp.where(lower, to_core[half - reach :], to_core[:reach])).astype(F32)
    from_far = swap_far(jnp.where(lower, to_far[:reach], to_far[half - reach :])).astype(F32)
    low = jnp.where(lower, from_far, from_core)
    high = jnp.where(lower, from_core, from_far)
    own = (ext[reach : reach + half] + jnp.concatenate([low, high], axis=0)).astype(HALF)
    other = swap_core(own)
    first = jnp.where(side == 0, own, other)
    second = jnp.where(side == 0, other, own)
    return jnp.concatenate([first, second], axis=0)


def solution(mesh):
    placed = (
        P("flux", None, None),
        P("flux", None, None, None),
        P("flux", None),
        P("obs", "flux", None, None, None),
        P("obs", "flux", None),
        P("obs", "flux", None),
        P("obs", "flux"),
        P("obs", None),
    )
    return jax.shard_map(
        shards, mesh=mesh, in_specs=placed, out_specs=P("flux", None, None), check_vma=False
    )
```
